32 devices in a mesh: seq: 8 (over z, x), head: 4 (over y, core).
Axes of the slice: x: 2, y: 2, z: 4, core: 2. Of those that a mesh axis runs over, the one named last changes fastest.
Arguments:
- stream: bfloat16 [3072, 2048], P('seq'), may hold values from -9 to 9
- seg_ids: int32 [3072], P('seq'), may hold values from 0 to 3, never falling along the last dimension, each value on 1 to 1536 neighbouring positions
- attn_gain: float32 [2048], replicated, may hold values from 0.5 to 1.5
- w_query: bfloat16 [2048, 2048], P(None, 'head'), may hold values from -0.375 to 0.375
- w_key: bfloat16 [2048, 2048], P(None, 'head'), may hold values from -0.375 to 0.375
- w_value: bfloat16 [2048, 2048], P(None, 'head'), may hold values from -0.125 to 0.125
- w_outgate: bfloat16 [2048, 2048], P(None, 'head'), may hold values from -0.125 to 0.125
- w_low: bfloat16 [2048, 64], P(None, 'head'), may hold values from -0.125 to 0.125
- w_slot: float32 [4, 16, 64], P('head'), may hold values from -1.5 to 1.5
- forget_bias: float32 [4, 64], P('head'), may hold values from 1 to 7
- head_gain: float32 [4, 512], P('head'), may hold values from 0.5 to 1.5
- w_out: bfloat16 [2048, 2048], P('head'), may hold values from -0.1875 to 0.1875
- mlp_gain: float32 [2048], replicated, may hold values from 0.5 to 1.5
- w_gate: bfloat16 [2048, 5632], P(None, 'head'), may hold values from -0.125 to 0.125
- w_up: bfloat16 [2048, 5632], P(None, 'head'), may hold values from -0.125 to 0.125
- w_down: bfloat16 [5632, 2048], P('head'), may hold values from -0.109375 to 0.109375
- cotangent: bfloat16 [3072, 2048], P('seq'), may hold values from -6 to 6
Outputs:
- out: bfloat16 [3072, 2048], P('seq')
- grad_stream: bfloat16 [3072, 2048], P('seq')
- grad_attn_gain: float32 [2048], P('seq')
- grad_w_query: float32 [2048, 2048], P('seq', 'head')
- grad_w_key: float32 [2048, 2048], P('seq', 'head')
- grad_w_value: float32 [2048, 2048], P('seq', 'head')
- grad_w_outgate: float32 [2048, 2048], P('seq', 'head')
- grad_w_low: float32 [2048, 64], P('seq', 'head')
- grad_w_slot: float32 [4, 16, 64], P('head', None, 'seq')
- grad_forget_bias: float32 [4, 64], P('head', 'seq')
- grad_head_gain: float32 [4, 512], P('head', 'seq')
- grad_w_out: float32 [2048, 2048], P('head', 'seq')
- grad_mlp_gain: float32 [2048], P('seq')
- grad_w_gate: float32 [2048, 5632], P('seq', 'head')
- grad_w_up: float32 [2048, 5632], P('seq', 'head')
- grad_w_down: float32 [5632, 2048], P('head', 'seq')
- stream_rms: float32 [3], replicated
The draws below stay inside these ranges and needn't reach their ends.
Inputs may be any that keep to these rules, and one draw needn't show every extreme that they name: `seg_ids`: document numbers never fall along the sequence; every document has 1 to 1536 tokens and one has exactly 1536.
All inputs are finite; a program needn't handle non-finite values.
Results may differ from the reference program's by a relative error of at most 0.013.
Values sent between devices are 32-bit elements; how exact they have to be, the bound alone decides.
A program may use at most 256 MiB of HBM per device.

```python
import math
import jax
import jax.numpy as jnp
import numpy as np
from jax import lax

D = 2048
HEADS = 4
HD = 512
SLOTS = 64
FF = 5632
RANK = 16
BLOCK = 64
TOKENS = 3072
DOC_MAX = 1536
DOCS = 4


def draw_stream(key, part):
    position = jnp.arange(TOKENS).astype(jnp.float32)
    scaling = 0.5 + position / TOKENS
    base = jnp.clip(jax.random.normal(key, (TOKENS, D), jnp.float32), -6.0, 6.0)
    return (base * scaling[:, None]).astype(jnp.bfloat16)


def level_of(own_key, shape, cuts, least, high):
    level = 1.0
    for dim, blocks in cuts:
        draws = jax.random.uniform(jax.random.fold_in(jax.random.fold_in(own_key, 6), dim), (blocks,), jnp.float32, least / len(cuts), high / len(cuts))
        level = level * jnp.repeat(jnp.exp(draws), shape[dim] // blocks).reshape((-1,) + (1,) * (len(shape) - 1 - dim))
    return level


def length_profile(count, total, reach, skew):
    portions = [(1 << 20) // math.isqrt(rank ** skew) + 1 for rank in range(2, count + 1)]
    rest, holding = total - reach - (count - 1), [1] * (count - 1)
    while rest > 0:
        candidates = [i for i in range(count - 1) if holding[i] < reach]
        mass, budget = sum([portions[i] for i in candidates]), rest
        for i in candidates:
            addition = min(reach - holding[i], max(1, budget * portions[i] // mass), rest)
            holding[i] = holding[i] + addition
            rest = rest - addition
    return np.array([reach] + holding)


def uneven_parts(rng, number_of, total, limit, lean):
    if number_of == 2:
        one = jax.random.randint(rng, (), max(1, total - limit), min(limit, total - 1) + 1)
        return jnp.stack([one, total - one])
    tallies = jnp.asarray(length_profile(number_of, total, limit, lean), jnp.int32)
    twos = (number_of - 1) // 2
    donor, taker = tallies[1:1 + 2 * twos:2], tallies[2:2 + 2 * twos:2]
    room = jnp.minimum(donor - 1, limit - taker)
    moved = jax.random.randint(jax.random.fold_in(rng, 1), (twos,), 0, 1 << 20) % (room + 1)
    tallies = tallies.at[1:1 + 2 * twos:2].set(donor - moved).at[2:2 + 2 * twos:2].set(taker + moved)
    return tallies[jax.random.permutation(jax.random.fold_in(rng, 2), number_of)]


def scatter_about(own_key, shape, deviation, bound, shards=(), kind=jnp.bfloat16):
    values = jax.random.normal(own_key, shape, jnp.float32) * deviation
    if len(shards) > 0:
        values = level_of(own_key, shape, shards, -0.22, 0.18) * values
    return jnp.clip(values, min=-bound, max=bound).astype(kind)


def setup_inputs(seed: int = 0) -> dict:
    keys = jax.random.split(jax.random.key(seed), 18)
    return {
        "stream": draw_stream(jax.random.fold_in(keys[17], 71), 0),
        "seg_ids": jnp.searchsorted(jnp.cumsum(uneven_parts(keys[1], DOCS, TOKENS, DOC_MAX, 1)), jnp.arange(TOKENS), side="right").astype(jnp.int32),
        "attn_gain": jnp.clip(1.0 + 0.1 * jax.random.normal(keys[2], (D,), jnp.float32), 0.5, 1.5),
        "w_query": scatter_about(keys[3], (D, HEADS * HD), (D // 8) ** -0.5, 0.375, ((1, 4),)),
        "w_key": scatter_about(keys[4], (D, HEADS * HD), (D // 8) ** -0.5, 0.375, ((1, 4),)),
        "w_value": scatter_about(keys[5], (D, HEADS * HD), D ** -0.5, 0.125, ((1, 4),)),
        "w_outgate": scatter_about(keys[6], (D, HEADS * HD), D ** -0.5, 0.125, ((1, 4),)),
        "w_low": scatter_about(keys[7], (D, HEADS * RANK), D ** -0.5, 0.125, ((1, 4),)),
        "w_slot": scatter_about(keys[8], (HEADS, RANK, SLOTS), RANK ** -0.5, 1.5, ((0, 4),), jnp.float32),
        "forget_bias": jnp.clip(1.0 + 6.0 * jax.random.uniform(keys[9], (HEADS, SLOTS), jnp.float32) ** level_of(keys[9], (HEADS, SLOTS), ((0, 4),), -0.2, 0.2), 1.0, 7.0),
        "head_gain": jnp.clip(1.0 + 0.1 * jax.random.normal(keys[10], (HEADS, HD), jnp.float32), 0.5, 1.5),
        "w_out": scatter_about(keys[11], (HEADS * HD, D), (HEADS * HD // 2) ** -0.5, 0.1875, ((0, 4),)),
        "mlp_gain": jnp.clip(1.0 + 0.1 * jax.random.normal(keys[12], (D,), jnp.float32), 0.5, 1.5),
        "w_gate": scatter_about(keys[13], (D, FF), D ** -0.5, 0.125, ((1, 4),)),
        "w_up": scatter_about(keys[14], (D, FF), D ** -0.5, 0.125, ((1, 4),)),
        "w_down": scatter_about(keys[15], (FF, D), (FF // 2) ** -0.5, 0.109375, ((0, 4),)),
        "cotangent": scatter_about(keys[16], (TOKENS, D), 1.0, 6.0, ((0, 8),)),
    }


EPSILON = 1e-06
GATE_NORM = 8.0
PRECISE = lax.Precision.HIGHEST

@jax.custom_vjp
def low(v):
    return lax.optimization_barrier(v.astype(jnp.bfloat16)).astype(jnp.float32)

@jax.custom_vjp
def low_back(v):
    return v

def low_keep(v):
    return (low(v), None)

def low_pass(kept, grad):
    return (grad,)

def back_keep(v):
    return (v, None)

def back_low(kept, grad):
    return (low(grad),)
low.defvjp(low_keep, low_pass)
low_back.defvjp(back_keep, back_low)

def round_both(value):
    return low(low_back(value))

def precise_dot(left, right):
    return jnp.dot(left, right, precision=PRECISE, preferred_element_type=jnp.float32)

def rms_scale(value):
    return lax.rsqrt(lax.optimization_barrier(jnp.mean(value * value, axis=-1, keepdims=True)) + EPSILON)

def block_step(state_in, inputs):
    key_state, value_state, seg_before = state_in
    queries, key_rows, value_rows, log_decay, segment = inputs
    positions = log_decay.shape[0]
    running = jnp.cumsum(log_decay, axis=0)
    position = jnp.arange(positions)
    same_doc = (segment[:, None] == segment[None, :]) & (position[:, None] >= position[None, :])
    same_doc = same_doc[:, :, None]
    decay_span = jnp.where(same_doc, running[:, None, :] - running[None, :, :], 0.0)
    weights = jnp.where(same_doc, jnp.exp(decay_span), 0.0) * (-jnp.expm1(log_decay))[None, :, :]
    carried = jnp.where((segment == seg_before)[:, None], jnp.exp(running), 0.0)
    scaling = queries.shape[1] ** (-0.5)
    affinity = precise_dot(queries, key_rows.T)
    scores = scaling * (carried * precise_dot(queries, key_state.T) + jnp.einsum('tjm,tj->tm', weights, affinity, precision=PRECISE))
    slot_probs = low(jax.nn.softmax(scores, axis=1))
    mixing = jnp.einsum('tm,tjm->tj', slot_probs, weights, precision=PRECISE)
    output = precise_dot(slot_probs * carried, value_state) + precise_dot(mixing, value_rows)
    last_row = weights[positions - 1]
    keep_last = carried[positions - 1][:, None]
    key_next = keep_last * key_state + precise_dot(last_row.T, key_rows)
    value_next = keep_last * value_state + precise_dot(last_row.T, value_rows)
    return ((key_next, value_next, segment[positions - 1]), output)

def to_blocks(array):
    return array.reshape((array.shape[0] // BLOCK, BLOCK) + array.shape[1:])

def head_scan(queries, key_rows, value_rows, log_decay, seg_ids):
    start = (jnp.zeros((log_decay.shape[1], queries.shape[1]), jnp.float32), jnp.zeros((log_decay.shape[1], value_rows.shape[1]), jnp.float32), jnp.array(-1, jnp.int32))
    final_state, reads = lax.scan(jax.checkpoint(block_step), start, (to_blocks(queries), to_blocks(key_rows), to_blocks(value_rows), to_blocks(log_decay), to_blocks(seg_ids)))
    return reads.reshape(queries.shape)

def heads_first(array):
    return array.reshape(TOKENS, HEADS, HD).transpose(1, 0, 2)

def layer(stream, attn_gain, w_query, w_key, w_value, w_outgate, w_low, w_slot, forget_bias, head_gain, w_out, mlp_gain, w_gate, w_up, w_down, seg_ids):
    normed_in = low(stream * rms_scale(stream) * attn_gain)
    queries = round_both(precise_dot(normed_in, w_query))
    key_rows = round_both(precise_dot(normed_in, w_key))
    value_rows = round_both(precise_dot(normed_in, w_value))
    gate_act = low_back(precise_dot(normed_in, w_outgate))
    ranked = precise_dot(normed_in, w_low).reshape(TOKENS, HEADS, RANK)
    log_decay = jax.nn.log_sigmoid(jnp.einsum('thr,hrm->thm', ranked, w_slot, precision=PRECISE) + forget_bias) / GATE_NORM
    slot_read = jax.vmap(head_scan, in_axes=(0, 0, 0, 0, None))(heads_first(queries), heads_first(key_rows), heads_first(value_rows), log_decay.transpose(1, 0, 2), seg_ids)
    slot_read = slot_read.transpose(1, 0, 2)
    normed_read = slot_read * rms_scale(slot_read) * head_gain
    mixed_heads = low((normed_read * jax.nn.silu(gate_act.reshape(TOKENS, HEADS, HD))).reshape(TOKENS, HEADS * HD))
    hidden = stream + low_back(precise_dot(mixed_heads, w_out))
    normed_mid = low(hidden * rms_scale(hidden) * mlp_gain)
    gate_pre = low_back(precise_dot(normed_mid, w_gate))
    up_pre = low_back(precise_dot(normed_mid, w_up))
    ffn_act = low(jax.nn.silu(gate_pre) * up_pre)
    result = hidden + low_back(precise_dot(ffn_act, w_down))
    return (result, (hidden, result))

def reference(stream, seg_ids, attn_gain, w_query, w_key, w_value, w_outgate, w_low, w_slot, forget_bias, head_gain, w_out, mlp_gain, w_gate, w_up, w_down, cotangent):
    as_floats = tuple((array.astype(jnp.float32) for array in (stream, attn_gain, w_query, w_key, w_value, w_outgate, w_low, w_slot, forget_bias, head_gain, w_out, mlp_gain, w_gate, w_up, w_down)))

    def forward(*inputs):
        return layer(*inputs, seg_ids)
    result, pullback, streams = jax.vjp(forward, *as_floats, has_aux=True)
    gradients = pullback(cotangent.astype(jnp.float32))
    stream_f = as_floats[0]
    hidden, final = streams
    stream_rms = jnp.sqrt(jnp.stack([jnp.mean(stream_f * stream_f), jnp.mean(hidden * hidden), jnp.mean(final * final)]))
    return (result.astype(jnp.bfloat16), gradients[0].astype(jnp.bfloat16), gradients[1], gradients[2], gradients[3], gradients[4], gradients[5], gradients[6], gradients[7], gradients[8], gradients[9], gradients[10], gradients[11], gradients[12], gradients[13], gradients[14], stream_rms)
```

```python
import jax
import jax.numpy as jnp
from jax import lax
from jax.experimental import pallas as pl
from jax.experimental.pallas import tpu as pltpu
from jax.sharding import PartitionSpec as P

CHUNK = 32
CHUNKS = 2
VMEM = 48 << 20
READ_COST = 17 << 30
BACK_COST = 34 << 30


EPSILON = 1e-06
GATE_NORM = 8.0
PRECISE = lax.Precision.HIGHEST


def passed_along(array, axis, by):
    devices = lax.axis_size(axis)
    pairs = [(i, i + by) for i in range(devices) if 0 <= i + by < devices]
    return lax.ppermute(array, axis, pairs)


def swapped(array, axis, by):
    return lax.ppermute(array, axis, [(i, i ^ by) for i in range(lax.axis_size(axis))])


def entering(part, axis, combine, identity, reverse):
    count = lax.axis_size(axis)
    place = lax.axis_index(axis)
    ahead = count - 1 - place if reverse else place
    sign = -1 if reverse else 1

    def from_before(state, by):
        moved = jax.tree.map(lambda a: passed_along(a, axis, sign * by), state)
        return jax.tree.map(lambda m, e: jnp.where(ahead >= by, m, e), moved, identity)

    state = from_before(part, 1)
    by = 1
    while by < count:
        state = combine(from_before(state, by), state)
        by *= 2
    return state


def head_sum(parts):
    count = lax.axis_size("head")
    low = lax.axis_index("head") % 2
    out = []
    for part in parts:
        rows = part.shape[0] // 2
        mine = lax.dynamic_slice_in_dim(part, low * rows, rows, 0)
        other = lax.dynamic_slice_in_dim(part, (1 - low) * rows, rows, 0)
        half = mine + swapped(other, "head", 1)
        by = 2
        while by < count:
            half = half + swapped(half, "head", by)
            by *= 2
        back = swapped(half, "head", 1)
        out.append(jnp.where(low == 0, half, back))
        out.append(jnp.where(low == 0, back, half))
    return jnp.concatenate(out, axis=0)


def sent(array):
    moved = swapped(array.astype(jnp.float32), "seq", 1)
    unit = jnp.minimum(lax.axis_index("seq").astype(jnp.float32) + 1.0, 1.0)
    return (moved * unit).astype(jnp.bfloat16)


def width_blocks(array):
    count = lax.axis_size("seq")
    lines = count // 2
    place = lax.axis_index("seq")
    line, odd = place // 2, place % 2
    wide = array.shape[1] // count
    roles = list(range(lines))
    if lines == 4:
        left = line < 2
        roles = [jnp.where(left, a, b) for a, b in ((2, 1), (3, 0), (1, 2), (0, 3))]

    def blocks(parity):
        return jnp.stack(
            [lax.dynamic_slice_in_dim(array, (2 * r + parity) * wide, wide, 1) for r in roles]
        )

    mine, theirs = blocks(odd), blocks(1 - odd)
    return mine, sent(theirs)


def seq_sum(wide, narrow, wide_first):
    count = lax.axis_size("seq")
    lines = count // 2
    place = lax.axis_index("seq") // 2
    mine, theirs = wide
    pair = (narrow, sent(narrow))
    rule = "ztd,tf->zdf" if wide_first else "ztd,tf->zfd"

    def product(lo, hi):
        return sum(
            jnp.einsum(rule, w[lo:hi], n, preferred_element_type=jnp.float32)
            for w, n in zip((mine, theirs), pair)
        )

    if lines != 4:
        groups = [[line * 2 + x for line in range(lines)] for x in range(2)]
        return lax.psum_scatter(
            product(0, lines), "seq", scatter_dimension=0, axis_index_groups=groups, tiled=True
        )[0]

    def moved(array, pairs):
        return lax.ppermute(
            array, "seq", [(2 * a + x, 2 * b + x) for a, b in pairs for x in range(2)]
        )

    far = product(0, 3)
    near = product(3, 4)
    from_end = moved(far, ((0, 1), (3, 2)))
    from_middle = moved(far[:2] + from_end[:2], ((1, 2), (2, 1)))
    to_end = moved(near + from_middle[1:], ((1, 0), (2, 3)))
    at_end = (place == 0) | (place == 3)
    return jnp.where(at_end, near[0] + to_end[0], far[2] + from_end[2] + from_middle[0])


def precise_dot(left, right):
    return jnp.dot(left, right, precision=PRECISE, preferred_element_type=jnp.float32)


def plain_dot(left, right):
    return jnp.dot(left, right, preferred_element_type=jnp.float32)


def dot_right_t(left, right):
    return lax.dot_general(
        left, right, (((1,), (1,)), ((), ())), preferred_element_type=jnp.float32
    )


def dot_left_t(left, right):
    return lax.dot_general(
        left, right, (((0,), (0,)), ((), ())), preferred_element_type=jnp.float32
    )


def precise_left_t(left, right):
    return lax.dot_general(
        left, right, (((0,), (0,)), ((), ())), precision=PRECISE, preferred_element_type=jnp.float32
    )


def precise_right_t(left, right):
    return lax.dot_general(
        left, right, (((1,), (1,)), ((), ())), precision=PRECISE, preferred_element_type=jnp.float32
    )


def rms_scale(value):
    return lax.rsqrt(jnp.mean(value * value, axis=-1, keepdims=True) + EPSILON)


def split(value):
    high = value.astype(jnp.bfloat16)
    return high, (value - high.astype(jnp.float32)).astype(jnp.bfloat16)


def nn(left, right):
    return jnp.dot(left, right, preferred_element_type=jnp.float32)


def nt(left, right):
    return lax.dot_general(
        left, right, (((1,), (1,)), ((), ())), preferred_element_type=jnp.float32
    )


def two(product, left, right):
    high, low = split(right)
    return product(left, high) + product(left, low)


def three(product, left, right):
    left_high, left_low = split(left)
    right_high, right_low = split(right)
    return product(left_high, right_high) + (
        product(left_low, right_high) + product(left_high, right_low)
    )


def row_blocks(value):
    return [value[r : r + 8] for r in range(0, value.shape[0], 8)]


def exact_dot(left, right):
    return jnp.dot(left, right, precision=PRECISE, preferred_element_type=jnp.float32)


def triangle(size, upper):
    row = lax.broadcasted_iota(jnp.int32, (size, size), 0)
    column = lax.broadcasted_iota(jnp.int32, (size, size), 1)
    keep = row <= column if upper else row >= column
    return jnp.where(keep, 1.0, 0.0)


def spans(running, docs, span_s):
    size = running.shape[0]
    run, doc = row_blocks(running), row_blocks(docs)
    place = lax.broadcasted_iota(jnp.int32, (8, running.shape[1]), 0)
    for j in range(size):
        for r in range(j // 8, size // 8):
            ok = doc[r] == docs[j : j + 1]
            if r == j // 8 and j % 8:
                ok = ok & (place >= j % 8)
            span_s[j, 8 * r : 8 * r + 8] = jnp.where(ok, jnp.exp(run[r] - running[j : j + 1]), 0.0)


def to_end(running, docs):
    last = running.shape[0] - 1
    return jnp.where(
        docs == docs[last : last + 1], jnp.exp(running[last : last + 1] - running), 0.0
    )


def turned(to_end_weights, kept):
    size, slots = to_end_weights.shape
    fill = jnp.broadcast_to(kept, (128 - size, slots))
    both = jnp.concatenate([to_end_weights, fill], axis=0).T
    return both[:, :size], both[:, size : size + 1]


def read_kernel(
    q_ref, k_ref, v_ref, log_ref, new_ref, doc_ref, prev_ref, kin_ref, vin_ref,
    read_ref, score_ref, prob_ref, ks_ref, vs_ref, span_s,
):
    size = span_s.shape[0]
    lower = triangle(size, False)
    scaling = q_ref.shape[1] ** (-0.5)
    ks_ref[0] = kin_ref[...]
    vs_ref[0] = vin_ref[...]
    lane = lax.broadcasted_iota(jnp.int32, (8, size), 1)

    def chunk(i, carry):
        rows = pl.ds(pl.multiple_of(i * size, size), size)
        queries, keys, values = q_ref[rows, :], k_ref[rows, :], v_ref[rows, :]
        new, docs = new_ref[rows, :], doc_ref[rows, :]
        running = exact_dot(lower, log_ref[rows, :])
        carried = jnp.where(docs == prev_ref[rows, :], jnp.exp(running), 0.0)
        key_state, value_state = ks_ref[i], vs_ref[i]
        spans(running, docs, span_s)
        affinity = row_blocks(nt(queries, keys))
        scores = row_blocks(carried * two(nt, queries, key_state))
        for j in range(size):
            for r in range(j // 8, size // 8):
                weight = span_s[j, 8 * r : 8 * r + 8] * new[j : j + 1]
                scores[r] = scores[r] + weight * affinity[r][:, j : j + 1]
        scores = scaling * jnp.concatenate(scores, axis=0)
        probs = jnp.exp(scores - jnp.max(scores, axis=1, keepdims=True))
        probs = probs / jnp.sum(probs, axis=1, keepdims=True)
        score_ref[rows, :] = scores
        prob_ref[rows, :] = probs
        used = probs.astype(jnp.bfloat16).astype(jnp.float32)
        part = row_blocks(used)
        mixing = [jnp.zeros((8, size), jnp.float32) for _ in part]
        for j in range(size):
            for r in range(j // 8, size // 8):
                weight = span_s[j, 8 * r : 8 * r + 8] * new[j : j + 1]
                total = jnp.sum(part[r] * weight, axis=1, keepdims=True)
                mixing[r] = jnp.where(lane == j, total, mixing[r])
        high, low = split(jnp.concatenate(mixing, axis=0))
        read_ref[rows, :] = (
            three(nn, used * carried, value_state) + nn(high, values) + nn(low, values)
        )
        end, kept = turned(to_end(running, docs) * new, carried[size - 1 : size])
        high, low = split(end)
        ks_ref[i + 1] = kept * key_state + (nn(high, keys) + nn(low, keys))
        vs_ref[i + 1] = kept * value_state + (nn(high, values) + nn(low, values))
        return carry

    lax.fori_loop(0, q_ref.shape[0] // size, chunk, 0)


def back_query_kernel(
    q_ref, k_ref, v_ref, log_ref, new_ref, doc_ref, prev_ref, score_ref, prob_ref, ks_ref, vs_ref, g_ref,
    dq_ref, dk_ref, dv_ref, held_ref, gained_ref, xk_ref, xv_ref, dkin_ref, dvin_ref, span_s,
):
    size = span_s.shape[0]
    count = q_ref.shape[0] // size
    lower = triangle(size, False)
    scaling = q_ref.shape[1] ** (-0.5)
    dkin_ref[...] = jnp.zeros_like(dkin_ref)
    dvin_ref[...] = jnp.zeros_like(dvin_ref)
    lane = lax.broadcasted_iota(jnp.int32, (8, size), 1)

    def chunk(turn, carry):
        i = count - 1 - turn
        start = pl.multiple_of(i * size, size)
        rows = pl.ds(start, size)
        queries, keys, values, grads = q_ref[rows, :], k_ref[rows, :], v_ref[rows, :], g_ref[rows, :]
        new, docs = new_ref[rows, :], doc_ref[rows, :]
        running = exact_dot(lower, log_ref[rows, :])
        carried = jnp.where(docs == prev_ref[rows, :], jnp.exp(running), 0.0)
        spans(running, docs, span_s)
        affinity = row_blocks(nt(queries, keys))
        grad_high, grad_low = split(grads)
        pull = row_blocks(nt(grad_high, values) + nt(grad_low, values))
        back = row_blocks(carried * three(nt, grads, vs_ref[i]))
        for j in range(size):
            for r in range(j // 8, size // 8):
                weight = span_s[j, 8 * r : 8 * r + 8] * new[j : j + 1]
                back[r] = back[r] + weight * pull[r][:, j : j + 1]
        back = jnp.concatenate(back, axis=0)
        probs = prob_ref[rows, :]
        used = probs.astype(jnp.bfloat16).astype(jnp.float32)
        inner = probs * (back - jnp.sum(probs * back, axis=1, keepdims=True))
        gained_ref[rows, :] = inner * score_ref[rows, :] + used * back
        outer = scaling * inner
        part, used_part = row_blocks(outer), row_blocks(used)
        key_mix = [jnp.zeros((8, size), jnp.float32) for _ in part]
        value_mix = [jnp.zeros((8, size), jnp.float32) for _ in part]
        for j in range(size):
            held = None
            for r in range(j // 8, size // 8):
                span = span_s[j, 8 * r : 8 * r + 8]
                key_side, value_side = part[r] * span, used_part[r] * span
                own = key_side * affinity[r][:, j : j + 1] + value_side * pull[r][:, j : j + 1]
                held = own if held is None else held + own
                fresh = new[j : j + 1]
                key_mix[r] = jnp.where(
                    lane == j, jnp.sum(key_side * fresh, axis=1, keepdims=True), key_mix[r]
                )
                value_mix[r] = jnp.where(
                    lane == j, jnp.sum(value_side * fresh, axis=1, keepdims=True), value_mix[r]
                )
            held_ref[pl.ds(start + j, 1), :] = jnp.sum(held, axis=0, keepdims=True)
        key_mix = jnp.concatenate(key_mix, axis=0)
        value_mix = jnp.concatenate(value_mix, axis=0)
        outer_in, used_in = outer * carried, used * carried
        high, low = split(key_mix)
        dq_ref[rows, :] = three(nn, outer_in, ks_ref[i]) + (nn(high, keys) + nn(low, keys))
        fill = jnp.zeros((128 - size, size), jnp.float32)
        high, low = split(jnp.concatenate([key_mix, fill], axis=0).T[:, :size])
        dk_ref[rows, :] = nn(high, queries) + nn(low, queries)
        mixed = jnp.concatenate([value_mix, fill], axis=0).T[:, :size]
        dv_ref[rows, :] = three(nn, mixed, grads)
        outer_t, kept = turned(outer_in, carried[size - 1 : size])
        used_t, kept = turned(used_in, carried[size - 1 : size])
        high, low = split(outer_t)
        to_key = nn(high, queries) + nn(low, queries)
        to_value = three(nn, used_t, grads)
        xk_ref[i] = to_key
        xv_ref[i] = to_value
        dkin_ref[...] = kept * dkin_ref[...] + to_key
        dvin_ref[...] = kept * dvin_ref[...] + to_value
        return carry

    lax.fori_loop(0, count, chunk, 0)


def back_key_kernel(
    k_ref, v_ref, log_ref, new_ref, doc_ref, prev_ref, dk_in_ref, dv_in_ref, held_ref, gained_ref,
    xk_ref, xv_ref, dkend_ref, dvend_ref, total_ref,
    dk_ref, dv_ref, dlog_ref, ks, vs, total,
):
    size = CHUNK
    count = k_ref.shape[0] // size
    lower, upper = triangle(size, False), triangle(size, True)
    ks[...] = dkend_ref[...]
    vs[...] = dvend_ref[...]
    total[...] = total_ref[...]

    def chunk(turn, carry):
        i = count - 1 - turn
        rows = pl.ds(pl.multiple_of(i * size, size), size)
        keys, values = k_ref[rows, :], v_ref[rows, :]
        logs, new, docs = log_ref[rows, :], new_ref[rows, :], doc_ref[rows, :]
        running = exact_dot(lower, logs)
        carried = jnp.where(docs == prev_ref[rows, :], jnp.exp(running), 0.0)
        end = to_end(running, docs)
        weight = end * new
        dk_ref[rows, :] = (dk_in_ref[rows, :] + three(nn, weight, ks[...])).astype(dk_ref.dtype)
        dv_ref[rows, :] = (dv_in_ref[rows, :] + three(nn, weight, vs[...])).astype(dv_ref.dtype)
        held = held_ref[rows, :] + end * (two(nt, keys, ks[...]) + two(nt, values, vs[...]))
        change = gained_ref[rows, :] - new * held
        after = exact_dot(upper, change) + total[...]
        dlog_ref[rows, :] = after - jnp.exp(logs) * held
        total[...] = after[:1]
        unused, kept = turned(carried, carried[size - 1 : size])
        ks[...] = kept * ks[...] + xk_ref[i]
        vs[...] = kept * vs[...] + xv_ref[i]
        return carry

    lax.fori_loop(0, count, chunk, 0)


def cost(flops, moved):
    return pl.CostEstimate(flops=flops, bytes_accessed=moved, transcendentals=0)


def read_slots(queries, keys, values, logs, new, docs, prev, key_in, value_in):
    rows, width = queries.shape
    slots = logs.shape[1]
    count = rows // CHUNK
    f32 = jnp.float32
    return pl.pallas_call(
        read_kernel,
        out_shape=(
            jax.ShapeDtypeStruct((rows, width), f32),
            jax.ShapeDtypeStruct((rows, slots), f32),
            jax.ShapeDtypeStruct((rows, slots), f32),
            jax.ShapeDtypeStruct((count + 1, slots, width), f32),
            jax.ShapeDtypeStruct((count + 1, slots, width), f32),
        ),
        scratch_shapes=[pltpu.VMEM((CHUNK, CHUNK, slots), f32)],
        compiler_params=pltpu.CompilerParams(vmem_limit_bytes=VMEM),
        cost_estimate=cost(READ_COST, 5 << 20),
    )(queries, keys, values, logs, new, docs, prev, key_in, value_in)


def back_query(queries, keys, values, logs, new, docs, prev, scores, probs, key_states, value_states, grads):
    rows, width = queries.shape
    slots = logs.shape[1]
    count = rows // CHUNK
    f32 = jnp.float32
    narrow = jax.ShapeDtypeStruct((rows, slots), f32)
    wide = jax.ShapeDtypeStruct((rows, width), f32)
    states = jax.ShapeDtypeStruct((count, slots, width), f32)
    state = jax.ShapeDtypeStruct((slots, width), f32)
    return pl.pallas_call(
        back_query_kernel,
        out_shape=(wide, wide, wide, narrow, narrow, states, states, state, state),
        scratch_shapes=[pltpu.VMEM((CHUNK, CHUNK, slots), f32)],
        compiler_params=pltpu.CompilerParams(vmem_limit_bytes=VMEM),
        cost_estimate=cost(BACK_COST, 10 << 20),
    )(queries, keys, values, logs, new, docs, prev, scores, probs, key_states, value_states, grads)


def back_key(keys, values, logs, new, docs, prev, dk, dv, held, gained, xk, xv, dk_end, dv_end, total):
    rows, width = keys.shape
    slots = logs.shape[1]
    f32 = jnp.float32
    wide = jax.ShapeDtypeStruct((rows, width), jnp.bfloat16)
    return pl.pallas_call(
        back_key_kernel,
        out_shape=(wide, wide, jax.ShapeDtypeStruct((rows, slots), f32)),
        scratch_shapes=[
            pltpu.VMEM((slots, width), f32),
            pltpu.VMEM((slots, width), f32),
            pltpu.VMEM((1, slots), f32),
        ],
        compiler_params=pltpu.CompilerParams(vmem_limit_bytes=VMEM),
        cost_estimate=cost(READ_COST, 8 << 20),
    )(keys, values, logs, new, docs, prev, dk, dv, held, gained, xk, xv, dk_end, dv_end, total)


def compose(earlier, later):
    factor = later[0][:, None]
    return (earlier[0] * later[0], factor * earlier[1] + later[1], factor * earlier[2] + later[2])


def body(
    stream,
    seg_ids,
    attn_gain,
    w_query,
    w_key,
    w_value,
    w_outgate,
    w_low,
    w_slot,
    forget_bias,
    head_gain,
    w_out,
    mlp_gain,
    w_gate,
    w_up,
    w_down,
    cotangent,
):
    tok_rows = stream.shape[0]
    width = stream.shape[1]
    slots = w_slot.shape[2]
    head_width = w_query.shape[1]
    prior = passed_along(seg_ids[tok_rows - 1 :], "seq", 1)[0]
    stream_f = stream.astype(jnp.float32)
    scale_in = rms_scale(stream_f)
    normed_in = (stream_f * scale_in * attn_gain).astype(jnp.bfloat16)
    query_rows = plain_dot(normed_in, w_query).astype(jnp.bfloat16)
    key_rows = plain_dot(normed_in, w_key).astype(jnp.bfloat16)
    value_rows = plain_dot(normed_in, w_value).astype(jnp.bfloat16)
    gate_act = plain_dot(normed_in, w_outgate)
    ranked = plain_dot(normed_in, w_low)

    def decay_logs(ranked_in, slot_map, bias_row):
        return jax.nn.log_sigmoid(precise_dot(ranked_in, slot_map[0]) + bias_row[0]) / GATE_NORM

    log_decay, gate_pull = jax.vjp(decay_logs, ranked, w_slot, forget_bias)

    new = -jnp.expm1(log_decay)
    last_doc = seg_ids[tok_rows - 1]
    running = precise_dot(jnp.tril(jnp.ones((tok_rows, tok_rows), jnp.float32)), log_decay)
    total = running[tok_rows - 1]
    in_last = (seg_ids == last_doc)[:, None]
    factor = jnp.where(in_last, jnp.exp(jnp.where(in_last, total - running, 0.0)) * new, 0.0)
    docs = seg_ids.astype(jnp.float32)
    before = jnp.concatenate([prior.astype(jnp.float32)[None], docs[CHUNK - 1 : -1 : CHUNK]])
    docs = jnp.broadcast_to(docs[:, None], (tok_rows, slots))
    before = jnp.broadcast_to(jnp.repeat(before, CHUNK)[:, None], (tok_rows, slots))

    chunk = tok_rows // CHUNKS

    def over_heads(product):
        return head_sum(
            [product(lambda a, i=i: a[i * chunk : (i + 1) * chunk]) for i in range(CHUNKS)]
        )

    zero_state = jnp.zeros((slots, head_width), jnp.float32)
    local_key = precise_left_t(factor, key_rows.astype(jnp.float32))
    local_value = precise_left_t(factor, value_rows.astype(jnp.float32))
    decay_all = jnp.where(last_doc == prior, jnp.exp(total), 0.0)
    identity = (jnp.ones((slots,), jnp.float32), zero_state, zero_state)
    prefix = entering((decay_all, local_key, local_value), "seq", compose, identity, False)
    slot_read, scores, probs, key_states, value_states = read_slots(
        query_rows, key_rows, value_rows, log_decay, new, docs, before, prefix[1], prefix[2]
    )
    scale_read = rms_scale(slot_read)
    normed_read = slot_read * scale_read * head_gain[0]
    gate_sig = jax.nn.sigmoid(gate_act)
    gate_silu = gate_act * gate_sig
    mixed_heads = (normed_read * gate_silu).astype(jnp.bfloat16)
    branch = over_heads(lambda rows: plain_dot(rows(mixed_heads), w_out))
    hidden = stream_f + branch
    scale_mid = rms_scale(hidden)
    normed_mid = (hidden * scale_mid * mlp_gain).astype(jnp.bfloat16)
    gate_pre = plain_dot(normed_mid, w_gate)
    up_pre = plain_dot(normed_mid, w_up)
    pre_sig = jax.nn.sigmoid(gate_pre)
    pre_silu = gate_pre * pre_sig
    ffn_act = (pre_silu * up_pre).astype(jnp.bfloat16)
    ffn_out = over_heads(lambda rows: plain_dot(rows(ffn_act), w_down))
    result = hidden + ffn_out
    square_sums = lax.psum(
        jnp.stack(
            [jnp.sum(stream_f * stream_f), jnp.sum(hidden * hidden), jnp.sum(result * result)]
        ),
        "seq",
    )
    stream_rms = jnp.sqrt(square_sums / (tok_rows * lax.axis_size("seq") * width))
    upstream = cotangent.astype(jnp.float32)
    d_act = dot_right_t(cotangent, w_down)
    grad_down = seq_sum(width_blocks(cotangent), ffn_act, False)
    d_gate = (d_act * up_pre * pre_sig * (1.0 + gate_pre * (1.0 - pre_sig))).astype(jnp.bfloat16)
    d_up = (d_act * pre_silu).astype(jnp.bfloat16)
    d_mid = over_heads(
        lambda rows: dot_right_t(rows(d_gate), w_gate) + dot_right_t(rows(d_up), w_up)
    )
    wide_mid = width_blocks(normed_mid)
    grad_gate = seq_sum(wide_mid, d_gate, True)
    grad_up = seq_sum(wide_mid, d_up, True)
    grad_mlp_gain = jnp.sum(d_mid * hidden * scale_mid, axis=0)
    scaled_mid = d_mid * mlp_gain
    d_hidden = (
        upstream
        + scale_mid * scaled_mid
        - hidden * scale_mid**3 * jnp.mean(scaled_mid * hidden, axis=1, keepdims=True)
    )
    d_branch = d_hidden.astype(jnp.bfloat16)
    d_mixed = dot_right_t(d_branch, w_out)
    grad_out = seq_sum(width_blocks(d_branch), mixed_heads, False)
    d_gate_act = (d_mixed * normed_read * gate_sig * (1.0 + gate_act * (1.0 - gate_sig))).astype(
        jnp.bfloat16
    )
    d_normed = d_mixed * gate_silu
    grad_head_gain = jnp.sum(d_normed * slot_read * scale_read, axis=0)[None, :]
    scaled_read = d_normed * head_gain[0]
    d_read = scale_read * scaled_read - slot_read * scale_read**3 * jnp.mean(
        scaled_read * slot_read, axis=1, keepdims=True
    )
    d_query, d_key, d_value, held, gained, to_keys, to_values, key_back, value_back = back_query(
        query_rows, key_rows, value_rows, log_decay, new, docs, before, scores, probs, key_states, value_states, d_read
    )
    query_back = d_query.astype(jnp.bfloat16)
    suffix = entering((decay_all, key_back, value_back), "seq", compose, identity, True)
    end_total = jnp.sum(key_states[-1] * suffix[1] + value_states[-1] * suffix[2], axis=1)[None, :]
    key_back, value_back, d_logs = back_key(
        key_rows, value_rows, log_decay, new, docs, before, d_key, d_value, held, gained,
        to_keys, to_values, suffix[1], suffix[2], end_total,
    )
    d_ranked, grad_slot, grad_bias = gate_pull(d_logs)
    normed_f = normed_in.astype(jnp.float32)
    grad_low = precise_left_t(normed_f, d_ranked)
    wide_in = width_blocks(normed_in)
    grad_outgate = seq_sum(wide_in, d_gate_act, True)
    grad_query = seq_sum(wide_in, query_back, True)
    grad_key = seq_sum(wide_in, key_back, True)
    grad_value = seq_sum(wide_in, value_back, True)
    d_in = over_heads(
        lambda rows: dot_right_t(rows(query_back), w_query)
        + dot_right_t(rows(key_back), w_key)
        + dot_right_t(rows(value_back), w_value)
        + dot_right_t(rows(d_gate_act), w_outgate)
        + precise_right_t(rows(d_ranked), w_low.astype(jnp.float32))
    )
    grad_attn_gain = jnp.sum(d_in * stream_f * scale_in, axis=0)
    scaled_in = d_in * attn_gain
    grad_stream = (
        d_hidden
        + scale_in * scaled_in
        - stream_f * scale_in**3 * jnp.mean(scaled_in * stream_f, axis=1, keepdims=True)
    ).astype(jnp.bfloat16)
    count = lax.axis_size("seq")
    small = [
        grad_attn_gain.reshape(count, -1),
        grad_mlp_gain.reshape(count, -1),
        grad_low.reshape(count, -1),
        jnp.moveaxis(grad_slot[0].reshape(-1, count, slots // count), 1, 0).reshape(count, -1),
        grad_bias.reshape(count, -1),
        grad_head_gain.reshape(count, -1),
    ]
    sizes = [a.shape[1] for a in small]
    packed = jnp.concatenate(small, axis=1)
    packed = jnp.pad(packed, ((0, 0), (0, -packed.shape[1] % 128)))
    packed = lax.psum_scatter(packed, "seq", scatter_dimension=0, tiled=True)[0]
    ends = [sum(sizes[: i + 1]) for i in range(len(sizes))]
    small = [packed[end - size : end] for end, size in zip(ends, sizes)]
    summed = (
        small[0],
        grad_query,
        grad_key,
        grad_value,
        grad_outgate,
        small[2].reshape(width // count, -1),
        small[3].reshape(1, -1, slots // count),
        small[4][None, :],
        small[5][None, :],
        grad_out,
        small[1],
        grad_gate,
        grad_up,
        grad_down,
    )
    mixer_parts = summed[:10]
    ffn_parts = summed[10:]
    return (
        result.astype(jnp.bfloat16),
        grad_stream,
        mixer_parts[0],
        mixer_parts[1],
        mixer_parts[2],
        mixer_parts[3],
        mixer_parts[4],
        mixer_parts[5],
        mixer_parts[6],
        mixer_parts[7],
        mixer_parts[8],
        mixer_parts[9],
        ffn_parts[0],
        ffn_parts[1],
        ffn_parts[2],
        ffn_parts[3],
        stream_rms,
    )


def solution(mesh):
    in_specs = (
        P("seq", None),
        P("seq"),
        P(),
        P(None, "head"),
        P(None, "head"),
        P(None, "head"),
        P(None, "head"),
        P(None, "head"),
        P("head", None, None),
        P("head", None),
        P("head", None),
        P("head", None),
        P(),
        P(None, "head"),
        P(None, "head"),
        P("head", None),
        P("seq", None),
    )
    out_specs = (
        P("seq", None),
        P("seq", None),
        P("seq"),
        P("seq", "head"),
        P("seq", "head"),
        P("seq", "head"),
        P("seq", "head"),
        P("seq", "head"),
        P("head", None, "seq"),
        P("head", "seq"),
        P("head", "seq"),
        P("head", "seq"),
        P("seq"),
        P("seq", "head"),
        P("seq", "head"),
        P("head", "seq"),
        P(),
    )
    return jax.shard_map(body, mesh=mesh, in_specs=in_specs, out_specs=out_specs, check_vma=False)
```

```python
import functools

import jax
import jax.numpy as jnp
from jax import lax
from jax.experimental import pallas as pl
from jax.experimental.pallas import tpu as pltpu
from jax.sharding import PartitionSpec as P

CHUNK = 32
CHUNKS = 4
MESH = pl.DeviceIdType.MESH
VMEM = 48 << 20
READ_COST = 17 << 30
BACK_COST = 34 << 30


EPSILON = 1e-06
GATE_NORM = 8.0
PRECISE = lax.Precision.HIGHEST


def passed_along(array, axis, by):
    devices = lax.axis_size(axis)
    pairs = [(i, i + by) for i in range(devices) if 0 <= i + by < devices]
    return lax.ppermute(array, axis, pairs)


def width_blocks(array):
    count = lax.axis_size("seq")
    lines = count // 2
    place = lax.axis_index("seq")
    odd = place % 2
    wide = array.shape[1] // count
    roles = list(range(lines))

    def blocks(parity):
        return jnp.stack(
            [lax.dynamic_slice_in_dim(array, (2 * r + parity) * wide, wide, 1) for r in roles]
        )

    return blocks(odd), blocks(1 - odd).astype(jnp.float32)


def pair_product(wide, narrow, wide_first):
    rule = "ztd,tf->zdf" if wide_first else "ztd,tf->zfd"
    return sum(
        jnp.einsum(rule, w, n, preferred_element_type=jnp.float32)
        for w, n in zip(wide, narrow)
    )


def line_sum(product):
    lines = product.shape[0]
    groups = [[line * 2 + x for line in range(lines)] for x in range(2)]
    return lax.psum_scatter(
        product, "seq", scatter_dimension=0, axis_index_groups=groups, tiled=True
    )[0]


def together(*arrays):
    return lax.optimization_barrier(arrays)


def precise_dot(left, right):
    return jnp.dot(left, right, precision=PRECISE, preferred_element_type=jnp.float32)


def plain_dot(left, right):
    return jnp.dot(left, right, preferred_element_type=jnp.float32)


def dot_right_t(left, right):
    return lax.dot_general(
        left, right, (((1,), (1,)), ((), ())), preferred_element_type=jnp.float32
    )


def dot_left_t(left, right):
    return lax.dot_general(
        left, right, (((0,), (0,)), ((), ())), preferred_element_type=jnp.float32
    )


def precise_left_t(left, right):
    return lax.dot_general(
        left, right, (((0,), (0,)), ((), ())), precision=PRECISE, preferred_element_type=jnp.float32
    )


def precise_right_t(left, right):
    return lax.dot_general(
        left, right, (((1,), (1,)), ((), ())), precision=PRECISE, preferred_element_type=jnp.float32
    )


def rms_scale(value):
    return lax.rsqrt(jnp.mean(value * value, axis=-1, keepdims=True) + EPSILON)


def split(value):
    high = value.astype(jnp.bfloat16)
    return high, (value - high.astype(jnp.float32)).astype(jnp.bfloat16)


def nn(left, right):
    return jnp.dot(left, right, preferred_element_type=jnp.float32)


def nt(left, right):
    return lax.dot_general(
        left, right, (((1,), (1,)), ((), ())), preferred_element_type=jnp.float32
    )


def two(product, left, right):
    high, low = split(right)
    return product(left, high) + product(left, low)


def three(product, left, right):
    left_high, left_low = split(left)
    right_high, right_low = split(right)
    return product(left_high, right_high) + (
        product(left_low, right_high) + product(left_high, right_low)
    )


def row_blocks(value):
    return [value[r : r + 8] for r in range(0, value.shape[0], 8)]


def exact_dot(left, right):
    return jnp.dot(left, right, precision=PRECISE, preferred_element_type=jnp.float32)


def triangle(size, upper):
    row = lax.broadcasted_iota(jnp.int32, (size, size), 0)
    column = lax.broadcasted_iota(jnp.int32, (size, size), 1)
    keep = row <= column if upper else row >= column
    return jnp.where(keep, 1.0, 0.0)


def spans(running, docs, span_s):
    size = running.shape[0]
    run, doc = row_blocks(running), row_blocks(docs)
    place = lax.broadcasted_iota(jnp.int32, (8, running.shape[1]), 0)
    for j in range(size):
        for r in range(j // 8, size // 8):
            ok = doc[r] == docs[j : j + 1]
            if r == j // 8 and j % 8:
                ok = ok & (place >= j % 8)
            span_s[j, 8 * r : 8 * r + 8] = jnp.where(ok, jnp.exp(run[r] - running[j : j + 1]), 0.0)


def to_end(running, docs):
    last = running.shape[0] - 1
    return jnp.where(
        docs == docs[last : last + 1], jnp.exp(running[last : last + 1] - running), 0.0
    )


def turned(to_end_weights, kept):
    size, slots = to_end_weights.shape
    fill = jnp.broadcast_to(kept, (128 - size, slots))
    both = jnp.concatenate([to_end_weights, fill], axis=0).T
    return both[:, :size], both[:, size : size + 1]


def read_kernel(
    q_ref, k_ref, v_ref, log_ref, new_ref, doc_ref, prev_ref, kin_ref, vin_ref,
    read_ref, score_ref, prob_ref, ks_ref, vs_ref, span_s,
):
    size = span_s.shape[0]
    lower = triangle(size, False)
    scaling = q_ref.shape[1] ** (-0.5)
    ks_ref[0] = kin_ref[...]
    vs_ref[0] = vin_ref[...]
    lane = lax.broadcasted_iota(jnp.int32, (8, size), 1)

    def chunk(i, carry):
        rows = pl.ds(pl.multiple_of(i * size, size), size)
        queries, keys, values = q_ref[rows, :], k_ref[rows, :], v_ref[rows, :]
        new, docs = new_ref[rows, :], doc_ref[rows, :]
        running = exact_dot(lower, log_ref[rows, :])
        carried = jnp.where(docs == prev_ref[rows, :], jnp.exp(running), 0.0)
        key_state, value_state = ks_ref[i], vs_ref[i]
        spans(running, docs, span_s)
        affinity = row_blocks(nt(queries, keys))
        scores = row_blocks(carried * two(nt, queries, key_state))
        for j in range(size):
            for r in range(j // 8, size // 8):
                weight = span_s[j, 8 * r : 8 * r + 8] * new[j : j + 1]
                scores[r] = scores[r] + weight * affinity[r][:, j : j + 1]
        scores = scaling * jnp.concatenate(scores, axis=0)
        probs = jnp.exp(scores - jnp.max(scores, axis=1, keepdims=True))
        probs = probs / jnp.sum(probs, axis=1, keepdims=True)
        score_ref[rows, :] = scores
        prob_ref[rows, :] = probs
        used = probs.astype(jnp.bfloat16).astype(jnp.float32)
        part = row_blocks(used)
        mixing = [jnp.zeros((8, size), jnp.float32) for _ in part]
        for j in range(size):
            for r in range(j // 8, size // 8):
                weight = span_s[j, 8 * r : 8 * r + 8] * new[j : j + 1]
                total = jnp.sum(part[r] * weight, axis=1, keepdims=True)
                mixing[r] = jnp.where(lane == j, total, mixing[r])
        high, low = split(jnp.concatenate(mixing, axis=0))
        read_ref[rows, :] = (
            three(nn, used * carried, value_state) + nn(high, values) + nn(low, values)
        )
        end, kept = turned(to_end(running, docs) * new, carried[size - 1 : size])
        high, low = split(end)
        ks_ref[i + 1] = kept * key_state + (nn(high, keys) + nn(low, keys))
        vs_ref[i + 1] = kept * value_state + (nn(high, values) + nn(low, values))
        return carry

    lax.fori_loop(0, q_ref.shape[0] // size, chunk, 0)


def back_query_kernel(
    q_ref, k_ref, v_ref, log_ref, new_ref, doc_ref, prev_ref, score_ref, prob_ref, ks_ref, vs_ref, g_ref,
    dq_ref, dk_ref, dv_ref, held_ref, gained_ref, xk_ref, xv_ref, dkin_ref, dvin_ref, span_s,
):
    size = span_s.shape[0]
    count = q_ref.shape[0] // size
    lower = triangle(size, False)
    scaling = q_ref.shape[1] ** (-0.5)
    dkin_ref[...] = jnp.zeros_like(dkin_ref)
    dvin_ref[...] = jnp.zeros_like(dvin_ref)
    lane = lax.broadcasted_iota(jnp.int32, (8, size), 1)

    def chunk(turn, carry):
        i = count - 1 - turn
        start = pl.multiple_of(i * size, size)
        rows = pl.ds(start, size)
        queries, keys, values, grads = q_ref[rows, :], k_ref[rows, :], v_ref[rows, :], g_ref[rows, :]
        new, docs = new_ref[rows, :], doc_ref[rows, :]
        running = exact_dot(lower, log_ref[rows, :])
        carried = jnp.where(docs == prev_ref[rows, :], jnp.exp(running), 0.0)
        spans(running, docs, span_s)
        affinity = row_blocks(nt(queries, keys))
        grad_high, grad_low = split(grads)
        pull = row_blocks(nt(grad_high, values) + nt(grad_low, values))
        back = row_blocks(carried * three(nt, grads, vs_ref[i]))
        for j in range(size):
            for r in range(j // 8, size // 8):
                weight = span_s[j, 8 * r : 8 * r + 8] * new[j : j + 1]
                back[r] = back[r] + weight * pull[r][:, j : j + 1]
        back = jnp.concatenate(back, axis=0)
        probs = prob_ref[rows, :]
        used = probs.astype(jnp.bfloat16).astype(jnp.float32)
        inner = probs * (back - jnp.sum(probs * back, axis=1, keepdims=True))
        gained_ref[rows, :] = inner * score_ref[rows, :] + used * back
        outer = scaling * inner
        part, used_part = row_blocks(outer), row_blocks(used)
        key_mix = [jnp.zeros((8, size), jnp.float32) for _ in part]
        value_mix = [jnp.zeros((8, size), jnp.float32) for _ in part]
        for j in range(size):
            held = None
            for r in range(j // 8, size // 8):
                span = span_s[j, 8 * r : 8 * r + 8]
                key_side, value_side = part[r] * span, used_part[r] * span
                own = key_side * affinity[r][:, j : j + 1] + value_side * pull[r][:, j : j + 1]
                held = own if held is None else held + own
                fresh = new[j : j + 1]
                key_mix[r] = jnp.where(
                    lane == j, jnp.sum(key_side * fresh, axis=1, keepdims=True), key_mix[r]
                )
                value_mix[r] = jnp.where(
                    lane == j, jnp.sum(value_side * fresh, axis=1, keepdims=True), value_mix[r]
                )
            held_ref[pl.ds(start + j, 1), :] = jnp.sum(held, axis=0, keepdims=True)
        key_mix = jnp.concatenate(key_mix, axis=0)
        value_mix = jnp.concatenate(value_mix, axis=0)
        outer_in, used_in = outer * carried, used * carried
        high, low = split(key_mix)
        dq_ref[rows, :] = three(nn, outer_in, ks_ref[i]) + (nn(high, keys) + nn(low, keys))
        fill = jnp.zeros((128 - size, size), jnp.float32)
        high, low = split(jnp.concatenate([key_mix, fill], axis=0).T[:, :size])
        dk_ref[rows, :] = nn(high, queries) + nn(low, queries)
        mixed = jnp.concatenate([value_mix, fill], axis=0).T[:, :size]
        dv_ref[rows, :] = three(nn, mixed, grads)
        outer_t, kept = turned(outer_in, carried[size - 1 : size])
        used_t, kept = turned(used_in, carried[size - 1 : size])
        high, low = split(outer_t)
        to_key = nn(high, queries) + nn(low, queries)
        to_value = three(nn, used_t, grads)
        xk_ref[i] = to_key
        xv_ref[i] = to_value
        dkin_ref[...] = kept * dkin_ref[...] + to_key
        dvin_ref[...] = kept * dvin_ref[...] + to_value
        return carry

    lax.fori_loop(0, count, chunk, 0)


def back_key_kernel(
    k_ref, v_ref, log_ref, new_ref, doc_ref, prev_ref, dk_in_ref, dv_in_ref, held_ref, gained_ref,
    xk_ref, xv_ref, dkend_ref, dvend_ref, total_ref,
    dk_ref, dv_ref, dlog_ref, ks, vs, total,
):
    size = CHUNK
    count = k_ref.shape[0] // size
    lower, upper = triangle(size, False), triangle(size, True)
    ks[...] = dkend_ref[...]
    vs[...] = dvend_ref[...]
    total[...] = total_ref[...]

    def chunk(turn, carry):
        i = count - 1 - turn
        rows = pl.ds(pl.multiple_of(i * size, size), size)
        keys, values = k_ref[rows, :], v_ref[rows, :]
        logs, new, docs = log_ref[rows, :], new_ref[rows, :], doc_ref[rows, :]
        running = exact_dot(lower, logs)
        carried = jnp.where(docs == prev_ref[rows, :], jnp.exp(running), 0.0)
        end = to_end(running, docs)
        weight = end * new
        dk_ref[rows, :] = (dk_in_ref[rows, :] + three(nn, weight, ks[...])).astype(dk_ref.dtype)
        dv_ref[rows, :] = (dv_in_ref[rows, :] + three(nn, weight, vs[...])).astype(dv_ref.dtype)
        held = held_ref[rows, :] + end * (two(nt, keys, ks[...]) + two(nt, values, vs[...]))
        change = gained_ref[rows, :] - new * held
        after = exact_dot(upper, change) + total[...]
        dlog_ref[rows, :] = after - jnp.exp(logs) * held
        total[...] = after[:1]
        unused, kept = turned(carried, carried[size - 1 : size])
        ks[...] = kept * ks[...] + xk_ref[i]
        vs[...] = kept * vs[...] + xv_ref[i]
        return carry

    lax.fori_loop(0, count, chunk, 0)


def cost(flops, moved):
    return pl.CostEstimate(flops=flops, bytes_accessed=moved, transcendentals=0)


def read_slots(queries, keys, values, logs, new, docs, prev, key_in, value_in):
    rows, width = queries.shape
    slots = logs.shape[1]
    count = rows // CHUNK
    f32 = jnp.float32
    return pl.pallas_call(
        read_kernel,
        out_shape=(
            jax.ShapeDtypeStruct((rows, width), f32),
            jax.ShapeDtypeStruct((rows, slots), f32),
            jax.ShapeDtypeStruct((rows, slots), f32),
            jax.ShapeDtypeStruct((count + 1, slots, width), f32),
            jax.ShapeDtypeStruct((count + 1, slots, width), f32),
        ),
        scratch_shapes=[pltpu.VMEM((CHUNK, CHUNK, slots), f32)],
        compiler_params=pltpu.CompilerParams(vmem_limit_bytes=VMEM),
        cost_estimate=cost(READ_COST, 5 << 20),
    )(queries, keys, values, logs, new, docs, prev, key_in, value_in)


def back_query(queries, keys, values, logs, new, docs, prev, scores, probs, key_states, value_states, grads):
    rows, width = queries.shape
    slots = logs.shape[1]
    count = rows // CHUNK
    f32 = jnp.float32
    narrow = jax.ShapeDtypeStruct((rows, slots), f32)
    wide = jax.ShapeDtypeStruct((rows, width), f32)
    states = jax.ShapeDtypeStruct((count, slots, width), f32)
    state = jax.ShapeDtypeStruct((slots, width), f32)
    return pl.pallas_call(
        back_query_kernel,
        out_shape=(wide, wide, wide, narrow, narrow, states, states, state, state),
        scratch_shapes=[pltpu.VMEM((CHUNK, CHUNK, slots), f32)],
        compiler_params=pltpu.CompilerParams(vmem_limit_bytes=VMEM),
        cost_estimate=cost(BACK_COST, 10 << 20),
    )(queries, keys, values, logs, new, docs, prev, scores, probs, key_states, value_states, grads)


def back_key(keys, values, logs, new, docs, prev, dk, dv, held, gained, xk, xv, dk_end, dv_end, total):
    rows, width = keys.shape
    slots = logs.shape[1]
    f32 = jnp.float32
    wide = jax.ShapeDtypeStruct((rows, width), jnp.bfloat16)
    return pl.pallas_call(
        back_key_kernel,
        out_shape=(wide, wide, jax.ShapeDtypeStruct((rows, slots), f32)),
        scratch_shapes=[
            pltpu.VMEM((slots, width), f32),
            pltpu.VMEM((slots, width), f32),
            pltpu.VMEM((1, slots), f32),
        ],
        compiler_params=pltpu.CompilerParams(vmem_limit_bytes=VMEM),
        cost_estimate=cost(READ_COST, 8 << 20),
    )(keys, values, logs, new, docs, prev, dk, dv, held, gained, xk, xv, dk_end, dv_end, total)


def other_of(place, by):
    return place + by * (1 - 2 * ((place // by) % 2))


def exchange_kernel(names, count, heads, reverse, *refs):
    refs = dict(zip(names, refs))
    wides = [n for n in names if n.startswith("wide_in")]
    narrows = [n for n in names if n.startswith("narrow_in")]
    place, head = lax.axis_index("seq"), lax.axis_index("head")
    partner, sibling = {"seq": other_of(place, 1)}, {"head": other_of(head, 1)}
    line = -1 if reverse else 1
    ahead = count - 1 - place if reverse else place
    left = count - 1 - ahead
    spans_of = [1 << k for k in range(count.bit_length() - 1)]
    hops = [1 << k for k in range(1, heads.bit_length() - 1)]

    greeted = []
    if wides or narrows:
        greeted.append((partner, None))
    if wides or "part" in refs:
        greeted.append((sibling, None))
    if "part" in refs:
        greeted += [({"head": other_of(head, by)}, None) for by in hops]
    if "state" in refs:
        greeted += [({"seq": place + line * by}, left >= by) for by in spans_of]
        greeted += [({"seq": place - line * by}, ahead >= by) for by in spans_of]
    barrier = pltpu.get_barrier_semaphore()
    total = 0
    for device, ok in greeted:
        if ok is None:
            pl.semaphore_signal(barrier, inc=1, device_id=device, device_id_type=MESH)
            total = total + 1
        else:

            @pl.when(ok)
            def _(device=device):
                pl.semaphore_signal(barrier, inc=1, device_id=device, device_id_type=MESH)

            total = total + ok.astype(jnp.int32)
    pl.semaphore_wait(barrier, total)

    def copy(source, target, sems, device):
        return pltpu.make_async_remote_copy(
            src_ref=source, dst_ref=target, send_sem=sems[0], recv_sem=sems[1],
            device_id=device, device_id_type=MESH,
        )

    def sems(name, i):
        return refs[name + "_send"].at[i], refs[name + "_recv"].at[i]

    def half_of(ref):
        size = ref.shape[0] // 2
        return ref.at[pl.ds((head % 2) * size, size)]

    waits, forwards, states = [], [], []
    if "state" in refs:
        inside, received, before = refs["inside"], refs["received"], refs["before"]
        inside[0] = refs["state"][...]
        states = [
            copy(inside.at[k], received.at[k], sems("state", k), {"seq": place + line * by})
            for k, by in enumerate(spans_of)
        ]

        @pl.when(left >= 1)
        def _():
            states[0].start()

    if "part" in refs:
        part, added = refs["part"], refs["sum"]
        rows = part.shape[0] // CHUNKS
        half = rows // 2
        low = head % 2
        for c in range(CHUNKS):
            start = pl.multiple_of(c * rows + (1 - low) * half, 8)
            moved = copy(part.at[pl.ds(start, half)], refs["near"].at[c], sems("near", c), sibling)
            moved.start()
            waits.append(moved)
    for i, name in enumerate(wides):
        moved = copy(
            half_of(refs[name]), half_of(refs[name.replace("in", "out")]), sems("wide", i), partner
        )
        moved.start()
        forwards.append((name.replace("in", "out"), moved))
    for i, name in enumerate(narrows):
        moved = copy(refs[name], refs[name.replace("in", "out")], sems("narrow", i), partner)
        moved.start()
        waits.append(moved)

    if "state" in refs:
        lane = lax.broadcasted_iota(jnp.int32, before.shape, 1)
        before[...] = jnp.where(lane < 128, 1.0, 0.0)

        def composed(earlier, later):
            return later[:, :1] * earlier + jnp.where(lane >= 128, later, 0.0)

        for k, by in enumerate(spans_of):
            moved = states[k]
            if k:

                @pl.when(left >= by)
                def _(moved=moved):
                    moved.start()

            if k + 1 < len(spans_of):
                inside[k + 1] = inside[k]

            @pl.when(ahead >= by)
            def _(k=k, moved=moved):
                moved.wait_recv()
                before[...] = composed(received[k], before[...])
                if k + 1 < len(spans_of):
                    inside[k + 1] = composed(received[k], inside[k])

            @pl.when(left >= by)
            def _(moved=moved):
                moved.wait_send()

    if "part" in refs:
        own, arrived = refs["own"], refs["arrived"]
        across = []
        for c in range(CHUNKS):
            waits[c].wait_recv()
            start = pl.multiple_of(c * rows + low * half, 8)
            own[0, c] = part[pl.ds(start, half), :] + refs["near"][c]
            moved = copy(
                own.at[0, c], arrived.at[0, c], sems("across", c), {"head": other_of(head, 2)}
            )
            moved.start()
            across.append(moved)
        for k in range(1, len(hops)):
            later = []
            for c in range(CHUNKS):
                across[c].wait()
                own[k, c] = own[k - 1, c] + arrived[k - 1, c]
                moved = copy(
                    own.at[k, c], arrived.at[k, c], sems("across", k * CHUNKS + c),
                    {"head": other_of(head, hops[k])},
                )
                moved.start()
                later.append(moved)
            across = later
        back = []
        k = len(hops) - 1
        for c in range(CHUNKS):
            across[c].wait()
            start = pl.multiple_of(c * rows + low * half, 8)
            mine = pl.ds(start, half)
            added[mine, :] = own[k, c] + arrived[k, c]
            moved = copy(added.at[mine], added.at[mine], sems("back", c), sibling)
            moved.start()
            back.append(moved)
        for c in range(CHUNKS):
            waits[c].wait_send()
            back[c].wait()
        waits = waits[CHUNKS:]
    for i, (name, moved) in enumerate(forwards):
        moved.wait()
        onward = copy(half_of(refs[name]), half_of(refs[name]), sems("onward", i), sibling)
        onward.start()
        waits.append(onward)
    for moved in waits:
        moved.wait()


def exchange(number, part=None, state=None, reverse=False, wides=(), narrows=()):
    count, heads = lax.axis_size("seq"), lax.axis_size("head")
    f32 = jnp.float32
    vmem, hbm = pl.BlockSpec(memory_space=pltpu.VMEM), pl.BlockSpec(memory_space=pl.ANY)
    ins, outs, scratch = [], [], []
    if part is not None:
        ins.append(("part", part, vmem))
        outs.append(("sum", part, vmem))
        half = (CHUNKS, part.shape[0] // CHUNKS // 2, part.shape[1])
        steps = heads.bit_length() - 2
        scratch += [
            ("near", pltpu.VMEM(half, f32)),
            ("own", pltpu.VMEM((steps,) + half, f32)),
            ("arrived", pltpu.VMEM((steps,) + half, f32)),
        ]
        for name, size in (("near", CHUNKS), ("across", steps * CHUNKS), ("back", CHUNKS)):
            scratch += [(name + end, pltpu.SemaphoreType.DMA((size,))) for end in ("_send", "_recv")]
    if state is not None:
        ins.append(("state", state, vmem))
        outs.append(("before", state, vmem))
        steps = count.bit_length() - 1
        scratch += [(n, pltpu.VMEM((steps,) + state.shape, f32)) for n in ("inside", "received")]
        scratch += [("state" + end, pltpu.SemaphoreType.DMA((steps,))) for end in ("_send", "_recv")]
    for kind, arrays in (("wide", wides), ("narrow", narrows)):
        ins += [(f"{kind}_in{i}", a, hbm) for i, a in enumerate(arrays)]
        outs += [(f"{kind}_out{i}", a, hbm) for i, a in enumerate(arrays)]
        for name in (kind, "onward") if kind == "wide" else (kind,):
            if arrays:
                scratch += [
                    (name + end, pltpu.SemaphoreType.DMA((len(arrays),))) for end in ("_send", "_recv")
                ]
    names = [n for n, *_ in ins] + [n for n, *_ in outs] + [n for n, _ in scratch]
    return pl.pallas_call(
        functools.partial(exchange_kernel, names, count, heads, reverse),
        out_shape=tuple(jax.ShapeDtypeStruct(a.shape, f32) for _, a, _ in outs),
        in_specs=[spec for *_, spec in ins],
        out_specs=tuple(spec for *_, spec in outs),
        scratch_shapes=[s for _, s in scratch],
        compiler_params=pltpu.CompilerParams(
            collective_id=number, has_side_effects=True, vmem_limit_bytes=VMEM
        ),
        cost_estimate=cost(40 << 30, 16 << 20),
    )(*[a for _, a, _ in ins])


def scatter_kernel(count, in_ref, out_ref, slots, send, receive):
    place = lax.axis_index("seq")
    others = [{"seq": lax.rem(place + k, count)} for k in range(1, count)]
    barrier = pltpu.get_barrier_semaphore()
    for device in others:
        pl.semaphore_signal(barrier, inc=1, device_id=device, device_id_type=MESH)
    pl.semaphore_wait(barrier, count - 1)
    copies = []
    for k, device in enumerate(others):
        moved = pltpu.make_async_remote_copy(
            src_ref=in_ref.at[device["seq"]], dst_ref=slots.at[place],
            send_sem=send.at[k], recv_sem=receive.at[k], device_id=device, device_id_type=MESH,
        )
        moved.start()
        copies.append(moved)
    slots[place] = in_ref[place]
    for moved in copies:
        moved.wait()
    total = slots[0]
    for i in range(1, count):
        total = total + slots[i]
    out_ref[...] = total


def scatter_sum(number, array):
    count = array.shape[0]
    vmem = pl.BlockSpec(memory_space=pltpu.VMEM)
    return pl.pallas_call(
        functools.partial(scatter_kernel, count),
        out_shape=jax.ShapeDtypeStruct(array.shape[1:], jnp.float32),
        in_specs=[vmem],
        out_specs=vmem,
        scratch_shapes=[
            pltpu.VMEM(array.shape, jnp.float32),
            pltpu.SemaphoreType.DMA((count - 1,)),
            pltpu.SemaphoreType.DMA((count - 1,)),
        ],
        compiler_params=pltpu.CompilerParams(
            collective_id=number, has_side_effects=True, vmem_limit_bytes=VMEM
        ),
        cost_estimate=cost(4 << 30, 1 << 20),
    )(array)


def state_of(keep, keys, values):
    return jnp.concatenate([jnp.broadcast_to(keep[:, None], (keep.shape[0], 128)), keys, values], axis=1)


def body(
    stream,
    seg_ids,
    attn_gain,
    w_query,
    w_key,
    w_value,
    w_outgate,
    w_low,
    w_slot,
    forget_bias,
    head_gain,
    w_out,
    mlp_gain,
    w_gate,
    w_up,
    w_down,
    cotangent,
):
    tok_rows = stream.shape[0]
    width = stream.shape[1]
    slots = w_slot.shape[2]
    head_width = w_query.shape[1]
    prior = passed_along(seg_ids[tok_rows - 1 :], "seq", 1)[0]
    stream_f = stream.astype(jnp.float32)
    scale_in = rms_scale(stream_f)
    normed_in = (stream_f * scale_in * attn_gain).astype(jnp.bfloat16)
    query_rows = plain_dot(normed_in, w_query).astype(jnp.bfloat16)
    key_rows = plain_dot(normed_in, w_key).astype(jnp.bfloat16)
    value_rows = plain_dot(normed_in, w_value).astype(jnp.bfloat16)
    gate_act = plain_dot(normed_in, w_outgate)
    ranked = plain_dot(normed_in, w_low)

    def decay_logs(ranked_in, slot_map, bias_row):
        return jax.nn.log_sigmoid(precise_dot(ranked_in, slot_map[0]) + bias_row[0]) / GATE_NORM

    log_decay, gate_pull = jax.vjp(decay_logs, ranked, w_slot, forget_bias)

    new = -jnp.expm1(log_decay)
    last_doc = seg_ids[tok_rows - 1]
    running = precise_dot(jnp.tril(jnp.ones((tok_rows, tok_rows), jnp.float32)), log_decay)
    total = running[tok_rows - 1]
    in_last = (seg_ids == last_doc)[:, None]
    factor = jnp.where(in_last, jnp.exp(jnp.where(in_last, total - running, 0.0)) * new, 0.0)
    docs = seg_ids.astype(jnp.float32)
    before = jnp.concatenate([prior.astype(jnp.float32)[None], docs[CHUNK - 1 : -1 : CHUNK]])
    docs = jnp.broadcast_to(docs[:, None], (tok_rows, slots))
    before = jnp.broadcast_to(jnp.repeat(before, CHUNK)[:, None], (tok_rows, slots))

    def with_partner(own, received):
        return own, received.astype(jnp.bfloat16)

    def wide_float(array):
        return array.astype(jnp.float32)

    local_key = precise_left_t(factor, key_rows.astype(jnp.float32))
    local_value = precise_left_t(factor, value_rows.astype(jnp.float32))
    decay_all = jnp.where(last_doc == prior, jnp.exp(total), 0.0)
    (prefix,) = exchange(0, state=state_of(decay_all, local_key, local_value))
    key_in, value_in = prefix[:, 128 : 128 + head_width], prefix[:, 128 + head_width :]
    d_act = dot_right_t(cotangent, w_down)
    key_in, d_act = together(key_in, d_act)
    own_dy, their_dy = width_blocks(cotangent)
    own_in, their_in = width_blocks(normed_in)
    slot_read, scores, probs, key_states, value_states = read_slots(
        query_rows, key_rows, value_rows, log_decay, new, docs, before, key_in, value_in
    )
    scale_read = rms_scale(slot_read)
    normed_read = slot_read * scale_read * head_gain[0]
    gate_sig = jax.nn.sigmoid(gate_act)
    gate_silu = gate_act * gate_sig
    mixed_heads = (normed_read * gate_silu).astype(jnp.bfloat16)
    branch, from_dy, from_in = exchange(
        1, part=plain_dot(mixed_heads, w_out), wides=(their_dy, their_in)
    )
    wide_dy = with_partner(own_dy, from_dy)
    wide_in = with_partner(own_in, from_in)
    hidden = stream_f + branch
    scale_mid = rms_scale(hidden)
    normed_mid = (hidden * scale_mid * mlp_gain).astype(jnp.bfloat16)
    gate_pre = plain_dot(normed_mid, w_gate)
    up_pre = plain_dot(normed_mid, w_up)
    pre_sig = jax.nn.sigmoid(gate_pre)
    pre_silu = gate_pre * pre_sig
    ffn_act = (pre_silu * up_pre).astype(jnp.bfloat16)
    upstream = cotangent.astype(jnp.float32)
    d_gate = (d_act * up_pre * pre_sig * (1.0 + gate_pre * (1.0 - pre_sig))).astype(jnp.bfloat16)
    d_up = (d_act * pre_silu).astype(jnp.bfloat16)
    d_mid, from_act = exchange(
        2,
        part=dot_right_t(d_gate, w_gate) + dot_right_t(d_up, w_up),
        narrows=(wide_float(ffn_act),),
    )
    grad_down = pair_product(wide_dy, with_partner(ffn_act, from_act), False)
    d_mid, grad_down = together(d_mid, grad_down)
    grad_down = line_sum(grad_down)
    own_mid, their_mid = width_blocks(normed_mid)
    ffn_part, d_mid = together(plain_dot(ffn_act, w_down), d_mid)
    ffn_out, from_mid, from_gate = exchange(
        3, part=ffn_part, wides=(their_mid,), narrows=(wide_float(d_gate),)
    )
    wide_mid = with_partner(own_mid, from_mid)
    grad_gate = pair_product(wide_mid, with_partner(d_gate, from_gate), True)
    d_mid, grad_gate = together(d_mid, grad_gate)
    grad_mlp_gain = jnp.sum(d_mid * hidden * scale_mid, axis=0)
    scaled_mid = d_mid * mlp_gain
    d_hidden = (
        upstream
        + scale_mid * scaled_mid
        - hidden * scale_mid**3 * jnp.mean(scaled_mid * hidden, axis=1, keepdims=True)
    )
    d_branch = d_hidden.astype(jnp.bfloat16)
    d_mixed = dot_right_t(d_branch, w_out)
    own_branch, their_branch = width_blocks(d_branch)
    d_gate_act = (d_mixed * normed_read * gate_sig * (1.0 + gate_act * (1.0 - gate_sig))).astype(
        jnp.bfloat16
    )
    d_normed = d_mixed * gate_silu
    grad_head_gain = jnp.sum(d_normed * slot_read * scale_read, axis=0)[None, :]
    scaled_read = d_normed * head_gain[0]
    d_read = scale_read * scaled_read - slot_read * scale_read**3 * jnp.mean(
        scaled_read * slot_read, axis=1, keepdims=True
    )
    grad_gate, grad_down, unused_read = together(grad_gate, grad_down, d_read)
    grad_gate = line_sum(grad_gate)
    d_query, d_key, d_value, held, gained, to_keys, to_values, key_back, value_back = back_query(
        query_rows, key_rows, value_rows, log_decay, new, docs, before, scores, probs, key_states, value_states, d_read
    )
    query_back = d_query.astype(jnp.bfloat16)
    suffix, from_up, from_outgate = exchange(
        4,
        state=state_of(decay_all, key_back, value_back),
        reverse=True,
        narrows=(wide_float(d_up), wide_float(d_gate_act)),
    )
    grad_up = pair_product(wide_mid, with_partner(d_up, from_up), True)
    key_end, value_end = suffix[:, 128 : 128 + head_width], suffix[:, 128 + head_width :]
    end_total = jnp.sum(key_states[-1] * key_end + value_states[-1] * value_end, axis=1)[None, :]
    d_key, grad_up = together(d_key, grad_up)
    grad_up, grad_gate = together(grad_up, grad_gate)
    grad_up = line_sum(grad_up)
    key_back, value_back, d_logs = back_key(
        key_rows, value_rows, log_decay, new, docs, before, d_key, d_value, held, gained,
        to_keys, to_values, key_end, value_end, end_total,
    )
    d_ranked, grad_slot, grad_bias = gate_pull(d_logs)
    normed_f = normed_in.astype(jnp.float32)
    grad_low = precise_left_t(normed_f, d_ranked)
    d_in_part = (
        dot_right_t(query_back, w_query)
        + dot_right_t(key_back, w_key)
        + dot_right_t(value_back, w_value)
        + dot_right_t(d_gate_act, w_outgate)
        + precise_right_t(d_ranked, w_low.astype(jnp.float32))
    )
    d_in, from_branch, *from_mixer = exchange(
        5,
        part=d_in_part,
        wides=(their_branch,),
        narrows=[wide_float(a) for a in (query_back, key_back, value_back, mixed_heads)],
    )
    from_mixed = from_mixer.pop()
    from_mixer = [from_outgate, *from_mixer]
    wide_branch = with_partner(own_branch, from_branch)
    grad_out = pair_product(wide_branch, with_partner(mixed_heads, from_mixed), False)
    own_mixer = jnp.concatenate([d_gate_act, query_back, key_back, value_back], axis=1)
    their_mixer = jnp.concatenate([a.astype(jnp.bfloat16) for a in from_mixer], axis=1)
    grad_mixer = pair_product(wide_in, (own_mixer, their_mixer), True)
    grad_out, grad_up, d_in = together(grad_out, grad_up, d_in)
    grad_out = line_sum(grad_out)
    grad_mixer = line_sum(grad_mixer)
    grad_outgate, grad_query, grad_key, grad_value = jnp.split(grad_mixer, 4, axis=1)
    result = hidden + ffn_out
    squares = jnp.stack(
        [jnp.sum(stream_f * stream_f), jnp.sum(hidden * hidden), jnp.sum(result * result)]
    )
    grad_attn_gain = jnp.sum(d_in * stream_f * scale_in, axis=0)
    scaled_in = d_in * attn_gain
    grad_stream = (
        d_hidden
        + scale_in * scaled_in
        - stream_f * scale_in**3 * jnp.mean(scaled_in * stream_f, axis=1, keepdims=True)
    ).astype(jnp.bfloat16)
    count = lax.axis_size("seq")
    small = [
        grad_attn_gain.reshape(count, -1),
        grad_mlp_gain.reshape(count, -1),
        grad_low.reshape(count, -1),
        jnp.moveaxis(grad_slot[0].reshape(-1, count, slots // count), 1, 0).reshape(count, -1),
        grad_bias.reshape(count, -1),
        grad_head_gain.reshape(count, -1),
        jnp.broadcast_to(squares, (count, 3)),
    ]
    sizes = [a.shape[1] for a in small]
    packed = jnp.concatenate(small, axis=1)
    packed = jnp.pad(packed, ((0, 0), (0, -packed.shape[1] % 1024)))
    packed = scatter_sum(6, packed.reshape(count, -1, 128)).reshape(-1)
    ends = [sum(sizes[: i + 1]) for i in range(len(sizes))]
    small = [packed[end - size : end] for end, size in zip(ends, sizes)]
    stream_rms = jnp.sqrt(small[6] / (tok_rows * count * width))
    summed = (
        small[0],
        grad_query,
        grad_key,
        grad_value,
        grad_outgate,
        small[2].reshape(width // count, -1),
        small[3].reshape(1, -1, slots // count),
        small[4][None, :],
        small[5][None, :],
        grad_out,
        small[1],
        grad_gate,
        grad_up,
        grad_down,
    )
    mixer_parts = summed[:10]
    ffn_parts = summed[10:]
    return (
        result.astype(jnp.bfloat16),
        grad_stream,
        mixer_parts[0],
        mixer_parts[1],
        mixer_parts[2],
        mixer_parts[3],
        mixer_parts[4],
        mixer_parts[5],
        mixer_parts[6],
        mixer_parts[7],
        mixer_parts[8],
        mixer_parts[9],
        ffn_parts[0],
        ffn_parts[1],
        ffn_parts[2],
        ffn_parts[3],
        stream_rms,
    )


def solution(mesh):
    in_specs = (
        P("seq", None),
        P("seq"),
        P(),
        P(None, "head"),
        P(None, "head"),
        P(None, "head"),
        P(None, "head"),
        P(None, "head"),
        P("head", None, None),
        P("head", None),
        P("head", None),
        P("head", None),
        P(),
        P(None, "head"),
        P(None, "head"),
        P("head", None),
        P("seq", None),
    )
    out_specs = (
        P("seq", None),
        P("seq", None),
        P("seq"),
        P("seq", "head"),
        P("seq", "head"),
        P("seq", "head"),
        P("seq", "head"),
        P("seq", "head"),
        P("head", None, "seq"),
        P("head", "seq"),
        P("head", "seq"),
        P("head", "seq"),
        P("seq"),
        P("seq", "head"),
        P("seq", "head"),
        P("head", "seq"),
        P(),
    )
    return jax.shard_map(body, mesh=mesh, in_specs=in_specs, out_specs=out_specs, check_vma=False)
```

```python
import functools

import jax
import jax.numpy as jnp
from jax import lax
from jax.experimental import pallas as pl
from jax.experimental.pallas import tpu as pltpu
from jax.sharding import PartitionSpec as P

CHUNK = 32
CHUNKS = 4
MESH = pl.DeviceIdType.MESH
VMEM = 50 << 20
READ_COST = 17 << 30


EPSILON = 1e-06
GATE_NORM = 8.0
PRECISE = lax.Precision.HIGHEST


def width_blocks(array, parity):
    count = lax.axis_size("seq")
    wide = array.shape[1] // count
    return jnp.stack(
        [
            lax.dynamic_slice_in_dim(array, (2 * line + parity) * wide, wide, 1)
            for line in range(count // 2)
        ]
    )


def whole_tiles(array):
    return array.shape[1] // lax.axis_size("seq") % 128 == 0


def wide_to_send(array):
    array = array.astype(jnp.float32)
    if whole_tiles(array):
        return array
    return width_blocks(array, 1 - lax.axis_index("seq") % 2)


def product_kernel(layout, *refs):
    out_ref, sides = refs[-2:]
    refs = list(refs[1:-2])
    first = pl.program_id(0) == 0
    at = 0
    for narrows in layout:
        own, theirs = refs.pop(0), refs.pop(0)
        block = jnp.concatenate(
            [own[...].reshape(own.shape[-2:]), theirs[0].astype(jnp.bfloat16)], axis=0
        )
        for _ in range(narrows):
            own_narrow, their_narrow = refs.pop(0), refs.pop(0)
            rows, size = own_narrow.shape

            @pl.when(first)
            def _(at=at, own_narrow=own_narrow, their_narrow=their_narrow, rows=rows, size=size):
                sides[:rows, at : at + size] = own_narrow[...]
                sides[rows:, at : at + size] = their_narrow[...].astype(jnp.bfloat16)

            out_ref[0, :, at : at + size] = tn(block, sides[:, at : at + size])
            at += size


def pair_products(*jobs):
    count = lax.axis_size("seq")
    lines = count // 2
    parity = lax.axis_index("seq") % 2
    ins, specs, total = [], [], 0
    for (own, theirs), narrows in jobs:
        rows, wide = own.shape[0], own.shape[1] // count
        if whole_tiles(own):
            ins.append(own)
            specs.append(pl.BlockSpec((rows, wide), lambda i, p: (0, 2 * i + p[0])))
        else:
            ins.append(width_blocks(own, parity))
            specs.append(pl.BlockSpec((1, rows, wide), lambda i, p: (i, 0, 0)))
        ins.append(theirs)
        specs.append(pl.BlockSpec((1, rows, wide), lambda i, p: (i, 0, 0)))
        for pair in narrows:
            for side in pair:
                ins.append(side)
                specs.append(pl.BlockSpec(side.shape, lambda i, p: (0, 0)))
            total += pair[0].shape[1]
    return pl.pallas_call(
        functools.partial(product_kernel, [len(narrows) for _, narrows in jobs]),
        out_shape=jax.ShapeDtypeStruct((lines, wide, total), jnp.float32),
        grid_spec=pltpu.PrefetchScalarGridSpec(
            num_scalar_prefetch=1,
            grid=(lines,),
            in_specs=specs,
            out_specs=pl.BlockSpec((1, wide, total), lambda i, p: (i, 0, 0)),
            scratch_shapes=[pltpu.VMEM((2 * rows, total), jnp.bfloat16)],
        ),
        compiler_params=pltpu.CompilerParams(vmem_limit_bytes=VMEM),
        cost_estimate=cost(4 * rows * wide * lines * total, 8 * wide * lines * total),
    )(parity.reshape(1).astype(jnp.int32), *ins)


def line_sum(product):
    lines = product.shape[0]
    groups = [[line * 2 + x for line in range(lines)] for x in range(2)]
    return lax.psum_scatter(
        product, "seq", scatter_dimension=0, axis_index_groups=groups, tiled=True
    )[0]


def together(*arrays):
    return lax.optimization_barrier(arrays)


def precise_dot(left, right):
    return jnp.dot(left, right, precision=PRECISE, preferred_element_type=jnp.float32)


def plain_dot(left, right):
    return jnp.dot(left, right, preferred_element_type=jnp.float32)


def dot_right_t(left, right):
    return lax.dot_general(
        left, right, (((1,), (1,)), ((), ())), preferred_element_type=jnp.float32
    )


def dot_left_t(left, right):
    return lax.dot_general(
        left, right, (((0,), (0,)), ((), ())), preferred_element_type=jnp.float32
    )


def precise_left_t(left, right):
    return lax.dot_general(
        left, right, (((0,), (0,)), ((), ())), precision=PRECISE, preferred_element_type=jnp.float32
    )


def precise_right_t(left, right):
    return lax.dot_general(
        left, right, (((1,), (1,)), ((), ())), precision=PRECISE, preferred_element_type=jnp.float32
    )


def rms_scale(value):
    return lax.rsqrt(jnp.mean(value * value, axis=-1, keepdims=True) + EPSILON)


def split(value):
    high = value.astype(jnp.bfloat16)
    return high, (value - high.astype(jnp.float32)).astype(jnp.bfloat16)


def nn(left, right):
    return jnp.dot(left, right, preferred_element_type=jnp.float32)


def nt(left, right):
    return lax.dot_general(
        left, right, (((1,), (1,)), ((), ())), preferred_element_type=jnp.float32
    )


def tn(left, right):
    return lax.dot_general(
        left, right, (((0,), (0,)), ((), ())), preferred_element_type=jnp.float32
    )


def two(product, left, right):
    high, low = split(right)
    return product(left, high) + product(left, low)


def three(product, left, right):
    left_high, left_low = split(left)
    right_high, right_low = split(right)
    return product(left_high, right_high) + (
        product(left_low, right_high) + product(left_high, right_low)
    )


def row_blocks(value):
    return [value[r : r + 8] for r in range(0, value.shape[0], 8)]


def exact_dot(left, right):
    return jnp.dot(left, right, precision=PRECISE, preferred_element_type=jnp.float32)


def triangle(size, upper):
    row = lax.broadcasted_iota(jnp.int32, (size, size), 0)
    column = lax.broadcasted_iota(jnp.int32, (size, size), 1)
    keep = row <= column if upper else row >= column
    return jnp.where(keep, 1.0, 0.0)


def spans(running, docs, span_s):
    size = running.shape[0]
    run, doc = row_blocks(running), row_blocks(docs)
    place = lax.broadcasted_iota(jnp.int32, (8, running.shape[1]), 0)
    for j in range(size):
        for r in range(j // 8, size // 8):
            ok = doc[r] == docs[j : j + 1]
            if r == j // 8 and j % 8:
                ok = ok & (place >= j % 8)
            span_s[j, 8 * r : 8 * r + 8] = jnp.where(ok, jnp.exp(run[r] - running[j : j + 1]), 0.0)


def to_end(running, docs):
    last = running.shape[0] - 1
    return jnp.where(
        docs == docs[last : last + 1], jnp.exp(running[last : last + 1] - running), 0.0
    )


def turned(to_end_weights, kept):
    size, slots = to_end_weights.shape
    fill = jnp.broadcast_to(kept, (128 - size, slots))
    both = jnp.concatenate([to_end_weights, fill], axis=0).T
    return both[:, :size], both[:, size : size + 1]


def read_kernel(
    q_ref, k_ref, v_ref, log_ref, new_ref, doc_ref, prev_ref, kin_ref, vin_ref,
    read_ref, score_ref, prob_ref, ks_ref, vs_ref, span_s,
):
    size = span_s.shape[0]
    lower = triangle(size, False)
    scaling = q_ref.shape[1] ** (-0.5)
    ks_ref[0] = kin_ref[...]
    vs_ref[0] = vin_ref[...]
    lane = lax.broadcasted_iota(jnp.int32, (8, size), 1)

    def chunk(i, carry):
        rows = pl.ds(pl.multiple_of(i * size, size), size)
        queries, keys, values = q_ref[rows, :], k_ref[rows, :], v_ref[rows, :]
        new, docs = new_ref[rows, :], doc_ref[rows, :]
        running = exact_dot(lower, log_ref[rows, :])
        carried = jnp.where(docs == prev_ref[rows, :], jnp.exp(running), 0.0)
        key_state, value_state = ks_ref[i], vs_ref[i]
        spans(running, docs, span_s)
        affinity = row_blocks(nt(queries, keys))
        scores = row_blocks(carried * two(nt, queries, key_state))
        for j in range(size):
            for r in range(j // 8, size // 8):
                weight = span_s[j, 8 * r : 8 * r + 8] * new[j : j + 1]
                scores[r] = scores[r] + weight * affinity[r][:, j : j + 1]
        scores = scaling * jnp.concatenate(scores, axis=0)
        probs = jnp.exp(scores - jnp.max(scores, axis=1, keepdims=True))
        probs = probs / jnp.sum(probs, axis=1, keepdims=True)
        score_ref[rows, :] = scores
        prob_ref[rows, :] = probs
        used = probs.astype(jnp.bfloat16).astype(jnp.float32)
        part = row_blocks(used)
        mixing = [jnp.zeros((8, size), jnp.float32) for _ in part]
        for j in range(size):
            for r in range(j // 8, size // 8):
                weight = span_s[j, 8 * r : 8 * r + 8] * new[j : j + 1]
                total = jnp.sum(part[r] * weight, axis=1, keepdims=True)
                mixing[r] = jnp.where(lane == j, total, mixing[r])
        high, low = split(jnp.concatenate(mixing, axis=0))
        read_ref[rows, :] = (
            three(nn, used * carried, value_state) + nn(high, values) + nn(low, values)
        )
        end, kept = turned(to_end(running, docs) * new, carried[size - 1 : size])
        high, low = split(end)
        ks_ref[i + 1] = kept * key_state + (nn(high, keys) + nn(low, keys))
        vs_ref[i + 1] = kept * value_state + (nn(high, values) + nn(low, values))
        return carry

    lax.fori_loop(0, q_ref.shape[0] // size, chunk, 0)


def back_query_kernel(
    piece, pieces, q_ref, k_ref, v_ref, log_ref, new_ref, doc_ref, prev_ref, score_ref, prob_ref, ks_ref, vs_ref, g_ref,
    dq_ref, dk_ref, dv_ref, held_ref, gained_ref, xk_ref, xv_ref, dkin_ref, dvin_ref, span_s,
):
    size = span_s.shape[0]
    count = q_ref.shape[0] // size
    lower = triangle(size, False)
    scaling = q_ref.shape[1] ** (-0.5)
    dkin_ref[...] = jnp.zeros_like(dkin_ref)
    dvin_ref[...] = jnp.zeros_like(dvin_ref)
    lane = lax.broadcasted_iota(jnp.int32, (8, size), 1)

    def chunk(turn, carry):
        i = count - 1 - turn
        start = pl.multiple_of(i * size, size)
        rows = pl.ds(start, size)
        queries, keys, values, grads = q_ref[rows, :], k_ref[rows, :], v_ref[rows, :], g_ref[rows, :]
        new, docs = new_ref[rows, :], doc_ref[rows, :]
        running = exact_dot(lower, log_ref[rows, :])
        carried = jnp.where(docs == prev_ref[rows, :], jnp.exp(running), 0.0)
        spans(running, docs, span_s)
        affinity = row_blocks(nt(queries, keys))
        grad_high, grad_low = split(grads)
        pull = row_blocks(nt(grad_high, values) + nt(grad_low, values))
        back = row_blocks(carried * three(nt, grads, vs_ref[i]))
        for j in range(size):
            for r in range(j // 8, size // 8):
                weight = span_s[j, 8 * r : 8 * r + 8] * new[j : j + 1]
                back[r] = back[r] + weight * pull[r][:, j : j + 1]
        back = jnp.concatenate(back, axis=0)
        probs = prob_ref[rows, :]
        used = probs.astype(jnp.bfloat16).astype(jnp.float32)
        inner = probs * (back - jnp.sum(probs * back, axis=1, keepdims=True))
        gained_ref[rows, :] = inner * score_ref[rows, :] + used * back
        outer = scaling * inner
        part, used_part = row_blocks(outer), row_blocks(used)
        key_mix = [jnp.zeros((8, size), jnp.float32) for _ in part]
        value_mix = [jnp.zeros((8, size), jnp.float32) for _ in part]
        for j in range(size):
            held = None
            for r in range(j // 8, size // 8):
                span = span_s[j, 8 * r : 8 * r + 8]
                key_side, value_side = part[r] * span, used_part[r] * span
                own = key_side * affinity[r][:, j : j + 1] + value_side * pull[r][:, j : j + 1]
                held = own if held is None else held + own
                fresh = new[j : j + 1]
                key_mix[r] = jnp.where(
                    lane == j, jnp.sum(key_side * fresh, axis=1, keepdims=True), key_mix[r]
                )
                value_mix[r] = jnp.where(
                    lane == j, jnp.sum(value_side * fresh, axis=1, keepdims=True), value_mix[r]
                )
            held_ref[pl.ds(start + j, 1), :] = jnp.sum(held, axis=0, keepdims=True)
        key_mix = jnp.concatenate(key_mix, axis=0)
        value_mix = jnp.concatenate(value_mix, axis=0)
        outer_in, used_in = outer * carried, used * carried
        high, low = split(key_mix)
        dq_ref[rows, :] = three(nn, outer_in, ks_ref[i]) + (nn(high, keys) + nn(low, keys))
        fill = jnp.zeros((128 - size, size), jnp.float32)
        high, low = split(jnp.concatenate([key_mix, fill], axis=0).T[:, :size])
        dk_ref[rows, :] = nn(high, queries) + nn(low, queries)
        mixed = jnp.concatenate([value_mix, fill], axis=0).T[:, :size]
        dv_ref[rows, :] = three(nn, mixed, grads)
        outer_t, kept = turned(outer_in, carried[size - 1 : size])
        used_t, kept = turned(used_in, carried[size - 1 : size])
        high, low = split(outer_t)
        to_key = nn(high, queries) + nn(low, queries)
        to_value = three(nn, used_t, grads)
        xk_ref[i] = to_key
        xv_ref[i] = to_value
        dkin_ref[...] = kept * dkin_ref[...] + to_key
        dvin_ref[...] = kept * dvin_ref[...] + to_value
        return carry

    lax.fori_loop(0, count, chunk, 0)


def back_key_kernel(
    k_ref, v_ref, log_ref, new_ref, doc_ref, prev_ref, dk_in_ref, dv_in_ref, held_ref, gained_ref,
    xk_ref, xv_ref, dkend_ref, dvend_ref, total_ref,
    dk_ref, dv_ref, dlog_ref, ks, vs, total,
):
    size = CHUNK
    count = k_ref.shape[0] // size
    lower, upper = triangle(size, False), triangle(size, True)
    ks[...] = dkend_ref[...]
    vs[...] = dvend_ref[...]
    total[...] = total_ref[...]

    def chunk(turn, carry):
        i = count - 1 - turn
        rows = pl.ds(pl.multiple_of(i * size, size), size)
        keys, values = k_ref[rows, :], v_ref[rows, :]
        logs, new, docs = log_ref[rows, :], new_ref[rows, :], doc_ref[rows, :]
        running = exact_dot(lower, logs)
        carried = jnp.where(docs == prev_ref[rows, :], jnp.exp(running), 0.0)
        end = to_end(running, docs)
        weight = end * new
        dk_ref[rows, :] = (dk_in_ref[rows, :] + three(nn, weight, ks[...])).astype(dk_ref.dtype)
        dv_ref[rows, :] = (dv_in_ref[rows, :] + three(nn, weight, vs[...])).astype(dv_ref.dtype)
        held = held_ref[rows, :] + end * (two(nt, keys, ks[...]) + two(nt, values, vs[...]))
        change = gained_ref[rows, :] - new * held
        after = exact_dot(upper, change) + total[...]
        dlog_ref[rows, :] = after - jnp.exp(logs) * held
        total[...] = after[:1]
        unused, kept = turned(carried, carried[size - 1 : size])
        ks[...] = kept * ks[...] + xk_ref[i]
        vs[...] = kept * vs[...] + xv_ref[i]
        return carry

    lax.fori_loop(0, count, chunk, 0)


def cost(flops, moved):
    return pl.CostEstimate(flops=flops, bytes_accessed=moved, transcendentals=0)


def read_slots(queries, keys, values, logs, new, docs, prev, key_in, value_in):
    rows, width = queries.shape
    slots = logs.shape[1]
    count = rows // CHUNK
    f32 = jnp.float32
    return pl.pallas_call(
        read_kernel,
        out_shape=(
            jax.ShapeDtypeStruct((rows, width), f32),
            jax.ShapeDtypeStruct((rows, slots), f32),
            jax.ShapeDtypeStruct((rows, slots), f32),
            jax.ShapeDtypeStruct((count + 1, slots, width), f32),
            jax.ShapeDtypeStruct((count + 1, slots, width), f32),
        ),
        scratch_shapes=[pltpu.VMEM((CHUNK, CHUNK, slots), f32)],
        compiler_params=pltpu.CompilerParams(vmem_limit_bytes=VMEM),
        cost_estimate=cost(READ_COST, 5 << 20),
    )(queries, keys, values, logs, new, docs, prev, key_in, value_in)


def back_query(queries, keys, values, logs, new, docs, prev, scores, probs, key_states, value_states, grads):
    rows, width = queries.shape
    slots = logs.shape[1]
    count = rows // CHUNK
    f32 = jnp.float32
    narrow = jax.ShapeDtypeStruct((rows, slots), f32)
    wide = jax.ShapeDtypeStruct((rows, width), f32)
    states = jax.ShapeDtypeStruct((count, slots, width), f32)
    state = jax.ShapeDtypeStruct((slots, width), f32)
    return (
        back_query_kernel,
        (queries, keys, values, logs, new, docs, prev, scores, probs, key_states, value_states, grads),
        (wide, wide, wide, narrow, narrow, states, states, state, state),
        (pltpu.VMEM((CHUNK, CHUNK, slots), f32),),
        (False,) * 12,
    )


def back_key(keys, values, logs, new, docs, prev, dk, dv, held, gained, xk, xv, dk_end, dv_end, total):
    rows, width = keys.shape
    slots = logs.shape[1]
    f32 = jnp.float32
    wide = jax.ShapeDtypeStruct((rows, width), jnp.bfloat16)
    return pl.pallas_call(
        back_key_kernel,
        out_shape=(wide, wide, jax.ShapeDtypeStruct((rows, slots), f32)),
        scratch_shapes=[
            pltpu.VMEM((slots, width), f32),
            pltpu.VMEM((slots, width), f32),
            pltpu.VMEM((1, slots), f32),
        ],
        compiler_params=pltpu.CompilerParams(vmem_limit_bytes=VMEM),
        cost_estimate=cost(READ_COST, 8 << 20),
    )(keys, values, logs, new, docs, prev, dk, dv, held, gained, xk, xv, dk_end, dv_end, total)


def other_of(place, by):
    return place + by * (1 - 2 * ((place // by) % 2))


def exchange_kernel(names, count, heads, reverse, work, early, *refs):
    refs = dict(zip(names, refs))
    wides = [n for n in names if n.startswith("wide_in")]
    narrows = [n for n in names if n.startswith("narrow_in")]
    place, head = lax.axis_index("seq"), lax.axis_index("head")
    partner, sibling = {"seq": other_of(place, 1)}, {"head": other_of(head, 1)}
    line = -1 if reverse else 1
    ahead = count - 1 - place if reverse else place
    left = count - 1 - ahead
    spans_of = [1 << k for k in range(count.bit_length() - 1)]
    hops = [1 << k for k in range(1, heads.bit_length() - 1)]

    greeted = []
    if wides or narrows or early is not None:
        greeted.append((partner, None))
    if wides or "part" in refs:
        greeted.append((sibling, None))
    if "part" in refs:
        greeted += [({"head": other_of(head, by)}, None) for by in hops]
    if "state" in refs:
        greeted += [({"seq": place + line * by}, left >= by) for by in spans_of]
        greeted += [({"seq": place - line * by}, ahead >= by) for by in spans_of]
    barrier = pltpu.get_barrier_semaphore()
    total = 0
    for device, ok in greeted:
        if ok is None:
            pl.semaphore_signal(barrier, inc=1, device_id=device, device_id_type=MESH)
            total = total + 1
        else:

            @pl.when(ok)
            def _(device=device):
                pl.semaphore_signal(barrier, inc=1, device_id=device, device_id_type=MESH)

            total = total + ok.astype(jnp.int32)
    pl.semaphore_wait(barrier, total)

    def copy(source, target, sems, device):
        return pltpu.make_async_remote_copy(
            src_ref=source, dst_ref=target, send_sem=sems[0], recv_sem=sems[1],
            device_id=device, device_id_type=MESH,
        )

    def sems(name, i):
        return refs[name + "_send"].at[i], refs[name + "_recv"].at[i]

    def half_of(ref):
        size = ref.shape[0] // 2
        return ref.at[pl.ds((head % 2) * size, size)]

    def blocks_of(source, target, i):
        lines, rows, wide = target.shape
        if len(source.shape) == 3:
            return [copy(half_of(source), half_of(target), sems("wide", i * lines), partner)]
        copies = []
        for k in range(lines // 2):
            line = (head % 2) * (lines // 2) + k
            start = pl.multiple_of((2 * line + 1 - place % 2) * wide, 128)
            copies.append(
                copy(
                    source.at[:, pl.ds(start, wide)], target.at[line],
                    sems("wide", i * lines + k), partner,
                )
            )
        return copies

    waits, forwards, states = [], [], []
    fill = None
    if early is not None:
        source, target = refs["early_scratch0"], refs["narrow_out0"]

        def send_tile(i, columns):
            moved = copy(source.at[:, columns], target.at[:, columns], sems("narrow", i), partner)
            moved.start()
            waits.append(moved)

        fill = early(send_tile, refs, [refs[n] for n in names if n.startswith("early")])
    tiles_sent, waits = waits, []
    if "state" in refs:
        inside, received, before = refs["inside"], refs["received"], refs["before"]
        inside[0] = refs["state"][...]
        states = [
            copy(inside.at[k], received.at[k], sems("state", k), {"seq": place + line * by})
            for k, by in enumerate(spans_of)
        ]

        @pl.when(left >= 1)
        def _():
            states[0].start()

    if "part" in refs:
        part, added = refs["part"], refs["sum"]
        rows = part.shape[0] // CHUNKS
        half = rows // 2
        low = head % 2
        own, arrived = refs["own"], refs["arrived"]
        across = []

        def cross(c):
            waits[c].wait_recv()
            start = pl.multiple_of(c * rows + low * half, 8)
            own[0, c] = part[pl.ds(start, half), :] + refs["near"][c]
            moved = copy(
                own.at[0, c], arrived.at[0, c], sems("across", c), {"head": other_of(head, 2)}
            )
            moved.start()
            across.append(moved)

        for c in range(CHUNKS):
            if fill is not None:
                fill(c, rows)
            start = pl.multiple_of(c * rows + (1 - low) * half, 8)
            moved = copy(part.at[pl.ds(start, half)], refs["near"].at[c], sems("near", c), sibling)
            moved.start()
            waits.append(moved)
            if fill is not None:
                cross(c)
    for i, name in enumerate(wides):
        name, source = name.replace("in", "out"), refs[name]
        moved = blocks_of(source, refs[name], i)
        for one in moved:
            one.start()
        forwards.append((name, moved))
    for i, name in enumerate(narrows):
        moved = copy(refs[name], refs[name.replace("in", "out")], sems("narrow", i), partner)
        moved.start()
        waits.append(moved)

    def run_work(piece, pieces):
        if early is not None:
            outer_product_beside(piece, pieces, refs)
        if work is not None:
            work(piece, pieces, *[refs[n] for n in names if n.startswith("work")])

    if "part" in refs and fill is None:
        for c in range(CHUNKS):
            cross(c)
    if "state" not in refs:
        run_work(0, 1)
    if "state" in refs:
        lane = lax.broadcasted_iota(jnp.int32, before.shape, 1)
        before[...] = jnp.where(lane < 64, 1.0, jnp.where(lane < 128, -1.0, 0.0))

        def composed(earlier, later):
            keep = later[:, :1]
            if not reverse:
                keep = jnp.where(earlier[:, 64:65] == later[:, 64:65], keep, 0.0)
            values = keep * earlier + later
            return jnp.where(lane >= 128, values, jnp.where(lane < 64, earlier * later, later))

        for k, by in enumerate(spans_of):
            moved = states[k]
            if k:

                @pl.when(left >= by)
                def _(moved=moved):
                    moved.start()

            if k + 1 < len(spans_of):
                inside[k + 1] = inside[k]

            run_work(k, len(spans_of))

            @pl.when(ahead >= by)
            def _(k=k, moved=moved):
                moved.wait_recv()
                before[...] = composed(received[k], before[...]) if k else received[k]
                if k + 1 < len(spans_of):
                    inside[k + 1] = composed(received[k], inside[k])

            @pl.when(left >= by)
            def _(moved=moved):
                moved.wait_send()

    if "part" in refs:
        for k in range(1, len(hops)):
            later = []
            for c in range(CHUNKS):
                across[c].wait()
                own[k, c] = own[k - 1, c] + arrived[k - 1, c]
                moved = copy(
                    own.at[k, c], arrived.at[k, c], sems("across", k * CHUNKS + c),
                    {"head": other_of(head, hops[k])},
                )
                moved.start()
                later.append(moved)
            across = later
        back = []
        k = len(hops) - 1
        for c in range(CHUNKS):
            across[c].wait()
            start = pl.multiple_of(c * rows + low * half, 8)
            mine = pl.ds(start, half)
            added[mine, :] = own[k, c] + arrived[k, c]
            moved = copy(added.at[mine], added.at[mine], sems("back", c), sibling)
            moved.start()
            back.append(moved)
        for c in range(CHUNKS):
            waits[c].wait_send()
            back[c].wait()
        waits = waits[CHUNKS:]
    for i, (name, moved) in enumerate(forwards):
        for one in moved:
            one.wait()
        onward = copy(half_of(refs[name]), half_of(refs[name]), sems("onward", i), sibling)
        onward.start()
        waits.append(onward)
    for moved in waits + tiles_sent:
        moved.wait()
    if early is not None:
        for one in refs["finish"][-1]:
            one.wait()


def exchange(
    number, part=None, state=None, reverse=False, wides=(), narrows=(), work=None, early=None
):
    count, heads = lax.axis_size("seq"), lax.axis_size("head")
    f32 = jnp.float32
    vmem, hbm = pl.BlockSpec(memory_space=pltpu.VMEM), pl.BlockSpec(memory_space=pl.ANY)
    ins, outs, scratch = [], [], []
    if part is not None:
        if early is None:
            ins.append(("part", part, vmem))
        else:
            scratch.append(("part", pltpu.VMEM(part.shape, f32)))
        outs.append(("sum", part, vmem))
        half = (CHUNKS, part.shape[0] // CHUNKS // 2, part.shape[1])
        steps = heads.bit_length() - 2
        scratch += [
            ("near", pltpu.VMEM(half, f32)),
            ("own", pltpu.VMEM((steps,) + half, f32)),
            ("arrived", pltpu.VMEM((steps,) + half, f32)),
        ]
        for name, size in (("near", CHUNKS), ("across", steps * CHUNKS), ("back", CHUNKS)):
            scratch += [(name + end, pltpu.SemaphoreType.DMA((size,))) for end in ("_send", "_recv")]
    if state is not None:
        ins.append(("state", state, vmem))
        outs.append(("before", state, vmem))
        steps = count.bit_length() - 1
        scratch += [(n, pltpu.VMEM((steps,) + state.shape, f32)) for n in ("inside", "received")]
        scratch += [("state" + end, pltpu.SemaphoreType.DMA((steps,))) for end in ("_send", "_recv")]
    lines = count // 2
    for kind, arrays, each in (("wide", wides, lines), ("narrow", narrows, 1)):
        for i, a in enumerate(arrays):
            shape = a.shape
            if kind == "wide" and len(shape) == 2:
                shape = (lines, shape[0], shape[1] // count)
            ins.append((f"{kind}_in{i}", a, hbm))
            outs.append((f"{kind}_out{i}", jax.ShapeDtypeStruct(shape, f32), hbm))
        for name, size in ((kind, each), ("onward", 1)) if kind == "wide" else ((kind, 1),):
            if arrays:
                scratch += [
                    (name + end, pltpu.SemaphoreType.DMA((len(arrays) * size,)))
                    for end in ("_send", "_recv")
                ]
    if early is not None:
        early, given, sent_shape, tiles, made, extra = early
        ins += [(f"early_in{i}", a, hbm) for i, a in enumerate(given)]
        outs.append(("narrow_out0", jax.ShapeDtypeStruct(sent_shape, f32), hbm))
        outs += [(f"early_out{i}", a, hbm) for i, a in enumerate(made)]
        scratch += [(f"early_scratch{i}", a) for i, a in enumerate(extra)]
        scratch += [("narrow" + end, pltpu.SemaphoreType.DMA((tiles,))) for end in ("_send", "_recv")]
    if work is not None:
        work, given, made, extra, places = work
        ins += [(f"work_in{i}", a, hbm if p else vmem) for i, (a, p) in enumerate(zip(given, places))]
        outs += [(f"work_out{i}", a, vmem) for i, a in enumerate(made)]
        scratch += [(f"work_scratch{i}", a) for i, a in enumerate(extra)]
    names = [n for n, *_ in ins] + [n for n, *_ in outs] + [n for n, _ in scratch]
    return pl.pallas_call(
        functools.partial(exchange_kernel, names, count, heads, reverse, work, early),
        out_shape=tuple(jax.ShapeDtypeStruct(a.shape, a.dtype) for _, a, _ in outs),
        in_specs=[spec for *_, spec in ins],
        out_specs=tuple(spec for *_, spec in outs),
        scratch_shapes=[s for _, s in scratch],
        compiler_params=pltpu.CompilerParams(
            collective_id=number, has_side_effects=True, vmem_limit_bytes=VMEM
        ),
        cost_estimate=cost(40 << 30, 16 << 20),
    )(*[a for _, a, _ in ins])


def scatter_kernel(count, in_ref, out_ref, slots, send, receive):
    place = lax.axis_index("seq")
    others = [{"seq": lax.rem(place + k, count)} for k in range(1, count)]
    barrier = pltpu.get_barrier_semaphore()
    for device in others:
        pl.semaphore_signal(barrier, inc=1, device_id=device, device_id_type=MESH)
    pl.semaphore_wait(barrier, count - 1)
    copies = []
    for k, device in enumerate(others):
        moved = pltpu.make_async_remote_copy(
            src_ref=in_ref.at[device["seq"]], dst_ref=slots.at[place],
            send_sem=send.at[k], recv_sem=receive.at[k], device_id=device, device_id_type=MESH,
        )
        moved.start()
        copies.append(moved)
    slots[place] = in_ref[place]
    for moved in copies:
        moved.wait()
    total = slots[0]
    for i in range(1, count):
        total = total + slots[i]
    out_ref[...] = total


def scatter_sum(number, array):
    count = array.shape[0]
    vmem = pl.BlockSpec(memory_space=pltpu.VMEM)
    return pl.pallas_call(
        functools.partial(scatter_kernel, count),
        out_shape=jax.ShapeDtypeStruct(array.shape[1:], jnp.float32),
        in_specs=[vmem],
        out_specs=vmem,
        scratch_shapes=[
            pltpu.VMEM(array.shape, jnp.float32),
            pltpu.SemaphoreType.DMA((count - 1,)),
            pltpu.SemaphoreType.DMA((count - 1,)),
        ],
        compiler_params=pltpu.CompilerParams(
            collective_id=number, has_side_effects=True, vmem_limit_bytes=VMEM
        ),
        cost_estimate=cost(4 << 30, 1 << 20),
    )(array)


def state_of(keep, doc, keys, values):
    keep = jnp.broadcast_to(keep[:, None], (keep.shape[0], 64))
    return jnp.concatenate([keep, jnp.full_like(keep, doc), keys, values], axis=1)


def matmul_work(product, column, piece, pieces, left_ref, right_ref, out_ref, left, right, sems):
    copies = [
        pltpu.make_async_copy(left_ref, left, sems.at[0]),
        pltpu.make_async_copy(right_ref, right, sems.at[1]),
    ]
    if piece == 0:
        for one in copies:
            one.start()
        for one in copies:
            one.wait()

    def tile(i, carry):
        columns = pl.ds(pl.multiple_of(i * column, column), column)
        side = right[columns, :] if product is nt else right[:, columns]
        out_ref[:, columns] = product(left[...], side)
        return carry

    tiles = out_ref.shape[1] // column
    lax.fori_loop(tiles * piece // pieces, tiles * (piece + 1) // pieces, tile, 0)


def column_tiles(size):
    wide = 256 if size >= 256 else size
    return [(at, min(wide, size - at)) for at in range(0, size, wide)]


def hidden_units(send_tile, refs, own):
    (normed_in, gate_in, up_in, down_in, d_act_in, act_out, d_gate_out, d_up_out, gate_f_out, up_f_out, ffn_out,
     act_f, act_ref, d_gate_ref, d_up_ref, gate_f_ref, up_f_ref, ffn_ref, normed, w_gate, w_up, w_down, d_act, sems, tile_sems, out_sems) = own
    whole = [
        pltpu.make_async_copy(normed_in, normed, sems.at[0]),
        pltpu.make_async_copy(d_act_in, d_act, sems.at[1]),
        pltpu.make_async_copy(down_in, w_down, sems.at[2]),
    ]
    parts = []
    tiles = column_tiles(act_ref.shape[1])
    for i, (at, size) in enumerate(tiles):
        columns = pl.ds(at, size)
        parts.append(
            [
                pltpu.make_async_copy(gate_in.at[:, columns], w_gate.at[:, columns], tile_sems.at[0, i]),
                pltpu.make_async_copy(up_in.at[:, columns], w_up.at[:, columns], tile_sems.at[1, i]),
            ]
        )
    whole[0].start()
    for one in parts[0]:
        one.start()
    whole[1].start()
    for pair in parts[1:]:
        for one in pair:
            one.start()
    whole[2].start()
    whole[0].wait()
    for i, (at, size) in enumerate(tiles):
        columns = pl.ds(at, size)
        for one in parts[i]:
            one.wait()
        gate = nn(normed[...], w_gate[:, columns])
        up = nn(normed[...], w_up[:, columns])
        if i == 0:
            whole[1].wait()
        sig = jax.nn.sigmoid(gate)
        silu = gate * sig
        pull = d_act[:, columns]
        act = (silu * up).astype(jnp.bfloat16)
        act_ref[:, columns] = act
        act_f[:, columns] = act.astype(jnp.float32)
        send_tile(i, columns)
        d_gate = (pull * up * sig * (1.0 + gate * (1.0 - sig))).astype(jnp.bfloat16)
        d_up = (pull * silu).astype(jnp.bfloat16)
        d_gate_ref[:, columns] = d_gate
        d_up_ref[:, columns] = d_up
        gate_f_ref[:, columns] = d_gate.astype(jnp.float32)
        up_f_ref[:, columns] = d_up.astype(jnp.float32)

    kept = [(act_ref, act_out), (d_gate_ref, d_gate_out), (d_up_ref, d_up_out),
            (gate_f_ref, gate_f_out), (up_f_ref, up_f_out), (ffn_ref, ffn_out)]
    kept = [pltpu.make_async_copy(a, b, out_sems.at[i]) for i, (a, b) in enumerate(kept)]
    for one in kept[:-1]:
        one.start()
    part = refs["part"]

    def fill(c, rows):
        mine = pl.ds(c * rows, rows)

        def tile(i, carry):
            columns = pl.ds(pl.multiple_of(i * 256, 256), 256)
            part[mine, columns] = nt(d_gate_ref[mine, :], w_gate[columns, :]) + nt(
                d_up_ref[mine, :], w_up[columns, :]
            )
            return carry

        lax.fori_loop(0, part.shape[1] // 256, tile, 0)

    refs["finish"] = (whole[2], act_ref, w_down, ffn_ref, kept)
    return fill


def outer_product_beside(piece, pieces, refs):
    copied, act, w_down, out, kept = refs["finish"]
    copied.wait()

    def tile(i, carry):
        columns = pl.ds(pl.multiple_of(i * 256, 256), 256)
        out[:, columns] = nn(act[...], w_down[:, columns])
        return carry

    lax.fori_loop(0, out.shape[1] // 256, tile, 0)
    kept[-1].start()


def hidden_units_early(normed_mid, w_gate, w_up, w_down, d_act):
    rows, width = normed_mid.shape
    hidden = w_gate.shape[1]
    tiles = len(column_tiles(hidden))
    half = jax.ShapeDtypeStruct((rows, hidden), jnp.bfloat16)
    full = jax.ShapeDtypeStruct((rows, hidden), jnp.float32)
    return (
        hidden_units,
        (normed_mid, w_gate, w_up, w_down, d_act),
        (rows, hidden),
        tiles,
        (half, half, half, full, full, jax.ShapeDtypeStruct((rows, width), jnp.float32)),
        (
            pltpu.VMEM((rows, hidden), jnp.float32),
            pltpu.VMEM((rows, hidden), jnp.bfloat16),
            pltpu.VMEM((rows, hidden), jnp.bfloat16),
            pltpu.VMEM((rows, hidden), jnp.bfloat16),
            pltpu.VMEM((rows, hidden), jnp.float32),
            pltpu.VMEM((rows, hidden), jnp.float32),
            pltpu.VMEM((rows, width), jnp.float32),
            pltpu.VMEM(normed_mid.shape, jnp.bfloat16),
            pltpu.VMEM(w_gate.shape, jnp.bfloat16),
            pltpu.VMEM(w_up.shape, jnp.bfloat16),
            pltpu.VMEM(w_down.shape, jnp.bfloat16),
            pltpu.VMEM(d_act.shape, jnp.float32),
            pltpu.SemaphoreType.DMA((3,)),
            pltpu.SemaphoreType.DMA((2, tiles)),
            pltpu.SemaphoreType.DMA((6,)),
        ),
    )


def matmul_beside(product, left, right):
    columns = right.shape[0] if product is nt else right.shape[1]
    column = 256 if columns % 256 == 0 else 128
    return (
        functools.partial(matmul_work, product, column),
        (left, right),
        (jax.ShapeDtypeStruct((left.shape[0], columns), jnp.float32),),
        (
            pltpu.VMEM(left.shape, left.dtype),
            pltpu.VMEM(right.shape, right.dtype),
            pltpu.SemaphoreType.DMA((2,)),
        ),
        (True, True),
    )


def body(
    stream,
    seg_ids,
    attn_gain,
    w_query,
    w_key,
    w_value,
    w_outgate,
    w_low,
    w_slot,
    forget_bias,
    head_gain,
    w_out,
    mlp_gain,
    w_gate,
    w_up,
    w_down,
    cotangent,
):
    tok_rows = stream.shape[0]
    width = stream.shape[1]
    slots = w_slot.shape[2]
    head_width = w_query.shape[1]
    stream_f = stream.astype(jnp.float32)
    scale_in = rms_scale(stream_f)
    normed_in = (stream_f * scale_in * attn_gain).astype(jnp.bfloat16)
    query_rows = plain_dot(normed_in, w_query).astype(jnp.bfloat16)
    key_rows = plain_dot(normed_in, w_key).astype(jnp.bfloat16)
    value_rows = plain_dot(normed_in, w_value).astype(jnp.bfloat16)
    gate_act = plain_dot(normed_in, w_outgate)
    ranked = plain_dot(normed_in, w_low)

    def decay_logs(ranked_in, slot_map, bias_row):
        return jax.nn.log_sigmoid(precise_dot(ranked_in, slot_map[0]) + bias_row[0]) / GATE_NORM

    log_decay, gate_pull = jax.vjp(decay_logs, ranked, w_slot, forget_bias)

    new = -jnp.expm1(log_decay)
    last_doc = seg_ids[tok_rows - 1]
    running = precise_dot(jnp.tril(jnp.ones((tok_rows, tok_rows), jnp.float32)), log_decay)
    total = running[tok_rows - 1]
    in_last = (seg_ids == last_doc)[:, None]
    factor = jnp.where(in_last, jnp.exp(jnp.where(in_last, total - running, 0.0)) * new, 0.0)
    def wide_float(array):
        return array.astype(jnp.float32)

    local_key = precise_left_t(factor, key_rows.astype(jnp.float32))
    local_value = precise_left_t(factor, value_rows.astype(jnp.float32))
    docs = seg_ids.astype(jnp.float32)
    own_state = state_of(jnp.exp(total), docs[tok_rows - 1], local_key, local_value)
    prefix, d_act = exchange(0, state=own_state, work=matmul_beside(nt, cotangent, w_down))
    key_in, value_in = prefix[:, 128 : 128 + head_width], prefix[:, 128 + head_width :]
    prior = prefix[0, 64]
    decay_all = jnp.where(docs[tok_rows - 1] == prior, jnp.exp(total), 0.0)
    before = jnp.concatenate([prior[None], docs[CHUNK - 1 : -1 : CHUNK]])
    docs = jnp.broadcast_to(docs[:, None], (tok_rows, slots))
    before = jnp.broadcast_to(jnp.repeat(before, CHUNK)[:, None], (tok_rows, slots))
    slot_read, scores, probs, key_states, value_states = read_slots(
        query_rows, key_rows, value_rows, log_decay, new, docs, before, key_in, value_in
    )
    scale_read = rms_scale(slot_read)
    normed_read = slot_read * scale_read * head_gain[0]
    gate_sig = jax.nn.sigmoid(gate_act)
    gate_silu = gate_act * gate_sig
    mixed_heads = (normed_read * gate_silu).astype(jnp.bfloat16)
    branch, from_dy, from_in = exchange(
        1,
        part=plain_dot(mixed_heads, w_out),
        wides=(wide_to_send(cotangent), wide_to_send(normed_in)),
    )
    wide_dy = cotangent, from_dy
    wide_in = normed_in, from_in
    hidden = stream_f + branch
    scale_mid = rms_scale(hidden)
    normed_mid = (hidden * scale_mid * mlp_gain).astype(jnp.bfloat16)
    upstream = cotangent.astype(jnp.float32)
    d_mid, from_act, ffn_act, d_gate, d_up, d_gate_f, d_up_f, ffn_part = exchange(
        2,
        part=jax.ShapeDtypeStruct((tok_rows, width), jnp.float32),
        early=hidden_units_early(normed_mid, w_gate, w_up, w_down, d_act),
    )
    grad_down = pair_products((wide_dy, [(ffn_act, from_act)]))
    d_mid, grad_down = together(d_mid, grad_down)
    grad_down = line_sum(grad_down)
    grad_mlp_gain = jnp.sum(d_mid * hidden * scale_mid, axis=0)
    scaled_mid = d_mid * mlp_gain
    d_hidden = (
        upstream
        + scale_mid * scaled_mid
        - hidden * scale_mid**3 * jnp.mean(scaled_mid * hidden, axis=1, keepdims=True)
    )
    d_branch = d_hidden.astype(jnp.bfloat16)
    d_mixed = dot_right_t(d_branch, w_out)
    d_gate_act = (d_mixed * normed_read * gate_sig * (1.0 + gate_act * (1.0 - gate_sig))).astype(
        jnp.bfloat16
    )
    d_normed = d_mixed * gate_silu
    grad_head_gain = jnp.sum(d_normed * slot_read * scale_read, axis=0)[None, :]
    scaled_read = d_normed * head_gain[0]
    d_read = scale_read * scaled_read - slot_read * scale_read**3 * jnp.mean(
        scaled_read * slot_read, axis=1, keepdims=True
    )
    from_mid, from_gate, *back = exchange(
        3,
        wides=(wide_to_send(normed_mid),),
        narrows=(d_gate_f,),
        work=back_query(
            query_rows, key_rows, value_rows, log_decay, new, docs, before, scores, probs, key_states, value_states, d_read
        ),
    )
    wide_mid = normed_mid, from_mid
    grad_gate = pair_products((wide_mid, [(d_gate, from_gate)]))
    d_query, d_key, d_value, held, gained, to_keys, to_values, key_back, value_back = back
    query_back = d_query.astype(jnp.bfloat16)
    key_back, grad_gate = together(key_back, grad_gate)
    grad_gate, grad_down = together(grad_gate, grad_down)
    grad_gate = line_sum(grad_gate)
    ffn_out, suffix, from_up, from_outgate = exchange(
        4,
        part=ffn_part,
        state=state_of(decay_all, 0.0, key_back, value_back),
        reverse=True,
        narrows=(d_up_f, wide_float(d_gate_act)),
    )
    grad_up = pair_products((wide_mid, [(d_up, from_up)]))
    key_end, value_end = suffix[:, 128 : 128 + head_width], suffix[:, 128 + head_width :]
    end_total = jnp.sum(key_states[-1] * key_end + value_states[-1] * value_end, axis=1)[None, :]
    d_key, grad_up = together(d_key, grad_up)
    key_back, value_back, d_logs = back_key(
        key_rows, value_rows, log_decay, new, docs, before, d_key, d_value, held, gained,
        to_keys, to_values, key_end, value_end, end_total,
    )
    d_ranked, grad_slot, grad_bias = gate_pull(d_logs)
    normed_f = normed_in.astype(jnp.float32)
    grad_low = precise_left_t(normed_f, d_ranked)
    d_in_part = (
        dot_right_t(query_back, w_query)
        + dot_right_t(key_back, w_key)
        + dot_right_t(value_back, w_value)
        + dot_right_t(d_gate_act, w_outgate)
        + precise_right_t(d_ranked, w_low.astype(jnp.float32))
    )
    grad_up, grad_gate, d_in_part = together(grad_up, grad_gate, d_in_part)
    grad_up = line_sum(grad_up)
    d_in, from_branch, *from_mixer = exchange(
        5,
        part=d_in_part,
        wides=(wide_to_send(d_branch),),
        narrows=[wide_float(a) for a in (query_back, key_back, value_back, mixed_heads)],
    )
    grad_rest = pair_products(
        (
            wide_in,
            [
                (d_gate_act, from_outgate),
                (query_back, from_mixer[0]),
                (key_back, from_mixer[1]),
                (value_back, from_mixer[2]),
            ],
        ),
        ((d_branch, from_branch), [(mixed_heads, from_mixer[3])]),
    )
    grad_rest, grad_up, d_in = together(grad_rest, grad_up, d_in)
    grad_rest = line_sum(grad_rest)
    grad_outgate, grad_query, grad_key, grad_value, grad_out = jnp.split(grad_rest, 5, axis=1)
    result = hidden + ffn_out
    squares = jnp.stack(
        [jnp.sum(stream_f * stream_f), jnp.sum(hidden * hidden), jnp.sum(result * result)]
    )
    grad_attn_gain = jnp.sum(d_in * stream_f * scale_in, axis=0)
    scaled_in = d_in * attn_gain
    grad_stream = (
        d_hidden
        + scale_in * scaled_in
        - stream_f * scale_in**3 * jnp.mean(scaled_in * stream_f, axis=1, keepdims=True)
    ).astype(jnp.bfloat16)
    count = lax.axis_size("seq")
    small = [
        grad_attn_gain.reshape(count, -1),
        grad_mlp_gain.reshape(count, -1),
        grad_low.reshape(count, -1),
        jnp.moveaxis(grad_slot[0].reshape(-1, count, slots // count), 1, 0).reshape(count, -1),
        grad_bias.reshape(count, -1),
        grad_head_gain.reshape(count, -1),
        jnp.broadcast_to(squares, (count, 3)),
    ]
    sizes = [a.shape[1] for a in small]
    packed = jnp.concatenate(small, axis=1)
    packed = jnp.pad(packed, ((0, 0), (0, -packed.shape[1] % 1024)))
    packed = scatter_sum(6, packed.reshape(count, -1, 128)).reshape(-1)
    ends = [sum(sizes[: i + 1]) for i in range(len(sizes))]
    small = [packed[end - size : end] for end, size in zip(ends, sizes)]
    stream_rms = jnp.sqrt(small[6] / (tok_rows * count * width))
    summed = (
        small[0],
        grad_query,
        grad_key,
        grad_value,
        grad_outgate,
        small[2].reshape(width // count, -1),
        small[3].reshape(1, -1, slots // count),
        small[4][None, :],
        small[5][None, :],
        grad_out.T,
        small[1],
        grad_gate,
        grad_up,
        grad_down.T,
    )
    mixer_parts = summed[:10]
    ffn_parts = summed[10:]
    return (
        result.astype(jnp.bfloat16),
        grad_stream,
        mixer_parts[0],
        mixer_parts[1],
        mixer_parts[2],
        mixer_parts[3],
        mixer_parts[4],
        mixer_parts[5],
        mixer_parts[6],
        mixer_parts[7],
        mixer_parts[8],
        mixer_parts[9],
        ffn_parts[0],
        ffn_parts[1],
        ffn_parts[2],
        ffn_parts[3],
        stream_rms,
    )


def solution(mesh):
    in_specs = (
        P("seq", None),
        P("seq"),
        P(),
        P(None, "head"),
        P(None, "head"),
        P(None, "head"),
        P(None, "head"),
        P(None, "head"),
        P("head", None, None),
        P("head", None),
        P("head", None),
        P("head", None),
        P(),
        P(None, "head"),
        P(None, "head"),
        P("head", None),
        P("seq", None),
    )
    out_specs = (
        P("seq", None),
        P("seq", None),
        P("seq"),
        P("seq", "head"),
        P("seq", "head"),
        P("seq", "head"),
        P("seq", "head"),
        P("seq", "head"),
        P("head", None, "seq"),
        P("head", "seq"),
        P("head", "seq"),
        P("head", "seq"),
        P("seq"),
        P("seq", "head"),
        P("seq", "head"),
        P("head", "seq"),
        P(),
    )
    return jax.shard_map(body, mesh=mesh, in_specs=in_specs, out_specs=out_specs, check_vma=False)
```

```python
import functools
import math

import jax
import jax.numpy as jnp
from jax import lax
from jax.experimental import pallas as pl
from jax.experimental.pallas import tpu as pltpu
from jax.sharding import PartitionSpec as P

CHUNK = 32
CHUNKS = 4
MESH = pl.DeviceIdType.MESH
VMEM = 24 << 20
MORE = 10 << 20
EXCHANGE_VMEM = 50 << 20
FINAL_VMEM = 60 << 20
READ_COST = 17 << 30


EPSILON = 1e-06
GATE_NORM = 8.0
PRECISE = lax.Precision.HIGHEST


def width_blocks(array, parity):
    count = lax.axis_size("seq")
    wide = array.shape[1] // count
    return jnp.stack(
        [
            lax.dynamic_slice_in_dim(array, (2 * line + parity) * wide, wide, 1)
            for line in range(count // 2)
        ]
    )


def whole_tiles(array):
    return array.shape[1] // lax.axis_size("seq") % 128 == 0


def wide_to_send(array):
    array = array.astype(jnp.float32)
    if whole_tiles(array):
        return array
    return width_blocks(array, 1 - lax.axis_index("seq") % 2)


def product_kernel(layout, *refs):
    out_ref, sides = refs[-2:]
    refs = list(refs[1:-2])
    first = pl.program_id(0) == 0
    at = 0
    for narrows in layout:
        own, theirs = refs.pop(0), refs.pop(0)
        block = jnp.concatenate(
            [own[...].reshape(own.shape[-2:]), theirs[0].astype(jnp.bfloat16)], axis=0
        )
        for _ in range(narrows):
            own_narrow, their_narrow = refs.pop(0), refs.pop(0)
            rows, size = own_narrow.shape

            @pl.when(first)
            def _(at=at, own_narrow=own_narrow, their_narrow=their_narrow, rows=rows, size=size):
                sides[:rows, at : at + size] = own_narrow[...]
                sides[rows:, at : at + size] = their_narrow[...].astype(jnp.bfloat16)

            out_ref[0, :, at : at + size] = tn(block, sides[:, at : at + size])
            at += size


def pair_products(*jobs):
    count = lax.axis_size("seq")
    lines = count // 2
    parity = lax.axis_index("seq") % 2
    ins, specs, total = [], [], 0
    for (own, theirs), narrows in jobs:
        rows, wide = own.shape[0], own.shape[1] // count
        if whole_tiles(own):
            ins.append(own)
            specs.append(pl.BlockSpec((rows, wide), lambda i, p: (0, 2 * i + p[0])))
        else:
            ins.append(width_blocks(own, parity))
            specs.append(pl.BlockSpec((1, rows, wide), lambda i, p: (i, 0, 0)))
        ins.append(theirs)
        specs.append(pl.BlockSpec((1, rows, wide), lambda i, p: (i, 0, 0)))
        for pair in narrows:
            for side in pair:
                ins.append(side)
                specs.append(pl.BlockSpec(side.shape, lambda i, p: (0, 0)))
            total += pair[0].shape[1]
    return pl.pallas_call(
        functools.partial(product_kernel, [len(narrows) for _, narrows in jobs]),
        out_shape=jax.ShapeDtypeStruct((lines, wide, total), jnp.float32),
        grid_spec=pltpu.PrefetchScalarGridSpec(
            num_scalar_prefetch=1,
            grid=(lines,),
            in_specs=specs,
            out_specs=pl.BlockSpec((1, wide, total), lambda i, p: (i, 0, 0)),
            scratch_shapes=[pltpu.VMEM((2 * rows, total), jnp.bfloat16)],
        ),
        compiler_params=pltpu.CompilerParams(vmem_limit_bytes=VMEM),
        cost_estimate=cost(4 * rows * wide * lines * total, 8 * wide * lines * total),
    )(parity.reshape(1).astype(jnp.int32), *ins)


def line_sum(product):
    lines = product.shape[0]
    groups = [[line * 2 + x for line in range(lines)] for x in range(2)]
    return lax.psum_scatter(
        product, "seq", scatter_dimension=0, axis_index_groups=groups, tiled=True
    )[0]


def together(*arrays):
    return lax.optimization_barrier(arrays)


def precise_dot(left, right):
    return jnp.dot(left, right, precision=PRECISE, preferred_element_type=jnp.float32)


def plain_dot(left, right):
    return jnp.dot(left, right, preferred_element_type=jnp.float32)


def dot_right_t(left, right):
    return lax.dot_general(
        left, right, (((1,), (1,)), ((), ())), preferred_element_type=jnp.float32
    )


def dot_left_t(left, right):
    return lax.dot_general(
        left, right, (((0,), (0,)), ((), ())), preferred_element_type=jnp.float32
    )


def precise_left_t(left, right):
    return lax.dot_general(
        left, right, (((0,), (0,)), ((), ())), precision=PRECISE, preferred_element_type=jnp.float32
    )


def precise_right_t(left, right):
    return lax.dot_general(
        left, right, (((1,), (1,)), ((), ())), precision=PRECISE, preferred_element_type=jnp.float32
    )


def rms_scale(value):
    return lax.rsqrt(jnp.mean(value * value, axis=-1, keepdims=True) + EPSILON)


def split(value):
    high = value.astype(jnp.bfloat16)
    return high, (value - high.astype(jnp.float32)).astype(jnp.bfloat16)


def nn(left, right):
    return jnp.dot(left, right, preferred_element_type=jnp.float32)


def nt(left, right):
    return lax.dot_general(
        left, right, (((1,), (1,)), ((), ())), preferred_element_type=jnp.float32
    )


def tn(left, right):
    return lax.dot_general(
        left, right, (((0,), (0,)), ((), ())), preferred_element_type=jnp.float32
    )


def two(product, left, right):
    high, low = split(right)
    return product(left, high) + product(left, low)


def three(product, left, right):
    left_high, left_low = split(left)
    right_high, right_low = split(right)
    return product(left_high, right_high) + (
        product(left_low, right_high) + product(left_high, right_low)
    )


def row_blocks(value):
    return [value[r : r + 8] for r in range(0, value.shape[0], 8)]


def exact_dot(left, right):
    return jnp.dot(left, right, precision=PRECISE, preferred_element_type=jnp.float32)


def triangle(size, upper):
    row = lax.broadcasted_iota(jnp.int32, (size, size), 0)
    column = lax.broadcasted_iota(jnp.int32, (size, size), 1)
    keep = row <= column if upper else row >= column
    return jnp.where(keep, 1.0, 0.0)


def spans(running, docs, span_s):
    size = running.shape[0]
    run, doc = row_blocks(running), row_blocks(docs)
    place = lax.broadcasted_iota(jnp.int32, (8, running.shape[1]), 0)
    for j in range(size):
        for r in range(j // 8, size // 8):
            ok = doc[r] == docs[j : j + 1]
            if r == j // 8 and j % 8:
                ok = ok & (place >= j % 8)
            span_s[j, 8 * r : 8 * r + 8] = jnp.where(ok, jnp.exp(run[r] - running[j : j + 1]), 0.0)


def to_end(running, docs):
    last = running.shape[0] - 1
    return jnp.where(
        docs == docs[last : last + 1], jnp.exp(running[last : last + 1] - running), 0.0
    )


def turned(to_end_weights, kept):
    size, slots = to_end_weights.shape
    fill = jnp.broadcast_to(kept, (128 - size, slots))
    both = jnp.concatenate([to_end_weights, fill], axis=0).T
    return both[:, :size], both[:, size : size + 1]


def read_kernel(
    q_ref, k_ref, v_ref, log_ref, new_ref, doc_ref, prev_ref, kin_ref, vin_ref,
    read_ref, score_ref, prob_ref, ks_ref, vs_ref, span_s,
):
    size = span_s.shape[0]
    lower = triangle(size, False)
    scaling = q_ref.shape[1] ** (-0.5)
    ks_ref[0] = kin_ref[...]
    vs_ref[0] = vin_ref[...]
    lane = lax.broadcasted_iota(jnp.int32, (8, size), 1)

    def chunk(i, carry):
        rows = pl.ds(pl.multiple_of(i * size, size), size)
        queries, keys, values = q_ref[rows, :], k_ref[rows, :], v_ref[rows, :]
        new, docs = new_ref[rows, :], doc_ref[rows, :]
        running = exact_dot(lower, log_ref[rows, :])
        carried = jnp.where(docs == prev_ref[rows, :], jnp.exp(running), 0.0)
        key_state, value_state = ks_ref[i], vs_ref[i]
        spans(running, docs, span_s)
        affinity = row_blocks(nt(queries, keys))
        scores = row_blocks(carried * two(nt, queries, key_state))
        for j in range(size):
            for r in range(j // 8, size // 8):
                weight = span_s[j, 8 * r : 8 * r + 8] * new[j : j + 1]
                scores[r] = scores[r] + weight * affinity[r][:, j : j + 1]
        scores = scaling * jnp.concatenate(scores, axis=0)
        probs = jnp.exp(scores - jnp.max(scores, axis=1, keepdims=True))
        probs = probs / jnp.sum(probs, axis=1, keepdims=True)
        score_ref[rows, :] = scores
        prob_ref[rows, :] = probs
        used = probs.astype(jnp.bfloat16).astype(jnp.float32)
        part = row_blocks(used)
        mixing = [jnp.zeros((8, size), jnp.float32) for _ in part]
        for j in range(size):
            for r in range(j // 8, size // 8):
                weight = span_s[j, 8 * r : 8 * r + 8] * new[j : j + 1]
                total = jnp.sum(part[r] * weight, axis=1, keepdims=True)
                mixing[r] = jnp.where(lane == j, total, mixing[r])
        high, low = split(jnp.concatenate(mixing, axis=0))
        read_ref[rows, :] = (
            three(nn, used * carried, value_state) + nn(high, values) + nn(low, values)
        )
        end, kept = turned(to_end(running, docs) * new, carried[size - 1 : size])
        high, low = split(end)
        ks_ref[i + 1] = kept * key_state + (nn(high, keys) + nn(low, keys))
        vs_ref[i + 1] = kept * value_state + (nn(high, values) + nn(low, values))
        return carry

    lax.fori_loop(0, q_ref.shape[0] // size, chunk, 0)


def back_query_kernel(
    piece, pieces, q_ref, k_ref, v_ref, log_ref, new_ref, doc_ref, prev_ref, score_ref, prob_ref, ks_ref, vs_ref, g_ref,
    dq_ref, dk_ref, dv_ref, held_ref, gained_ref, xk_ref, xv_ref, dkin_ref, dvin_ref, span_s,
):
    if piece is None:
        return
    size = span_s.shape[0]
    count = q_ref.shape[0] // size
    lower = triangle(size, False)
    scaling = q_ref.shape[1] ** (-0.5)
    dkin_ref[...] = jnp.zeros_like(dkin_ref)
    dvin_ref[...] = jnp.zeros_like(dvin_ref)
    lane = lax.broadcasted_iota(jnp.int32, (8, size), 1)

    def chunk(turn, carry):
        i = count - 1 - turn
        start = pl.multiple_of(i * size, size)
        rows = pl.ds(start, size)
        queries, keys, values, grads = q_ref[rows, :], k_ref[rows, :], v_ref[rows, :], g_ref[rows, :]
        new, docs = new_ref[rows, :], doc_ref[rows, :]
        running = exact_dot(lower, log_ref[rows, :])
        carried = jnp.where(docs == prev_ref[rows, :], jnp.exp(running), 0.0)
        spans(running, docs, span_s)
        affinity = row_blocks(nt(queries, keys))
        grad_high, grad_low = split(grads)
        pull = row_blocks(nt(grad_high, values) + nt(grad_low, values))
        back = row_blocks(carried * three(nt, grads, vs_ref[i]))
        for j in range(size):
            for r in range(j // 8, size // 8):
                weight = span_s[j, 8 * r : 8 * r + 8] * new[j : j + 1]
                back[r] = back[r] + weight * pull[r][:, j : j + 1]
        back = jnp.concatenate(back, axis=0)
        probs = prob_ref[rows, :]
        used = probs.astype(jnp.bfloat16).astype(jnp.float32)
        inner = probs * (back - jnp.sum(probs * back, axis=1, keepdims=True))
        gained_ref[rows, :] = inner * score_ref[rows, :] + used * back
        outer = scaling * inner
        part, used_part = row_blocks(outer), row_blocks(used)
        key_mix = [jnp.zeros((8, size), jnp.float32) for _ in part]
        value_mix = [jnp.zeros((8, size), jnp.float32) for _ in part]
        for j in range(size):
            held = None
            for r in range(j // 8, size // 8):
                span = span_s[j, 8 * r : 8 * r + 8]
                key_side, value_side = part[r] * span, used_part[r] * span
                own = key_side * affinity[r][:, j : j + 1] + value_side * pull[r][:, j : j + 1]
                held = own if held is None else held + own
                fresh = new[j : j + 1]
                key_mix[r] = jnp.where(
                    lane == j, jnp.sum(key_side * fresh, axis=1, keepdims=True), key_mix[r]
                )
                value_mix[r] = jnp.where(
                    lane == j, jnp.sum(value_side * fresh, axis=1, keepdims=True), value_mix[r]
                )
            held_ref[pl.ds(start + j, 1), :] = jnp.sum(held, axis=0, keepdims=True)
        key_mix = jnp.concatenate(key_mix, axis=0)
        value_mix = jnp.concatenate(value_mix, axis=0)
        outer_in, used_in = outer * carried, used * carried
        high, low = split(key_mix)
        dq_ref[rows, :] = three(nn, outer_in, ks_ref[i]) + (nn(high, keys) + nn(low, keys))
        fill = jnp.zeros((128 - size, size), jnp.float32)
        high, low = split(jnp.concatenate([key_mix, fill], axis=0).T[:, :size])
        dk_ref[rows, :] = nn(high, queries) + nn(low, queries)
        mixed = jnp.concatenate([value_mix, fill], axis=0).T[:, :size]
        dv_ref[rows, :] = three(nn, mixed, grads)
        outer_t, kept = turned(outer_in, carried[size - 1 : size])
        used_t, kept = turned(used_in, carried[size - 1 : size])
        high, low = split(outer_t)
        to_key = nn(high, queries) + nn(low, queries)
        to_value = three(nn, used_t, grads)
        xk_ref[i] = to_key
        xv_ref[i] = to_value
        dkin_ref[...] = kept * dkin_ref[...] + to_key
        dvin_ref[...] = kept * dvin_ref[...] + to_value
        return carry

    lax.fori_loop(0, count, chunk, 0)


def back_key_kernel(
    k_ref, v_ref, log_ref, new_ref, doc_ref, prev_ref, dk_in_ref, dv_in_ref, held_ref, gained_ref,
    xk_ref, xv_ref, dkend_ref, dvend_ref, total_ref,
    dk_ref, dv_ref, dlog_ref, ks, vs, total,
):
    size = CHUNK
    count = k_ref.shape[0] // size
    lower, upper = triangle(size, False), triangle(size, True)
    ks[...] = dkend_ref[...]
    vs[...] = dvend_ref[...]
    total[...] = total_ref[...]

    def chunk(turn, carry):
        i = count - 1 - turn
        rows = pl.ds(pl.multiple_of(i * size, size), size)
        keys, values = k_ref[rows, :], v_ref[rows, :]
        logs, new, docs = log_ref[rows, :], new_ref[rows, :], doc_ref[rows, :]
        running = exact_dot(lower, logs)
        carried = jnp.where(docs == prev_ref[rows, :], jnp.exp(running), 0.0)
        end = to_end(running, docs)
        weight = end * new
        dk_ref[rows, :] = (dk_in_ref[rows, :] + three(nn, weight, ks[...])).astype(dk_ref.dtype)
        dv_ref[rows, :] = (dv_in_ref[rows, :] + three(nn, weight, vs[...])).astype(dv_ref.dtype)
        held = held_ref[rows, :] + end * (two(nt, keys, ks[...]) + two(nt, values, vs[...]))
        change = gained_ref[rows, :] - new * held
        after = exact_dot(upper, change) + total[...]
        dlog_ref[rows, :] = after - jnp.exp(logs) * held
        total[...] = after[:1]
        unused, kept = turned(carried, carried[size - 1 : size])
        ks[...] = kept * ks[...] + xk_ref[i]
        vs[...] = kept * vs[...] + xv_ref[i]
        return carry

    lax.fori_loop(0, count, chunk, 0)


def room(arrays):
    total = 0
    for a in arrays:
        shape = a.shape[:-1] + (-(-a.shape[-1] // 128) * 128,)
        total += math.prod(shape) * jnp.dtype(a.dtype).itemsize
    return total + MORE


def cost(flops, moved):
    return pl.CostEstimate(flops=flops, bytes_accessed=moved, transcendentals=0)


def read_slots(queries, keys, values, logs, new, docs, prev, key_in, value_in):
    rows, width = queries.shape
    slots = logs.shape[1]
    count = rows // CHUNK
    f32 = jnp.float32
    return pl.pallas_call(
        read_kernel,
        out_shape=(
            jax.ShapeDtypeStruct((rows, width), f32),
            jax.ShapeDtypeStruct((rows, slots), f32),
            jax.ShapeDtypeStruct((rows, slots), f32),
            jax.ShapeDtypeStruct((count + 1, slots, width), f32),
            jax.ShapeDtypeStruct((count + 1, slots, width), f32),
        ),
        scratch_shapes=[pltpu.VMEM((CHUNK, CHUNK, slots), f32)],
        compiler_params=pltpu.CompilerParams(vmem_limit_bytes=VMEM),
        cost_estimate=cost(READ_COST, 5 << 20),
    )(queries, keys, values, logs, new, docs, prev, key_in, value_in)


def back_query(queries, keys, values, logs, new, docs, prev, scores, probs, key_states, value_states, grads):
    rows, width = queries.shape
    slots = logs.shape[1]
    count = rows // CHUNK
    f32 = jnp.float32
    narrow = jax.ShapeDtypeStruct((rows, slots), f32)
    wide = jax.ShapeDtypeStruct((rows, width), f32)
    states = jax.ShapeDtypeStruct((count, slots, width), f32)
    state = jax.ShapeDtypeStruct((slots, width), f32)
    return (
        back_query_kernel,
        (queries, keys, values, logs, new, docs, prev, scores, probs, key_states, value_states, grads),
        (wide, wide, wide, narrow, narrow, states, states, state, state),
        (pltpu.VMEM((CHUNK, CHUNK, slots), f32),),
        (False,) * 12,
    )


def back_key(keys, values, logs, new, docs, prev, dk, dv, held, gained, xk, xv, dk_end, dv_end, total):
    rows, width = keys.shape
    slots = logs.shape[1]
    f32 = jnp.float32
    wide = jax.ShapeDtypeStruct((rows, width), jnp.bfloat16)
    return pl.pallas_call(
        back_key_kernel,
        out_shape=(wide, wide, jax.ShapeDtypeStruct((rows, slots), f32)),
        scratch_shapes=[
            pltpu.VMEM((slots, width), f32),
            pltpu.VMEM((slots, width), f32),
            pltpu.VMEM((1, slots), f32),
        ],
        compiler_params=pltpu.CompilerParams(vmem_limit_bytes=VMEM),
        cost_estimate=cost(READ_COST, 8 << 20),
    )(keys, values, logs, new, docs, prev, dk, dv, held, gained, xk, xv, dk_end, dv_end, total)


def other_of(place, by):
    return place + by * (1 - 2 * ((place // by) % 2))


def exchange_kernel(names, count, heads, reverse, work, early, after, *refs):
    refs = dict(zip(names, refs))
    wides = [n for n in names if n.startswith("wide_in")]
    narrows = [n for n in names if n.startswith("narrow_in")]
    place, head = lax.axis_index("seq"), lax.axis_index("head")
    partner, sibling = {"seq": other_of(place, 1)}, {"head": other_of(head, 1)}
    line = -1 if reverse else 1
    ahead = count - 1 - place if reverse else place
    left = count - 1 - ahead
    spans_of = [1 << k for k in range(count.bit_length() - 1)]
    hops = [1 << k for k in range(1, heads.bit_length() - 1)]

    relays = [n for n in names if n.startswith("relay_out")]
    relayed = bool(relays) or "ends_out" in refs
    beside = {"seq": other_of(place, 2)}
    at_end = (place // 2 == 0) | (place // 2 == 3)
    in_middle = jnp.logical_not(at_end)
    greeted = []
    if relayed:
        greeted.append((beside, None))
    if wides or narrows or early is not None:
        greeted.append((partner, None))
    if wides or relays or "part" in refs:
        greeted.append((sibling, None))
    if "part" in refs:
        greeted += [({"head": other_of(head, by)}, None) for by in hops]
    if "state" in refs:
        greeted += [({"seq": place + line * by}, left >= by) for by in spans_of]
        greeted += [({"seq": place - line * by}, ahead >= by) for by in spans_of]
    if work is not None:
        work(None, None, *[refs[n] for n in names if n.startswith("work")])
    barrier = pltpu.get_barrier_semaphore()
    total = 0
    for device, ok in greeted:
        if ok is None:
            pl.semaphore_signal(barrier, inc=1, device_id=device, device_id_type=MESH)
            total = total + 1
        else:

            @pl.when(ok)
            def _(device=device):
                pl.semaphore_signal(barrier, inc=1, device_id=device, device_id_type=MESH)

            total = total + ok.astype(jnp.int32)
    pl.semaphore_wait(barrier, total)

    def copy(source, target, sems, device):
        return pltpu.make_async_remote_copy(
            src_ref=source, dst_ref=target, send_sem=sems[0], recv_sem=sems[1],
            device_id=device, device_id_type=MESH,
        )

    def sems(name, i):
        return refs[name + "_send"].at[i], refs[name + "_recv"].at[i]

    def half_of(ref):
        size = ref.shape[0] // 2
        return ref.at[pl.ds((head % 2) * size, size)]

    def blocks_of(source, target, i):
        lines, rows, wide = target.shape
        if len(source.shape) == 3:
            return [copy(half_of(source), half_of(target), sems("wide", i * lines), partner)]
        copies = []
        for k in range(lines // 2):
            line = (head % 2) * (lines // 2) + k
            start = pl.multiple_of((2 * line + 1 - place % 2) * wide, 128)
            copies.append(
                copy(
                    source.at[:, pl.ds(start, wide)], target.at[line],
                    sems("wide", i * lines + k), partner,
                )
            )
        return copies

    waits, forwards, states = [], [], []
    fill = None
    if "state" in refs:
        inside, received, before = refs["inside"], refs["received"], refs["before"]
        inside[0] = refs["state"][...]
        states = [
            copy(inside.at[k], received.at[k], sems("state", k), {"seq": place + line * by})
            for k, by in enumerate(spans_of)
        ]

        @pl.when(left >= 1)
        def _():
            states[0].start()

    for i, name in enumerate(wides):
        name, source = name.replace("in", "out"), refs[name]
        moved = blocks_of(source, refs[name], i)
        for one in moved:
            one.start()
        forwards.append((name, moved))
    end_tiles, end_blocks = [], []
    for i, name in enumerate(relays):
        source, target = refs[f"relay_in{i}"], refs[name]
        lines, _, wide = target.shape
        for k in range(lines // 2):
            at = (head % 2) * (lines // 2) + k
            if len(source.shape) == 2:
                start = pl.multiple_of((2 * at + place % 2) * wide, 128)
                block = source.at[:, pl.ds(start, wide)]
            else:
                block = source.at[at]
            end_blocks.append(
                copy(block, target.at[at], sems("relay", i * (lines // 2) + k), beside)
            )

    @pl.when(at_end)
    def _():
        for moved in end_blocks:
            moved.start()

    if early is not None:
        source, target = refs["early_b0"], refs["narrow_out0"]

        def send_tile(i, columns):
            moved = copy(source.at[:, columns], target.at[:, columns], sems("narrow", i), partner)
            moved.start()
            waits.append(moved)
            if relayed:
                onward = copy(
                    refs["early_b1"].at[:, columns], refs["ends_out"].at[:, columns],
                    sems("ends", i), beside,
                )

                @pl.when(at_end)
                def _():
                    onward.start()

                end_tiles.append(onward)

        fill = early(send_tile, refs, [refs[n] for n in names if n.startswith("early")])
    tiles_sent, waits = waits, []
    if "part" in refs:
        part, added = refs["part"], refs["sum"]
        rows = part.shape[0] // CHUNKS
        half = rows // 2
        low = head % 2
        own, arrived = refs["own"], refs["arrived"]
        across = []

        def cross(c):
            waits[c].wait_recv()
            start = pl.multiple_of(c * rows + low * half, 8)
            own[0, c] = part[pl.ds(start, half), :] + refs["near"][c]
            moved = copy(
                own.at[0, c], arrived.at[0, c], sems("across", c), {"head": other_of(head, 2)}
            )
            moved.start()
            across.append(moved)

        for c in range(CHUNKS):
            if fill is not None:
                fill(c, rows)
            start = pl.multiple_of(c * rows + (1 - low) * half, 8)
            moved = copy(part.at[pl.ds(start, half)], refs["near"].at[c], sems("near", c), sibling)
            moved.start()
            waits.append(moved)
            if fill is not None:
                cross(c)
    for i, name in enumerate(narrows):
        moved = copy(refs[name], refs[name.replace("in", "out")], sems("narrow", i), partner)
        moved.start()
        waits.append(moved)

    def run_work(piece, pieces):
        if early is not None:
            outer_product_beside(piece, pieces, refs)
        if work is not None:
            work(piece, pieces, *[refs[n] for n in names if n.startswith("work")])

    if "part" in refs and fill is None:
        for c in range(CHUNKS):
            cross(c)
    if "state" not in refs:
        run_work(0, 1)
    if "state" in refs:
        lane = lax.broadcasted_iota(jnp.int32, before.shape, 1)
        before[...] = jnp.where(lane < 64, 1.0, jnp.where(lane < 128, -1.0, 0.0))

        def composed(earlier, later):
            keep = later[:, :1]
            if not reverse:
                keep = jnp.where(earlier[:, 64:65] == later[:, 64:65], keep, 0.0)
            values = keep * earlier + later
            return jnp.where(lane >= 128, values, jnp.where(lane < 64, earlier * later, later))

        for k, by in enumerate(spans_of):
            moved = states[k]
            if k:

                @pl.when(left >= by)
                def _(moved=moved):
                    moved.start()

            if k + 1 < len(spans_of):
                inside[k + 1] = inside[k]

            run_work(k, len(spans_of))

            @pl.when(ahead >= by)
            def _(k=k, moved=moved):
                moved.wait_recv()
                before[...] = composed(received[k], before[...]) if k else received[k]
                if k + 1 < len(spans_of):
                    inside[k + 1] = composed(received[k], inside[k])

            @pl.when(left >= by)
            def _(moved=moved):
                moved.wait_send()

    def pass_on():
        for i, (name, moved) in enumerate(forwards):
            for one in moved:
                one.wait()
            onward = copy(half_of(refs[name]), half_of(refs[name]), sems("onward", i), sibling)
            onward.start()
            waits.append(onward)

    early_pass = "part" in refs and "state" not in refs
    if early_pass:
        pass_on()
    if "part" in refs:
        for k in range(1, len(hops)):
            later = []
            for c in range(CHUNKS):
                across[c].wait()
                own[k, c] = own[k - 1, c] + arrived[k - 1, c]
                moved = copy(
                    own.at[k, c], arrived.at[k, c], sems("across", k * CHUNKS + c),
                    {"head": other_of(head, hops[k])},
                )
                moved.start()
                later.append(moved)
            across = later
        back = []
        k = len(hops) - 1

        def close(c):
            waits[c].wait_send()
            back[c].wait()
            if after is not None:
                after(c, rows, added, [refs[n] for n in names if n.startswith("after")])

        for c in range(CHUNKS):
            across[c].wait()
            start = pl.multiple_of(c * rows + low * half, 8)
            mine = pl.ds(start, half)
            added[mine, :] = own[k, c] + arrived[k, c]
            moved = copy(added.at[mine], added.at[mine], sems("back", c), sibling)
            moved.start()
            back.append(moved)
            if c:
                close(c - 1)
        close(CHUNKS - 1)
        waits = waits[CHUNKS:]
    if after is not None:
        after(None, rows, added, [refs[n] for n in names if n.startswith("after")])
    if not early_pass:
        pass_on()
    for moved in waits + tiles_sent:
        moved.wait()
    if relayed:

        @pl.when(at_end)
        def _():
            for moved in end_tiles + end_blocks:
                moved.wait_send()

        @pl.when(in_middle)
        def _():
            for moved in end_tiles + end_blocks:
                moved.wait_recv()
            passed = [
                copy(half_of(refs[name]), half_of(refs[name]), sems("passed", i), sibling)
                for i, name in enumerate(relays)
            ]
            for moved in passed:
                moved.start()
            for moved in passed:
                moved.wait()

    if early is not None:
        for one in refs["finish"][-1]:
            one.wait()


def exchange(
    number, part=None, state=None, reverse=False, wides=(), narrows=(), work=None, early=None, relay=(), after=None
):
    count, heads = lax.axis_size("seq"), lax.axis_size("head")
    f32 = jnp.float32
    vmem, hbm = pl.BlockSpec(memory_space=pltpu.VMEM), pl.BlockSpec(memory_space=pl.ANY)
    ins, outs, scratch = [], [], []
    buffers = ["part", "near", "own", "arrived", "inside", "received"]
    if part is not None:
        if early is None:
            ins.append(("part", part, vmem))
        else:
            scratch.append(("part", pltpu.VMEM(part.shape, f32)))
        outs.append(("sum", part, vmem))
        half = (CHUNKS, part.shape[0] // CHUNKS // 2, part.shape[1])
        steps = heads.bit_length() - 2
        scratch += [
            ("near", pltpu.VMEM(half, f32)),
            ("own", pltpu.VMEM((steps,) + half, f32)),
            ("arrived", pltpu.VMEM((steps,) + half, f32)),
        ]
        for name, size in (("near", CHUNKS), ("across", steps * CHUNKS), ("back", CHUNKS)):
            scratch += [(name + end, pltpu.SemaphoreType.DMA((size,))) for end in ("_send", "_recv")]
    if state is not None:
        ins.append(("state", state, vmem))
        outs.append(("before", state, vmem))
        steps = count.bit_length() - 1
        scratch += [(n, pltpu.VMEM((steps,) + state.shape, f32)) for n in ("inside", "received")]
        scratch += [("state" + end, pltpu.SemaphoreType.DMA((steps,))) for end in ("_send", "_recv")]
    lines = count // 2
    for kind, arrays, each in (("wide", wides, lines), ("narrow", narrows, 1)):
        for i, a in enumerate(arrays):
            shape = a.shape
            if kind == "wide" and len(shape) == 2:
                shape = (lines, shape[0], shape[1] // count)
            ins.append((f"{kind}_in{i}", a, hbm))
            outs.append((f"{kind}_out{i}", jax.ShapeDtypeStruct(shape, f32), hbm))
        for name, size in ((kind, each), ("onward", 1)) if kind == "wide" else ((kind, 1),):
            if arrays:
                scratch += [
                    (name + end, pltpu.SemaphoreType.DMA((len(arrays) * size,)))
                    for end in ("_send", "_recv")
                ]
    for i, a in enumerate(relay):
        ins.append((f"relay_in{i}", a, hbm))
        shape = a.shape if len(a.shape) == 3 else (lines, a.shape[0], a.shape[1] // count)
        outs.append((f"relay_out{i}", jax.ShapeDtypeStruct(shape, f32), hbm))
    if relay:
        for name, size in (("relay", len(relay) * shape[0] // 2), ("passed", len(relay))):
            scratch += [(name + end, pltpu.SemaphoreType.DMA((size,))) for end in ("_send", "_recv")]
    if early is not None:
        early, given, sent_shape, tiles, made, extra = early
        ins += [(f"early_in{i}", a, hbm) for i, a in enumerate(given)]
        outs.append(("narrow_out0", jax.ShapeDtypeStruct(sent_shape, f32), hbm))
        if lines == 4:
            outs.append(("ends_out", jax.ShapeDtypeStruct(sent_shape, f32), hbm))
            scratch += [("ends" + end, pltpu.SemaphoreType.DMA((tiles,))) for end in ("_send", "_recv")]
        outs += [(f"early_out{i}", a, hbm) for i, a in enumerate(made)]
        scratch += [(f"early_b{i}", a) for i, a in enumerate(extra)]
        buffers += [f"early_b{i}" for i in range(len(extra) - 3)]
        scratch += [("narrow" + end, pltpu.SemaphoreType.DMA((tiles,))) for end in ("_send", "_recv")]
    if after is not None:
        after, given, made, extra = after
        ins += [(f"after_in{i}", a, vmem) for i, a in enumerate(given)]
        outs += [(f"after_out{i}", a, hbm) for i, a in enumerate(made)]
        scratch += [(f"after_b{i}", a) for i, a in enumerate(extra)]
        buffers += [f"after_b{i}" for i in range(len(extra) - 1)]
    if work is not None:
        work, given, made, extra, places = work
        beside = work is not back_query_kernel
        ins += [(f"work_in{i}", a, hbm if p else vmem) for i, (a, p) in enumerate(zip(given, places))]
        outs += [(f"work_out{i}", a, vmem) for i, a in enumerate(made)]
        scratch += [(f"work_b{i}", a) for i, a in enumerate(extra)]
        buffers += [f"work_b{i}" for i in range(len(extra) - beside)]
    names = [n for n, *_ in ins] + [n for n, *_ in outs] + [n for n, _ in scratch]
    held = [a for _, a, spec in ins + outs if spec is vmem]
    held += [jax.ShapeDtypeStruct(a.shape, a.dtype) for n, a in scratch if n in buffers]
    return pl.pallas_call(
        functools.partial(exchange_kernel, names, count, heads, reverse, work, early, after),
        out_shape=tuple(jax.ShapeDtypeStruct(a.shape, a.dtype) for _, a, _ in outs),
        in_specs=[spec for *_, spec in ins],
        out_specs=tuple(spec for *_, spec in outs),
        scratch_shapes=[s for _, s in scratch],
        compiler_params=pltpu.CompilerParams(
            collective_id=number, has_side_effects=True, vmem_limit_bytes=EXCHANGE_VMEM
        ),
        cost_estimate=cost(40 << 30, 16 << 20),
    )(*[a for _, a, _ in ins])


def scatter_kernel(count, in_ref, out_ref, slots, send, receive):
    place = lax.axis_index("seq")
    others = [{"seq": lax.rem(place + k, count)} for k in range(1, count)]
    barrier = pltpu.get_barrier_semaphore()
    for device in others:
        pl.semaphore_signal(barrier, inc=1, device_id=device, device_id_type=MESH)
    pl.semaphore_wait(barrier, count - 1)
    copies = []
    for k, device in enumerate(others):
        moved = pltpu.make_async_remote_copy(
            src_ref=in_ref.at[device["seq"]], dst_ref=slots.at[place],
            send_sem=send.at[k], recv_sem=receive.at[k], device_id=device, device_id_type=MESH,
        )
        moved.start()
        copies.append(moved)
    slots[place] = in_ref[place]
    for moved in copies:
        moved.wait()
    total = slots[0]
    for i in range(1, count):
        total = total + slots[i]
    out_ref[...] = total


def scatter_sum(number, array):
    count = array.shape[0]
    vmem = pl.BlockSpec(memory_space=pltpu.VMEM)
    return pl.pallas_call(
        functools.partial(scatter_kernel, count),
        out_shape=jax.ShapeDtypeStruct(array.shape[1:], jnp.float32),
        in_specs=[vmem],
        out_specs=vmem,
        scratch_shapes=[
            pltpu.VMEM(array.shape, jnp.float32),
            pltpu.SemaphoreType.DMA((count - 1,)),
            pltpu.SemaphoreType.DMA((count - 1,)),
        ],
        compiler_params=pltpu.CompilerParams(
            collective_id=number, has_side_effects=True, vmem_limit_bytes=VMEM
        ),
        cost_estimate=cost(4 << 30, 1 << 20),
    )(array)


def state_of(keep, doc, keys, values):
    keep = jnp.broadcast_to(keep[:, None], (keep.shape[0], 64))
    return jnp.concatenate([keep, jnp.full_like(keep, doc), keys, values], axis=1)


def final_kernel(tiles, head_count, *refs):
    act_in, near_in, dy_own, dy_their, dy_near, dy_far, in_own, in_their, branch_own, branch_their = refs[:10]
    sides = refs[10 : 10 + 2 * head_count]
    part, outs = refs[10 + 2 * head_count], refs[11 + 2 * head_count : 11 + 3 * head_count]
    (out_down, added, far, across, wide_in, wide_branch, heads, stage, stage_head,
     act, their_act, near_act, far_act, wide_dy, head_tile, to_middle, from_middle, near, own_sum, arrived,
     own_sems, head_sems, stage_sems, act_sems, *sems) = refs[11 + 3 * head_count :]
    place = lax.axis_index("seq")
    line = place // 2
    at_end = (line == 0) | (line == 3)
    in_middle = jnp.logical_not(at_end)
    partner, beside = {"seq": other_of(place, 1)}, {"seq": other_of(place, 2)}
    opposite = {"seq": place + jnp.where(line == 1, 2, -2)}
    rows = act.shape[0]
    wide = out_down.shape[0]
    head = heads.shape[1] // head_count
    columns = [pl.ds(i * 256, 256) for i in range(heads.shape[1] // 256)]
    down = [pl.ds(*tile) for tile in tiles]
    out = [outs[i // 2].at[:, pl.ds(i % 2 * 256, 256)] for i in range(len(columns))]

    number = lax.axis_index("head")
    sibling, over_y = {"head": other_of(number, 1)}, {"head": other_of(number, 2)}
    barrier = pltpu.get_barrier_semaphore()
    for device in (beside, partner, sibling, over_y):
        pl.semaphore_signal(barrier, inc=1, device_id=device, device_id_type=MESH)

    @pl.when(in_middle)
    def _():
        pl.semaphore_signal(barrier, inc=1, device_id=opposite, device_id_type=MESH)

    roles = [jnp.where(line < 2, a, b) for a, b in ((2, 1), (3, 0), (1, 2), (0, 3))]
    starts = [pl.multiple_of((2 * role + place % 2) * wide, 128) for role in roles]

    def load(source, target, sem):
        copied = pltpu.make_async_copy(source, target, sem)
        copied.start()
        return copied

    in_loads, branch_loads, dy_loads = (
        [
            load(
                source.at[:, pl.ds(start, wide)],
                target.at[pl.ds(0, rows), pl.ds(r * wide, wide)],
                own_sems.at[k, r],
            )
            for r, start in enumerate(starts)
        ]
        for k, (source, target) in enumerate(
            ((in_own, wide_in), (branch_own, wide_branch), (dy_own, wide_dy))
        )
    )
    head_loads = [
        load(sides[2 * i], heads.at[pl.ds(0, rows), pl.ds(i * head, head)], head_sems.at[0, i])
        for i in range(head_count)
    ]
    ready = (0, head_count - 1)
    head_loads += [load(sides[2 * i + 1], stage_head.at[i], head_sems.at[1, i]) for i in ready]
    act_loads = [
        load(act_in, act, act_sems.at[0]),
        load(near_in, near_act, act_sems.at[1]),
    ]
    jobs = [(in_their, wide_in, 1), (branch_their, wide_branch, 1)]
    jobs += [(dy_their, wide_dy, 1), (dy_near, wide_dy, 2), (dy_far, wide_dy, 3)]

    def staged(k):
        return [
            load(jobs[k][0].at[role], stage.at[k % 2, r], stage_sems.at[k % 2, r])
            for r, role in enumerate(roles)
        ]

    under_way = {0: staged(0), 1: staged(1)}

    def settle(k):
        for one in under_way[k]:
            one.wait()
        _, target, group = jobs[k]
        for r in range(4):
            target[group * rows : (group + 1) * rows, r * wide : (r + 1) * wide] = stage[
                k % 2, r
            ].astype(jnp.bfloat16)

    pl.semaphore_wait(barrier, 4 + in_middle.astype(jnp.int32))

    def remote(source, target, kind, i, device):
        return pltpu.make_async_remote_copy(
            src_ref=source, dst_ref=target, send_sem=sems[2 * kind].at[i],
            recv_sem=sems[2 * kind + 1].at[i], device_id=device, device_id_type=MESH,
        )

    chunk = part.shape[0] // CHUNKS
    half = chunk // 2
    low = number % 2
    mine_of = [pl.ds(pl.multiple_of(c * chunk + low * half, 8), half) for c in range(CHUNKS)]
    other_half = [pl.ds(pl.multiple_of(c * chunk + (1 - low) * half, 8), half) for c in range(CHUNKS)]
    nears = [remote(part.at[h], near.at[c], 8, c, sibling) for c, h in enumerate(other_half)]
    sums = [remote(own_sum.at[c], arrived.at[c], 9, c, over_y) for c in range(CHUNKS)]
    backs = [remote(added.at[h], added.at[h], 10, c, sibling) for c, h in enumerate(mine_of)]
    head_trades = [
        remote(sides[2 * i + 1], stage_head.at[i], 7, i - 1, partner)
        for i in range(1, head_count - 1)
    ]
    for one in nears:
        one.start()
    for one in in_loads + head_loads:
        one.wait()
    settle(0)
    settle(1)

    second = pl.ds(wide, wide)
    to_side = [remote(far.at[:, c], far.at[:, c], 0, i, beside) for i, c in enumerate(columns)]
    over = [
        remote(far.at[pl.ds(0, 2 * wide), c], across.at[:, c], 1, i, opposite) for i, c in enumerate(columns)
    ]
    home = [remote(across.at[second, c], out[i], 2, i, beside) for i, c in enumerate(columns)]
    trades = [remote(act_in.at[:, c], their_act.at[:, c], 3, i, partner) for i, c in enumerate(down)]
    passes = [remote(near_in.at[:, c], far_act.at[:, c], 4, i, partner) for i, c in enumerate(down)]
    over_down = [
        remote(to_middle.at[:, c], from_middle.at[:, c], 5, i, opposite) for i, c in enumerate(down)
    ]
    home_down = [
        remote(from_middle.at[second, c], out_down.at[:, c], 6, i, beside) for i, c in enumerate(down)
    ]

    @pl.when(at_end)
    def _():
        for one in head_trades:
            one.start()

    @pl.when(in_middle)
    def _():
        under_way[2], under_way[3] = staged(2), staged(3)
        settle(2)
        under_way[4] = staged(4)
        settle(3)
        settle(4)
        for i, (trade, onward) in enumerate(zip(trades, passes)):
            trade.start()
            onward.start()
            if i < len(head_trades):
                head_trades[i].start()

    for c in range(CHUNKS):
        nears[c].wait_recv()
        own_sum[c] = part[mine_of[c], :] + near[c]
        sums[c].start()

    def receive(i):
        if 0 < i < head_count - 1:
            head_trades[i - 1].wait_recv()
        heads[rows:, i * head : (i + 1) * head] = stage_head[i].astype(jnp.bfloat16)

    for i in ready:
        receive(i)

    down_at = {min(2 * j, len(columns) - len(down) + j): j for j in range(len(down))}
    order = [0, 1, 2 * head_count - 2, 2 * head_count - 1, *range(2, 2 * head_count - 2)]

    def wide_of(i):
        return wide_branch if i >= 2 * (head_count - 1) else wide_in

    def settle_down():
        for one in dy_loads + act_loads:
            one.wait()

    for one in branch_loads:
        one.wait()

    @pl.when(at_end)
    def _():
        for k, i in enumerate(order):
            if k > 3 and i % 2 == 0:
                receive(i // 2)
            far[:, columns[i]] = tn(wide_of(i)[:, : 3 * wide], heads[:, columns[i]])
            to_side[i].start()
        settle_down()

    @pl.when(at_end)
    def _():
        for k, i in enumerate(order):
            c = columns[i]
            mine = tn(wide_of(i)[:, 3 * wide :], heads[:, c])
            home[i].wait_recv()
            out[i][...] = out[i][...] + mine
            if k in down_at:
                home_down[down_at[k]].wait_recv()
        for one in to_side:
            one.wait_send()

    @pl.when(in_middle)
    def _():
        def finish(i):
            c = columns[i]
            mine = tn(wide_of(i)[:, 3 * wide :], heads[:, c])
            over[i].wait_recv()
            across[wide:, c] = across[wide:, c] + mine
            home[i].start()
            out[i][...] = far[2 * wide :, c] + across[:wide, c]

        settle_down()
        for k, i in enumerate(order):
            c = columns[i]
            if k > 3 and i % 2 == 0:
                receive(i // 2)
            j = down_at.get(k)
            if j is not None:
                d = down[j]
                size = tiles[j][1]
                tile = head_tile.at[:, pl.ds(0, size)]
                trades[j].wait_recv()
                passes[j].wait_recv()
                for g, side in enumerate((act, their_act, near_act, far_act)):
                    tile[g * rows : (g + 1) * rows, :] = side[:, d].astype(jnp.bfloat16)
                to_middle[:, d] = tn(wide_dy[:, : 2 * wide], tile[...])
                over_down[j].start()
                out_down[:, d] = tn(wide_dy[:, 2 * wide : 3 * wide], tile[...])
                home_part = tn(wide_dy[:, 3 * wide :], tile[...])
            mine = tn(wide_of(i)[:, : 3 * wide], heads[:, c])
            to_side[i].wait_recv()
            far[:, c] = far[:, c] + mine
            over[i].start()
            if j is not None:
                over_down[j].wait_recv()
                from_middle[wide:, d] = from_middle[wide:, d] + home_part
                home_down[j].start()
                out_down[:, d] = out_down[:, d] + from_middle[:wide, d]
            if k:
                finish(order[k - 1])
        finish(order[-1])
        for one in over + home + trades + passes + over_down + home_down:
            one.wait_send()

    for c in range(CHUNKS):
        sums[c].wait()
        added[mine_of[c], :] = own_sum[c] + arrived[c]
        backs[c].start()
    for one in head_trades + nears:
        one.wait_send()
    for one in backs:
        one.wait()


def final_gradients(number, part, act, near_act, dy, wide_in, wide_branch, heads):
    rows, hidden = act.shape
    wide = dy[1].shape[2]
    head = heads[0][0].shape[1]
    count = len(heads)
    total = head * count
    tiles = column_tiles(hidden)
    f32, bf16 = jnp.float32, jnp.bfloat16
    dma = pltpu.SemaphoreType.DMA
    hbm, vmem = pl.BlockSpec(memory_space=pl.ANY), pl.BlockSpec(memory_space=pltpu.VMEM)
    whole = pltpu.VMEM((rows, hidden), f32)
    sides = [a for pair in heads for a in pair]
    half = (CHUNKS, rows // CHUNKS // 2, part.shape[1])
    return pl.pallas_call(
        functools.partial(final_kernel, tiles, count),
        out_shape=(
            *[jax.ShapeDtypeStruct((wide, head), f32)] * count,
            jax.ShapeDtypeStruct((wide, hidden), f32),
            jax.ShapeDtypeStruct(part.shape, f32),
        ),
        in_specs=[hbm] * (10 + len(sides)) + [vmem],
        out_specs=(vmem,) * (count + 2),
        scratch_shapes=[
            pltpu.VMEM((3 * wide, total), f32),
            pltpu.VMEM((2 * wide, total), f32),
            pltpu.VMEM((2 * rows, 4 * wide), bf16),
            pltpu.VMEM((2 * rows, 4 * wide), bf16),
            pltpu.VMEM((2 * rows, total), bf16),
            pltpu.VMEM((2, 4, rows, wide), f32),
            pltpu.VMEM((count, rows, head), f32),
            whole, whole, whole, whole,
            pltpu.VMEM((4 * rows, 4 * wide), bf16),
            pltpu.VMEM((4 * rows, 256), bf16),
            pltpu.VMEM((2 * wide, hidden), f32),
            pltpu.VMEM((2 * wide, hidden), f32),
            pltpu.VMEM(half, f32), pltpu.VMEM(half, f32), pltpu.VMEM(half, f32),
            dma((3, 4)), dma((2, count)), dma((2, 4)), dma((2,)),
        ]
        + [dma((total // 256,))] * 6
        + [dma((len(tiles),))] * 8
        + [dma((count - 2,))] * 2
        + [dma((CHUNKS,))] * 6,
        compiler_params=pltpu.CompilerParams(
            collective_id=number, has_side_effects=True, vmem_limit_bytes=FINAL_VMEM
        ),
        cost_estimate=cost(200 << 30, 16 << 20),
    )(act, near_act, *dy, *wide_in, *wide_branch, *sides, part)


def normed_after(c, rows, added, own):
    stream, gain, normed_out, float_out, normed, normed_f, sems = own

    def copies(c):
        mine = pl.ds(c * rows, rows)
        return [
            pltpu.make_async_copy(normed.at[mine], normed_out.at[mine], sems.at[0, c]),
            pltpu.make_async_copy(normed_f.at[mine], float_out.at[mine], sems.at[1, c]),
        ]

    if c is None:
        for i in range(CHUNKS):
            for one in copies(i):
                one.wait()
        return
    mine = pl.ds(c * rows, rows)
    hidden = stream[mine, :].astype(jnp.float32) + added[mine, :]
    added[mine, :] = hidden
    rounded = (hidden * rms_scale(hidden) * gain[...]).astype(jnp.bfloat16)
    normed[mine, :] = rounded
    normed_f[mine, :] = rounded.astype(jnp.float32)
    for one in copies(c):
        one.start()


def norm_after(stream, gain):
    half, full = (jax.ShapeDtypeStruct(stream.shape, t) for t in (jnp.bfloat16, jnp.float32))
    return (
        normed_after,
        (stream, gain.reshape(1, -1)),
        (half, full),
        (
            pltpu.VMEM(stream.shape, jnp.bfloat16),
            pltpu.VMEM(stream.shape, jnp.float32),
            pltpu.SemaphoreType.DMA((2, CHUNKS)),
        ),
    )


def matmul_work(product, column, count, piece, pieces, left_ref, *refs):
    rights, outs, left = refs[:count], refs[count : 2 * count], refs[2 * count]
    sides, sems = refs[2 * count + 1 : -1], refs[-1]
    copies = [pltpu.make_async_copy(left_ref, left, sems.at[0])]
    copies += [pltpu.make_async_copy(a, b, sems.at[1 + i]) for i, (a, b) in enumerate(zip(rights, sides))]
    if piece is None:
        for one in copies:
            one.start()
        return
    if piece == 0:
        for one in copies:
            one.wait()
    for right, out in zip(sides, outs):

        def tile(i, carry):
            columns = pl.ds(pl.multiple_of(i * column, column), column)
            side = right[columns, :] if product is nt else right[:, columns]
            out[:, columns] = product(left[...], side)
            return carry

        tiles = out.shape[1] // column
        lax.fori_loop(tiles * piece // pieces, tiles * (piece + 1) // pieces, tile, 0)


def column_tiles(size):
    wide = 256 if size >= 256 else size
    return [(at, min(wide, size - at)) for at in range(0, size, wide)]


def hidden_units(send_tile, refs, own):
    (normed_in, gate_in, up_in, down_in, d_act_in, act_f_out, d_gate_out, d_up_out, up_f_out, ffn_out,
     gate_f, act_f, act_ref, d_gate_ref, d_up_ref, up_f_ref, ffn_ref, normed, w_gate, w_up, w_down, d_act, sems, tile_sems, out_sems) = own
    whole = [
        pltpu.make_async_copy(normed_in, normed, sems.at[0]),
        pltpu.make_async_copy(d_act_in, d_act, sems.at[1]),
        pltpu.make_async_copy(down_in, w_down, sems.at[2]),
    ]
    parts = []
    tiles = column_tiles(act_ref.shape[1])
    for i, (at, size) in enumerate(tiles):
        columns = pl.ds(at, size)
        parts.append(
            [
                pltpu.make_async_copy(gate_in.at[:, columns], w_gate.at[:, columns], tile_sems.at[0, i]),
                pltpu.make_async_copy(up_in.at[:, columns], w_up.at[:, columns], tile_sems.at[1, i]),
            ]
        )
    whole[0].start()
    for one in parts[0]:
        one.start()
    whole[1].start()
    for pair in parts[1:]:
        for one in pair:
            one.start()
    whole[2].start()
    whole[0].wait()
    for i, (at, size) in enumerate(tiles):
        columns = pl.ds(at, size)
        for one in parts[i]:
            one.wait()
        gate = nn(normed[...], w_gate[:, columns])
        up = nn(normed[...], w_up[:, columns])
        if i == 0:
            whole[1].wait()
        sig = jax.nn.sigmoid(gate)
        silu = gate * sig
        pull = d_act[:, columns]
        act = (silu * up).astype(jnp.bfloat16)
        act_ref[:, columns] = act
        act_f[:, columns] = act.astype(jnp.float32)
        d_gate = (pull * up * sig * (1.0 + gate * (1.0 - sig))).astype(jnp.bfloat16)
        d_up = (pull * silu).astype(jnp.bfloat16)
        d_gate_ref[:, columns] = d_gate
        d_up_ref[:, columns] = d_up
        gate_f[:, columns] = d_gate.astype(jnp.float32)
        send_tile(i, columns)
        up_f_ref[:, columns] = d_up.astype(jnp.float32)

    kept = [(act_f, act_f_out), (d_gate_ref, d_gate_out), (d_up_ref, d_up_out),
            (up_f_ref, up_f_out), (ffn_ref, ffn_out)]
    kept = [pltpu.make_async_copy(a, b, out_sems.at[i]) for i, (a, b) in enumerate(kept)]
    for one in kept[:-1]:
        one.start()
    part = refs["part"]

    def fill(c, rows):
        mine = pl.ds(c * rows, rows)

        def tile(i, carry):
            columns = pl.ds(pl.multiple_of(i * 256, 256), 256)
            part[mine, columns] = nt(d_gate_ref[mine, :], w_gate[columns, :]) + nt(
                d_up_ref[mine, :], w_up[columns, :]
            )
            return carry

        lax.fori_loop(0, part.shape[1] // 256, tile, 0)

    refs["finish"] = (whole[2], act_ref, w_down, ffn_ref, kept)
    return fill


def outer_product_beside(piece, pieces, refs):
    copied, act, w_down, out, kept = refs["finish"]
    copied.wait()

    def tile(i, carry):
        columns = pl.ds(pl.multiple_of(i * 256, 256), 256)
        out[:, columns] = nn(act[...], w_down[:, columns])
        return carry

    lax.fori_loop(0, out.shape[1] // 256, tile, 0)
    kept[-1].start()


def hidden_units_early(normed_mid, w_gate, w_up, w_down, d_act):
    rows, width = normed_mid.shape
    hidden = w_gate.shape[1]
    tiles = len(column_tiles(hidden))
    half = jax.ShapeDtypeStruct((rows, hidden), jnp.bfloat16)
    full = jax.ShapeDtypeStruct((rows, hidden), jnp.float32)
    return (
        hidden_units,
        (normed_mid, w_gate, w_up, w_down, d_act),
        (rows, hidden),
        tiles,
        (full, half, half, full, jax.ShapeDtypeStruct((rows, width), jnp.float32)),
        (
            pltpu.VMEM((rows, hidden), jnp.float32),
            pltpu.VMEM((rows, hidden), jnp.float32),
            pltpu.VMEM((rows, hidden), jnp.bfloat16),
            pltpu.VMEM((rows, hidden), jnp.bfloat16),
            pltpu.VMEM((rows, hidden), jnp.bfloat16),
            pltpu.VMEM((rows, hidden), jnp.float32),
            pltpu.VMEM((rows, width), jnp.float32),
            pltpu.VMEM(normed_mid.shape, jnp.bfloat16),
            pltpu.VMEM(w_gate.shape, jnp.bfloat16),
            pltpu.VMEM(w_up.shape, jnp.bfloat16),
            pltpu.VMEM(w_down.shape, jnp.bfloat16),
            pltpu.VMEM(d_act.shape, jnp.float32),
            pltpu.SemaphoreType.DMA((3,)),
            pltpu.SemaphoreType.DMA((2, tiles)),
            pltpu.SemaphoreType.DMA((5,)),
        ),
    )


def matmul_beside(product, left, *rights):
    columns = rights[0].shape[0] if product is nt else rights[0].shape[1]
    column = 256 if columns % 256 == 0 else 128
    return (
        functools.partial(matmul_work, product, column, len(rights)),
        (left, *rights),
        (jax.ShapeDtypeStruct((left.shape[0], columns), jnp.float32),) * len(rights),
        (
            pltpu.VMEM(left.shape, left.dtype),
            *[pltpu.VMEM(right.shape, right.dtype) for right in rights],
            pltpu.SemaphoreType.DMA((1 + len(rights),)),
        ),
        (True,) * (1 + len(rights)),
    )


def body(
    stream,
    seg_ids,
    attn_gain,
    w_query,
    w_key,
    w_value,
    w_outgate,
    w_low,
    w_slot,
    forget_bias,
    head_gain,
    w_out,
    mlp_gain,
    w_gate,
    w_up,
    w_down,
    cotangent,
):
    tok_rows = stream.shape[0]
    width = stream.shape[1]
    slots = w_slot.shape[2]
    head_width = w_query.shape[1]
    stream_f = stream.astype(jnp.float32)
    scale_in = rms_scale(stream_f)
    normed_in = (stream_f * scale_in * attn_gain).astype(jnp.bfloat16)
    key_rows = plain_dot(normed_in, w_key).astype(jnp.bfloat16)
    value_rows = plain_dot(normed_in, w_value).astype(jnp.bfloat16)
    ranked = plain_dot(normed_in, w_low)

    def decay_logs(ranked_in, slot_map, bias_row):
        return jax.nn.log_sigmoid(precise_dot(ranked_in, slot_map[0]) + bias_row[0]) / GATE_NORM

    log_decay, gate_pull = jax.vjp(decay_logs, ranked, w_slot, forget_bias)

    new = -jnp.expm1(log_decay)
    last_doc = seg_ids[tok_rows - 1]
    running = precise_dot(jnp.tril(jnp.ones((tok_rows, tok_rows), jnp.float32)), log_decay)
    total = running[tok_rows - 1]
    in_last = (seg_ids == last_doc)[:, None]
    factor = jnp.where(in_last, jnp.exp(jnp.where(in_last, total - running, 0.0)) * new, 0.0)
    def wide_float(array):
        return array.astype(jnp.float32)

    local_key = precise_left_t(factor, key_rows.astype(jnp.float32))
    local_value = precise_left_t(factor, value_rows.astype(jnp.float32))
    docs = seg_ids.astype(jnp.float32)
    own_state = state_of(jnp.exp(total), docs[tok_rows - 1], local_key, local_value)
    dy_f = cotangent.astype(jnp.float32)
    prefix, query_rows, gate_act = exchange(
        0,
        state=own_state,
        work=matmul_beside(nn, normed_in, w_query, w_outgate),
    )
    query_rows = query_rows.astype(jnp.bfloat16)
    key_in, value_in = prefix[:, 128 : 128 + head_width], prefix[:, 128 + head_width :]
    prior = prefix[0, 64]
    decay_all = jnp.where(docs[tok_rows - 1] == prior, jnp.exp(total), 0.0)
    before = jnp.concatenate([prior[None], docs[CHUNK - 1 : -1 : CHUNK]])
    docs = jnp.broadcast_to(docs[:, None], (tok_rows, slots))
    before = jnp.broadcast_to(jnp.repeat(before, CHUNK)[:, None], (tok_rows, slots))
    slot_read, scores, probs, key_states, value_states = read_slots(
        query_rows, key_rows, value_rows, log_decay, new, docs, before, key_in, value_in
    )
    scale_read = rms_scale(slot_read)
    normed_read = slot_read * scale_read * head_gain[0]
    gate_sig = jax.nn.sigmoid(gate_act)
    gate_silu = gate_act * gate_sig
    mixed_heads = (normed_read * gate_silu).astype(jnp.bfloat16)
    four = lax.axis_size("seq") == 8
    hidden, from_dy, *near_dy, normed_mid, normed_mid_f, d_act = exchange(
        1,
        part=plain_dot(mixed_heads, w_out),
        wides=(wide_to_send(cotangent),),
        relay=(dy_f,) if four else (),
        work=matmul_beside(nt, cotangent, w_down),
        after=norm_after(stream, mlp_gain),
    )
    wide_dy = cotangent, from_dy
    scale_mid = rms_scale(hidden)
    upstream = cotangent.astype(jnp.float32)
    d_mid, from_mid, *made = exchange(
        2,
        part=jax.ShapeDtypeStruct((tok_rows, width), jnp.float32),
        wides=(wide_to_send(normed_mid_f),),
        relay=(from_dy,) if four else (),
        early=hidden_units_early(normed_mid, w_gate, w_up, w_down, d_act),
    )
    if four:
        far_dy, from_gate, end_act, *made = made
    else:
        from_gate, *made = made
    act_f, d_gate, d_up, d_up_f, ffn_part = made
    wide_mid = normed_mid, from_mid
    grad_gate = pair_products((wide_mid, [(d_gate, from_gate)]))
    d_mid, grad_gate = together(d_mid, grad_gate)
    grad_gate = line_sum(grad_gate)
    grad_mlp_gain = jnp.sum(d_mid * hidden * scale_mid, axis=0)
    scaled_mid = d_mid * mlp_gain
    d_hidden = (
        upstream
        + scale_mid * scaled_mid
        - hidden * scale_mid**3 * jnp.mean(scaled_mid * hidden, axis=1, keepdims=True)
    )
    d_branch = d_hidden.astype(jnp.bfloat16)
    d_mixed = dot_right_t(d_branch, w_out)
    d_gate_act = (d_mixed * normed_read * gate_sig * (1.0 + gate_act * (1.0 - gate_sig))).astype(
        jnp.bfloat16
    )
    d_normed = d_mixed * gate_silu
    grad_head_gain = jnp.sum(d_normed * slot_read * scale_read, axis=0)[None, :]
    scaled_read = d_normed * head_gain[0]
    d_read = scale_read * scaled_read - slot_read * scale_read**3 * jnp.mean(
        scaled_read * slot_read, axis=1, keepdims=True
    )
    normed_f, ffn_part = together(wide_to_send(normed_in), ffn_part)
    ffn_out, from_in, from_up, *back = exchange(
        3,
        part=ffn_part,
        wides=(normed_f,),
        narrows=(d_up_f,),
        work=back_query(
            query_rows, key_rows, value_rows, log_decay, new, docs, before, scores, probs, key_states, value_states, d_read
        ),
    )
    wide_in = normed_in, from_in
    grad_up = pair_products((wide_mid, [(d_up, from_up)]))
    d_query, d_key, d_value, held, gained, to_keys, to_values, key_back, value_back = back
    query_back = d_query.astype(jnp.bfloat16)
    result = hidden + ffn_out
    squares = jnp.stack(
        [jnp.sum(stream_f * stream_f), jnp.sum(hidden * hidden), jnp.sum(result * result)]
    )
    key_back, grad_up, grad_gate, grad_mlp_gain, grad_head_gain, squares = together(
        key_back, grad_up, grad_gate, grad_mlp_gain, grad_head_gain, squares
    )
    grad_up = line_sum(grad_up)
    suffix, from_branch, from_outgate, from_mixed = exchange(
        4,
        state=state_of(decay_all, 0.0, key_back, value_back),
        reverse=True,
        wides=(wide_to_send(d_branch),),
        narrows=(wide_float(d_gate_act), wide_float(mixed_heads)),
    )
    key_end, value_end = suffix[:, 128 : 128 + head_width], suffix[:, 128 + head_width :]
    end_total = jnp.sum(key_states[-1] * key_end + value_states[-1] * value_end, axis=1)[None, :]
    key_back, value_back, d_logs = back_key(
        key_rows, value_rows, log_decay, new, docs, before, d_key, d_value, held, gained,
        to_keys, to_values, key_end, value_end, end_total,
    )
    d_ranked, grad_slot, grad_bias = gate_pull(d_logs)
    normed_f = normed_in.astype(jnp.float32)
    grad_low = precise_left_t(normed_f, d_ranked)
    d_in_part = (
        dot_right_t(query_back, w_query)
        + dot_right_t(key_back, w_key)
        + dot_right_t(value_back, w_value)
        + dot_right_t(d_gate_act, w_outgate)
        + precise_right_t(d_ranked, w_low.astype(jnp.float32))
    )
    late = [wide_float(a) for a in (query_back, key_back, value_back)]
    wide_branch = d_branch, from_branch
    if four:
        sides = [(d_gate_act, from_outgate), *zip((query_back, key_back, value_back), late), (mixed_heads, from_mixed)]
        act_f, grad_up = together(act_f, grad_up)
        *grad_rest, grad_down, d_in = final_gradients(
            5, d_in_part, act_f, end_act, (cotangent, from_dy, *near_dy, far_dy), wide_in, wide_branch, sides
        )
    else:
        d_in, *late = exchange(5, part=d_in_part, narrows=late)
        head_sides = [(d_gate_act, from_outgate), *zip((query_back, key_back, value_back), late), (mixed_heads, from_mixed)]
        grad_rest = pair_products((wide_in, head_sides[:4]), (wide_branch, head_sides[4:]))
        grad_rest = line_sum(grad_rest)
        (from_act,) = exchange(6, narrows=(act_f,))
        grad_down = pair_products((wide_dy, [(act_f.astype(jnp.bfloat16), from_act)]))
        grad_down = line_sum(grad_down)
        grad_rest = jnp.split(grad_rest, 5, axis=1)
    grad_outgate, grad_query, grad_key, grad_value, grad_out = grad_rest
    grad_attn_gain = jnp.sum(d_in * stream_f * scale_in, axis=0)
    scaled_in = d_in * attn_gain
    grad_stream = (
        d_hidden
        + scale_in * scaled_in
        - stream_f * scale_in**3 * jnp.mean(scaled_in * stream_f, axis=1, keepdims=True)
    ).astype(jnp.bfloat16)
    count = lax.axis_size("seq")
    small = [
        grad_attn_gain.reshape(count, -1),
        grad_mlp_gain.reshape(count, -1),
        grad_low.reshape(count, -1),
        jnp.moveaxis(grad_slot[0].reshape(-1, count, slots // count), 1, 0).reshape(count, -1),
        grad_bias.reshape(count, -1),
        grad_head_gain.reshape(count, -1),
        jnp.broadcast_to(squares, (count, 3)),
    ]
    sizes = [a.shape[1] for a in small]
    packed = jnp.concatenate(small, axis=1)
    packed = jnp.pad(packed, ((0, 0), (0, -packed.shape[1] % 1024)))
    packed = scatter_sum(7, packed.reshape(count, -1, 128)).reshape(-1)
    ends = [sum(sizes[: i + 1]) for i in range(len(sizes))]
    small = [packed[end - size : end] for end, size in zip(ends, sizes)]
    stream_rms = jnp.sqrt(small[6] / (tok_rows * count * width))
    summed = (
        small[0],
        grad_query,
        grad_key,
        grad_value,
        grad_outgate,
        small[2].reshape(width // count, -1),
        small[3].reshape(1, -1, slots // count),
        small[4][None, :],
        small[5][None, :],
        grad_out.T,
        small[1],
        grad_gate,
        grad_up,
        grad_down.T,
    )
    mixer_parts = summed[:10]
    ffn_parts = summed[10:]
    return (
        result.astype(jnp.bfloat16),
        grad_stream,
        mixer_parts[0],
        mixer_parts[1],
        mixer_parts[2],
        mixer_parts[3],
        mixer_parts[4],
        mixer_parts[5],
        mixer_parts[6],
        mixer_parts[7],
        mixer_parts[8],
        mixer_parts[9],
        ffn_parts[0],
        ffn_parts[1],
        ffn_parts[2],
        ffn_parts[3],
        stream_rms,
    )


def solution(mesh):
    in_specs = (
        P("seq", None),
        P("seq"),
        P(),
        P(None, "head"),
        P(None, "head"),
        P(None, "head"),
        P(None, "head"),
        P(None, "head"),
        P("head", None, None),
        P("head", None),
        P("head", None),
        P("head", None),
        P(),
        P(None, "head"),
        P(None, "head"),
        P("head", None),
        P("seq", None),
    )
    out_specs = (
        P("seq", None),
        P("seq", None),
        P("seq"),
        P("seq", "head"),
        P("seq", "head"),
        P("seq", "head"),
        P("seq", "head"),
        P("seq", "head"),
        P("head", None, "seq"),
        P("head", "seq"),
        P("head", "seq"),
        P("head", "seq"),
        P("seq"),
        P("seq", "head"),
        P("seq", "head"),
        P("head", "seq"),
        P(),
    )
    return jax.shard_map(body, mesh=mesh, in_specs=in_specs, out_specs=out_specs, check_vma=False)
```

```python
import functools
import math

import jax
import jax.numpy as jnp
from jax import lax
from jax.experimental import pallas as pl
from jax.experimental.pallas import tpu as pltpu
from jax.sharding import PartitionSpec as P

CHUNK = 64
CHUNKS = 4
MESH = pl.DeviceIdType.MESH
VMEM = 24 << 20
MORE = 10 << 20
EXCHANGE_VMEM = 50 << 20
FINAL_VMEM = 60 << 20
READ_COST = 17 << 30


EPSILON = 1e-06
GATE_NORM = 8.0
PRECISE = lax.Precision.HIGHEST


def width_blocks(array, parity):
    count = lax.axis_size("seq")
    wide = array.shape[1] // count
    return jnp.stack(
        [
            lax.dynamic_slice_in_dim(array, (2 * line + parity) * wide, wide, 1)
            for line in range(count // 2)
        ]
    )


def whole_tiles(array):
    return array.shape[1] // lax.axis_size("seq") % 128 == 0


def wide_to_send(array):
    array = array.astype(jnp.float32)
    if whole_tiles(array):
        return array
    return width_blocks(array, 1 - lax.axis_index("seq") % 2)


def product_kernel(layout, *refs):
    out_ref, sides = refs[-2:]
    refs = list(refs[1:-2])
    first = pl.program_id(0) == 0
    at = 0
    for narrows in layout:
        own, theirs = refs.pop(0), refs.pop(0)
        block = jnp.concatenate(
            [own[...].reshape(own.shape[-2:]), theirs[0].astype(jnp.bfloat16)], axis=0
        )
        for _ in range(narrows):
            own_narrow, their_narrow = refs.pop(0), refs.pop(0)
            rows, size = own_narrow.shape

            @pl.when(first)
            def _(at=at, own_narrow=own_narrow, their_narrow=their_narrow, rows=rows, size=size):
                sides[:rows, at : at + size] = own_narrow[...]
                sides[rows:, at : at + size] = their_narrow[...].astype(jnp.bfloat16)

            out_ref[0, :, at : at + size] = tn(block, sides[:, at : at + size])
            at += size


def pair_products(*jobs):
    count = lax.axis_size("seq")
    lines = count // 2
    parity = lax.axis_index("seq") % 2
    ins, specs, total = [], [], 0
    for (own, theirs), narrows in jobs:
        rows, wide = own.shape[0], own.shape[1] // count
        if whole_tiles(own):
            ins.append(own)
            specs.append(pl.BlockSpec((rows, wide), lambda i, p: (0, 2 * i + p[0])))
        else:
            ins.append(width_blocks(own, parity))
            specs.append(pl.BlockSpec((1, rows, wide), lambda i, p: (i, 0, 0)))
        ins.append(theirs)
        specs.append(pl.BlockSpec((1, rows, wide), lambda i, p: (i, 0, 0)))
        for pair in narrows:
            for side in pair:
                ins.append(side)
                specs.append(pl.BlockSpec(side.shape, lambda i, p: (0, 0)))
            total += pair[0].shape[1]
    return pl.pallas_call(
        functools.partial(product_kernel, [len(narrows) for _, narrows in jobs]),
        out_shape=jax.ShapeDtypeStruct((lines, wide, total), jnp.float32),
        grid_spec=pltpu.PrefetchScalarGridSpec(
            num_scalar_prefetch=1,
            grid=(lines,),
            in_specs=specs,
            out_specs=pl.BlockSpec((1, wide, total), lambda i, p: (i, 0, 0)),
            scratch_shapes=[pltpu.VMEM((2 * rows, total), jnp.bfloat16)],
        ),
        compiler_params=pltpu.CompilerParams(vmem_limit_bytes=VMEM),
        cost_estimate=cost(4 * rows * wide * lines * total, 8 * wide * lines * total),
    )(parity.reshape(1).astype(jnp.int32), *ins)


def line_sum(product):
    lines = product.shape[0]
    groups = [[line * 2 + x for line in range(lines)] for x in range(2)]
    return lax.psum_scatter(
        product, "seq", scatter_dimension=0, axis_index_groups=groups, tiled=True
    )[0]


def together(*arrays):
    return lax.optimization_barrier(arrays)


def precise_dot(left, right):
    return jnp.dot(left, right, precision=PRECISE, preferred_element_type=jnp.float32)


def plain_dot(left, right):
    return jnp.dot(left, right, preferred_element_type=jnp.float32)


def dot_right_t(left, right):
    return lax.dot_general(
        left, right, (((1,), (1,)), ((), ())), preferred_element_type=jnp.float32
    )


def dot_left_t(left, right):
    return lax.dot_general(
        left, right, (((0,), (0,)), ((), ())), preferred_element_type=jnp.float32
    )


def precise_left_t(left, right):
    return lax.dot_general(
        left, right, (((0,), (0,)), ((), ())), precision=PRECISE, preferred_element_type=jnp.float32
    )


def precise_right_t(left, right):
    return lax.dot_general(
        left, right, (((1,), (1,)), ((), ())), precision=PRECISE, preferred_element_type=jnp.float32
    )


def rms_scale(value):
    return lax.rsqrt(jnp.mean(value * value, axis=-1, keepdims=True) + EPSILON)


def split(value):
    high = value.astype(jnp.bfloat16)
    return high, (value - high.astype(jnp.float32)).astype(jnp.bfloat16)


def nn(left, right):
    return jnp.dot(left, right, preferred_element_type=jnp.float32)


def nt(left, right):
    return lax.dot_general(
        left, right, (((1,), (1,)), ((), ())), preferred_element_type=jnp.float32
    )


def tn(left, right):
    return lax.dot_general(
        left, right, (((0,), (0,)), ((), ())), preferred_element_type=jnp.float32
    )


def two(product, left, right):
    high, low = split(right)
    return product(left, high) + product(left, low)


def three(product, left, right):
    left_high, left_low = split(left)
    right_high, right_low = split(right)
    return product(left_high, right_high) + (
        product(left_low, right_high) + product(left_high, right_low)
    )


def row_blocks(value):
    return [value[r : r + 8] for r in range(0, value.shape[0], 8)]


def exact_dot(left, right):
    return jnp.dot(left, right, precision=PRECISE, preferred_element_type=jnp.float32)


def triangle(size, upper):
    row = lax.broadcasted_iota(jnp.int32, (size, size), 0)
    column = lax.broadcasted_iota(jnp.int32, (size, size), 1)
    keep = row <= column if upper else row >= column
    return jnp.where(keep, 1.0, 0.0)


def spans(running, docs, span_s):
    size = running.shape[0]
    run, doc = row_blocks(running), row_blocks(docs)
    place = lax.broadcasted_iota(jnp.int32, (8, running.shape[1]), 0)
    for j in range(size):
        for r in range(j // 8, size // 8):
            ok = doc[r] == docs[j : j + 1]
            if r == j // 8 and j % 8:
                ok = ok & (place >= j % 8)
            span_s[j, 8 * r : 8 * r + 8] = jnp.where(ok, jnp.exp(run[r] - running[j : j + 1]), 0.0)


def to_end(running, docs):
    last = running.shape[0] - 1
    return jnp.where(
        docs == docs[last : last + 1], jnp.exp(running[last : last + 1] - running), 0.0
    )


def turned(to_end_weights, kept):
    size, slots = to_end_weights.shape
    fill = jnp.broadcast_to(kept, (128 - size, slots))
    both = jnp.concatenate([to_end_weights, fill], axis=0).T
    return both[:, :size], both[:, size : size + 1]


def read_kernel(
    q_ref, k_ref, v_ref, log_ref, new_ref, doc_ref, prev_ref, kin_ref, vin_ref,
    read_ref, score_ref, prob_ref, ks_ref, vs_ref, span_s,
):
    size = span_s.shape[0]
    lower = triangle(size, False)
    scaling = q_ref.shape[1] ** (-0.5)
    ks_ref[0] = kin_ref[...]
    vs_ref[0] = vin_ref[...]
    lane = lax.broadcasted_iota(jnp.int32, (8, size), 1)

    def chunk(i, carry):
        rows = pl.ds(pl.multiple_of(i * size, size), size)
        queries, keys, values = q_ref[rows, :], k_ref[rows, :], v_ref[rows, :]
        new, docs = new_ref[rows, :], doc_ref[rows, :]
        running = exact_dot(lower, log_ref[rows, :])
        carried = jnp.where(docs == prev_ref[rows, :], jnp.exp(running), 0.0)
        key_state, value_state = ks_ref[i], vs_ref[i]
        spans(running, docs, span_s)
        affinity = row_blocks(nt(queries, keys))
        scores = row_blocks(carried * two(nt, queries, key_state))
        for j in range(size):
            for r in range(j // 8, size // 8):
                weight = span_s[j, 8 * r : 8 * r + 8] * new[j : j + 1]
                scores[r] = scores[r] + weight * affinity[r][:, j : j + 1]
        scores = scaling * jnp.concatenate(scores, axis=0)
        probs = jnp.exp(scores - jnp.max(scores, axis=1, keepdims=True))
        probs = probs / jnp.sum(probs, axis=1, keepdims=True)
        score_ref[rows, :] = scores
        prob_ref[rows, :] = probs
        used = probs.astype(jnp.bfloat16).astype(jnp.float32)
        part = row_blocks(used)
        mixing = [jnp.zeros((8, size), jnp.float32) for _ in part]
        for j in range(size):
            for r in range(j // 8, size // 8):
                weight = span_s[j, 8 * r : 8 * r + 8] * new[j : j + 1]
                total = jnp.sum(part[r] * weight, axis=1, keepdims=True)
                mixing[r] = jnp.where(lane == j, total, mixing[r])
        high, low = split(jnp.concatenate(mixing, axis=0))
        read_ref[rows, :] = (
            three(nn, used * carried, value_state) + nn(high, values) + nn(low, values)
        )
        end, kept = turned(to_end(running, docs) * new, carried[size - 1 : size])
        high, low = split(end)
        ks_ref[i + 1] = kept * key_state + (nn(high, keys) + nn(low, keys))
        vs_ref[i + 1] = kept * value_state + (nn(high, values) + nn(low, values))
        return carry

    lax.fori_loop(0, q_ref.shape[0] // size, chunk, 0)


def back_query_kernel(
    piece, pieces, q_ref, k_ref, v_ref, log_ref, new_ref, doc_ref, prev_ref, score_ref, prob_ref, ks_ref, vs_ref, g_ref,
    dq_ref, dk_ref, dv_ref, held_ref, gained_ref, xk_ref, xv_ref, dkin_ref, dvin_ref, span_s,
):
    if piece is None:
        return
    size = span_s.shape[0]
    count = q_ref.shape[0] // size
    lower = triangle(size, False)
    scaling = q_ref.shape[1] ** (-0.5)
    dkin_ref[...] = jnp.zeros_like(dkin_ref)
    dvin_ref[...] = jnp.zeros_like(dvin_ref)
    lane = lax.broadcasted_iota(jnp.int32, (8, size), 1)

    def chunk(turn, carry):
        i = count - 1 - turn
        start = pl.multiple_of(i * size, size)
        rows = pl.ds(start, size)
        queries, keys, values, grads = q_ref[rows, :], k_ref[rows, :], v_ref[rows, :], g_ref[rows, :]
        new, docs = new_ref[rows, :], doc_ref[rows, :]
        running = exact_dot(lower, log_ref[rows, :])
        carried = jnp.where(docs == prev_ref[rows, :], jnp.exp(running), 0.0)
        spans(running, docs, span_s)
        affinity = row_blocks(nt(queries, keys))
        grad_high, grad_low = split(grads)
        pull = row_blocks(nt(grad_high, values) + nt(grad_low, values))
        back = row_blocks(carried * three(nt, grads, vs_ref[i]))
        for j in range(size):
            for r in range(j // 8, size // 8):
                weight = span_s[j, 8 * r : 8 * r + 8] * new[j : j + 1]
                back[r] = back[r] + weight * pull[r][:, j : j + 1]
        back = jnp.concatenate(back, axis=0)
        probs = prob_ref[rows, :]
        used = probs.astype(jnp.bfloat16).astype(jnp.float32)
        inner = probs * (back - jnp.sum(probs * back, axis=1, keepdims=True))
        gained_ref[rows, :] = inner * score_ref[rows, :] + used * back
        outer = scaling * inner
        part, used_part = row_blocks(outer), row_blocks(used)
        key_mix = [jnp.zeros((8, size), jnp.float32) for _ in part]
        value_mix = [jnp.zeros((8, size), jnp.float32) for _ in part]
        for j in range(size):
            held = None
            for r in range(j // 8, size // 8):
                span = span_s[j, 8 * r : 8 * r + 8]
                key_side, value_side = part[r] * span, used_part[r] * span
                own = key_side * affinity[r][:, j : j + 1] + value_side * pull[r][:, j : j + 1]
                held = own if held is None else held + own
                fresh = new[j : j + 1]
                key_mix[r] = jnp.where(
                    lane == j, jnp.sum(key_side * fresh, axis=1, keepdims=True), key_mix[r]
                )
                value_mix[r] = jnp.where(
                    lane == j, jnp.sum(value_side * fresh, axis=1, keepdims=True), value_mix[r]
                )
            held_ref[pl.ds(start + j, 1), :] = jnp.sum(held, axis=0, keepdims=True)
        key_mix = jnp.concatenate(key_mix, axis=0)
        value_mix = jnp.concatenate(value_mix, axis=0)
        outer_in, used_in = outer * carried, used * carried
        high, low = split(key_mix)
        dq_ref[rows, :] = three(nn, outer_in, ks_ref[i]) + (nn(high, keys) + nn(low, keys))
        fill = jnp.zeros((128 - size, size), jnp.float32)
        high, low = split(jnp.concatenate([key_mix, fill], axis=0).T[:, :size])
        dk_ref[rows, :] = nn(high, queries) + nn(low, queries)
        mixed = jnp.concatenate([value_mix, fill], axis=0).T[:, :size]
        dv_ref[rows, :] = three(nn, mixed, grads)
        outer_t, kept = turned(outer_in, carried[size - 1 : size])
        used_t, kept = turned(used_in, carried[size - 1 : size])
        high, low = split(outer_t)
        to_key = nn(high, queries) + nn(low, queries)
        to_value = three(nn, used_t, grads)
        xk_ref[i] = to_key
        xv_ref[i] = to_value
        dkin_ref[...] = kept * dkin_ref[...] + to_key
        dvin_ref[...] = kept * dvin_ref[...] + to_value
        return carry

    lax.fori_loop(0, count, chunk, 0)


def back_key_kernel(
    k_ref, v_ref, log_ref, new_ref, doc_ref, prev_ref, dk_in_ref, dv_in_ref, held_ref, gained_ref,
    xk_ref, xv_ref, dkend_ref, dvend_ref, total_ref,
    dk_ref, dv_ref, dlog_ref, ks, vs, total,
):
    size = CHUNK
    count = k_ref.shape[0] // size
    lower, upper = triangle(size, False), triangle(size, True)
    ks[...] = dkend_ref[...]
    vs[...] = dvend_ref[...]
    total[...] = total_ref[...]

    def chunk(turn, carry):
        i = count - 1 - turn
        rows = pl.ds(pl.multiple_of(i * size, size), size)
        keys, values = k_ref[rows, :], v_ref[rows, :]
        logs, new, docs = log_ref[rows, :], new_ref[rows, :], doc_ref[rows, :]
        running = exact_dot(lower, logs)
        carried = jnp.where(docs == prev_ref[rows, :], jnp.exp(running), 0.0)
        end = to_end(running, docs)
        weight = end * new
        dk_ref[rows, :] = (dk_in_ref[rows, :] + three(nn, weight, ks[...])).astype(dk_ref.dtype)
        dv_ref[rows, :] = (dv_in_ref[rows, :] + three(nn, weight, vs[...])).astype(dv_ref.dtype)
        held = held_ref[rows, :] + end * (two(nt, keys, ks[...]) + two(nt, values, vs[...]))
        change = gained_ref[rows, :] - new * held
        after = exact_dot(upper, change) + total[...]
        dlog_ref[rows, :] = after - jnp.exp(logs) * held
        total[...] = after[:1]
        unused, kept = turned(carried, carried[size - 1 : size])
        ks[...] = kept * ks[...] + xk_ref[i]
        vs[...] = kept * vs[...] + xv_ref[i]
        return carry

    lax.fori_loop(0, count, chunk, 0)


def room(arrays):
    total = 0
    for a in arrays:
        shape = a.shape[:-1] + (-(-a.shape[-1] // 128) * 128,)
        total += math.prod(shape) * jnp.dtype(a.dtype).itemsize
    return total + MORE


def cost(flops, moved):
    return pl.CostEstimate(flops=flops, bytes_accessed=moved, transcendentals=0)


def read_slots(queries, keys, values, logs, new, docs, prev, key_in, value_in):
    rows, width = queries.shape
    slots = logs.shape[1]
    count = rows // CHUNK
    f32 = jnp.float32
    return pl.pallas_call(
        read_kernel,
        out_shape=(
            jax.ShapeDtypeStruct((rows, width), f32),
            jax.ShapeDtypeStruct((rows, slots), f32),
            jax.ShapeDtypeStruct((rows, slots), f32),
            jax.ShapeDtypeStruct((count + 1, slots, width), f32),
            jax.ShapeDtypeStruct((count + 1, slots, width), f32),
        ),
        scratch_shapes=[pltpu.VMEM((CHUNK, CHUNK, slots), f32)],
        compiler_params=pltpu.CompilerParams(vmem_limit_bytes=VMEM),
        cost_estimate=cost(READ_COST, 5 << 20),
    )(queries, keys, values, logs, new, docs, prev, key_in, value_in)


def back_query(queries, keys, values, logs, new, docs, prev, scores, probs, key_states, value_states, grads):
    rows, width = queries.shape
    slots = logs.shape[1]
    count = rows // CHUNK
    f32 = jnp.float32
    narrow = jax.ShapeDtypeStruct((rows, slots), f32)
    wide = jax.ShapeDtypeStruct((rows, width), f32)
    states = jax.ShapeDtypeStruct((count, slots, width), f32)
    state = jax.ShapeDtypeStruct((slots, width), f32)
    return (
        back_query_kernel,
        (queries, keys, values, logs, new, docs, prev, scores, probs, key_states, value_states, grads),
        (wide, wide, wide, narrow, narrow, states, states, state, state),
        (pltpu.VMEM((CHUNK, CHUNK, slots), f32),),
        (False,) * 12,
    )


def back_key(keys, values, logs, new, docs, prev, dk, dv, held, gained, xk, xv, dk_end, dv_end, total):
    rows, width = keys.shape
    slots = logs.shape[1]
    f32 = jnp.float32
    wide = jax.ShapeDtypeStruct((rows, width), jnp.bfloat16)
    return pl.pallas_call(
        back_key_kernel,
        out_shape=(wide, wide, jax.ShapeDtypeStruct((rows, slots), f32)),
        scratch_shapes=[
            pltpu.VMEM((slots, width), f32),
            pltpu.VMEM((slots, width), f32),
            pltpu.VMEM((1, slots), f32),
        ],
        compiler_params=pltpu.CompilerParams(vmem_limit_bytes=VMEM),
        cost_estimate=cost(READ_COST, 8 << 20),
    )(keys, values, logs, new, docs, prev, dk, dv, held, gained, xk, xv, dk_end, dv_end, total)


def other_of(place, by):
    return place + by * (1 - 2 * ((place // by) % 2))


def exchange_kernel(names, count, heads, reverse, work, early, after, *refs):
    refs = dict(zip(names, refs))
    wides = [n for n in names if n.startswith("wide_in")]
    narrows = [n for n in names if n.startswith("narrow_in")]
    place, head = lax.axis_index("seq"), lax.axis_index("head")
    partner, sibling = {"seq": other_of(place, 1)}, {"head": other_of(head, 1)}
    line = -1 if reverse else 1
    ahead = count - 1 - place if reverse else place
    left = count - 1 - ahead
    spans_of = [1 << k for k in range(count.bit_length() - 1)]
    hops = [1 << k for k in range(1, heads.bit_length() - 1)]

    relays = [n for n in names if n.startswith("relay_out")]
    relayed = bool(relays) or "ends_out" in refs
    beside = {"seq": other_of(place, 2)}
    at_end = (place // 2 == 0) | (place // 2 == 3)
    in_middle = jnp.logical_not(at_end)
    greeted = []
    if relayed:
        greeted.append((beside, None))
    if wides or narrows or early is not None:
        greeted.append((partner, None))
    if wides or relays or "part" in refs:
        greeted.append((sibling, None))
    if "part" in refs:
        greeted += [({"head": other_of(head, by)}, None) for by in hops]
    if "state" in refs:
        greeted += [({"seq": place + line * by}, left >= by) for by in spans_of]
        greeted += [({"seq": place - line * by}, ahead >= by) for by in spans_of]
    if work is not None:
        work(None, None, *[refs[n] for n in names if n.startswith("work")])
    barrier = pltpu.get_barrier_semaphore()
    total = 0
    for device, ok in greeted:
        if ok is None:
            pl.semaphore_signal(barrier, inc=1, device_id=device, device_id_type=MESH)
            total = total + 1
        else:

            @pl.when(ok)
            def _(device=device):
                pl.semaphore_signal(barrier, inc=1, device_id=device, device_id_type=MESH)

            total = total + ok.astype(jnp.int32)
    pl.semaphore_wait(barrier, total)

    def copy(source, target, sems, device):
        return pltpu.make_async_remote_copy(
            src_ref=source, dst_ref=target, send_sem=sems[0], recv_sem=sems[1],
            device_id=device, device_id_type=MESH,
        )

    def sems(name, i):
        return refs[name + "_send"].at[i], refs[name + "_recv"].at[i]

    def half_of(ref):
        size = ref.shape[0] // 2
        return ref.at[pl.ds((head % 2) * size, size)]

    def blocks_of(source, target, i):
        lines, rows, wide = target.shape
        if len(source.shape) == 3:
            return [copy(half_of(source), half_of(target), sems("wide", i * lines), partner)]
        copies = []
        for k in range(lines // 2):
            line = (head % 2) * (lines // 2) + k
            start = pl.multiple_of((2 * line + 1 - place % 2) * wide, 128)
            copies.append(
                copy(
                    source.at[:, pl.ds(start, wide)], target.at[line],
                    sems("wide", i * lines + k), partner,
                )
            )
        return copies

    waits, forwards, states = [], [], []
    fill = None
    if "state" in refs:
        inside, received, before = refs["inside"], refs["received"], refs["before"]
        inside[0] = refs["state"][...]
        states = [
            copy(inside.at[k], received.at[k], sems("state", k), {"seq": place + line * by})
            for k, by in enumerate(spans_of)
        ]

        @pl.when(left >= 1)
        def _():
            states[0].start()

    for i, name in enumerate(wides):
        name, source = name.replace("in", "out"), refs[name]
        moved = blocks_of(source, refs[name], i)
        for one in moved:
            one.start()
        forwards.append((name, moved))
    end_tiles, end_blocks = [], []
    for i, name in enumerate(relays):
        source, target = refs[f"relay_in{i}"], refs[name]
        lines, _, wide = target.shape
        for k in range(lines // 2):
            at = (head % 2) * (lines // 2) + k
            if len(source.shape) == 2:
                start = pl.multiple_of((2 * at + place % 2) * wide, 128)
                block = source.at[:, pl.ds(start, wide)]
            else:
                block = source.at[at]
            end_blocks.append(
                copy(block, target.at[at], sems("relay", i * (lines // 2) + k), beside)
            )

    @pl.when(at_end)
    def _():
        for moved in end_blocks:
            moved.start()

    if early is not None:
        source, target = refs["early_b0"], refs["narrow_out0"]

        def send_tile(i, columns):
            moved = copy(source.at[:, columns], target.at[:, columns], sems("narrow", i), partner)
            moved.start()
            waits.append(moved)
            if relayed:
                onward = copy(
                    refs["early_b1"].at[:, columns], refs["ends_out"].at[:, columns],
                    sems("ends", i), beside,
                )

                @pl.when(at_end)
                def _():
                    onward.start()

                end_tiles.append(onward)

        fill = early(send_tile, refs, [refs[n] for n in names if n.startswith("early")])
    tiles_sent, waits = waits, []
    if "part" in refs:
        part, added = refs["part"], refs["sum"]
        rows = part.shape[0] // CHUNKS
        half = rows // 2
        low = head % 2
        own, arrived = refs["own"], refs["arrived"]
        across = []

        def cross(c):
            waits[c].wait_recv()
            start = pl.multiple_of(c * rows + low * half, 8)
            own[0, c] = part[pl.ds(start, half), :] + refs["near"][c]
            moved = copy(
                own.at[0, c], arrived.at[0, c], sems("across", c), {"head": other_of(head, 2)}
            )
            moved.start()
            across.append(moved)

        for c in range(CHUNKS):
            if fill is not None:
                fill(c, rows)
            start = pl.multiple_of(c * rows + (1 - low) * half, 8)
            moved = copy(part.at[pl.ds(start, half)], refs["near"].at[c], sems("near", c), sibling)
            moved.start()
            waits.append(moved)
            if fill is not None:
                cross(c)
    for i, name in enumerate(narrows):
        moved = copy(refs[name], refs[name.replace("in", "out")], sems("narrow", i), partner)
        moved.start()
        waits.append(moved)

    def run_work(piece, pieces):
        if early is not None:
            outer_product_beside(piece, pieces, refs)
        if work is not None:
            work(piece, pieces, *[refs[n] for n in names if n.startswith("work")])

    if "part" in refs and fill is None:
        for c in range(CHUNKS):
            cross(c)
    if "state" not in refs:
        run_work(0, 1)
    if "state" in refs:
        lane = lax.broadcasted_iota(jnp.int32, before.shape, 1)
        before[...] = jnp.where(lane < 64, 1.0, jnp.where(lane < 128, -1.0, 0.0))

        def composed(earlier, later):
            keep = later[:, :1]
            if not reverse:
                keep = jnp.where(earlier[:, 64:65] == later[:, 64:65], keep, 0.0)
            values = keep * earlier + later
            return jnp.where(lane >= 128, values, jnp.where(lane < 64, earlier * later, later))

        for k, by in enumerate(spans_of):
            moved = states[k]
            if k:

                @pl.when(left >= by)
                def _(moved=moved):
                    moved.start()

            if k + 1 < len(spans_of):
                inside[k + 1] = inside[k]

            run_work(k, len(spans_of))

            @pl.when(ahead >= by)
            def _(k=k, moved=moved):
                moved.wait_recv()
                before[...] = composed(received[k], before[...]) if k else received[k]
                if k + 1 < len(spans_of):
                    inside[k + 1] = composed(received[k], inside[k])

            @pl.when(left >= by)
            def _(moved=moved):
                moved.wait_send()

    def pass_on():
        for i, (name, moved) in enumerate(forwards):
            for one in moved:
                one.wait()
            onward = copy(half_of(refs[name]), half_of(refs[name]), sems("onward", i), sibling)
            onward.start()
            waits.append(onward)

    early_pass = "part" in refs and "state" not in refs
    if early_pass:
        pass_on()
    if "part" in refs:
        for k in range(1, len(hops)):
            later = []
            for c in range(CHUNKS):
                across[c].wait()
                own[k, c] = own[k - 1, c] + arrived[k - 1, c]
                moved = copy(
                    own.at[k, c], arrived.at[k, c], sems("across", k * CHUNKS + c),
                    {"head": other_of(head, hops[k])},
                )
                moved.start()
                later.append(moved)
            across = later
        back = []
        k = len(hops) - 1

        def close(c):
            waits[c].wait_send()
            back[c].wait()
            if after is not None:
                after(c, rows, added, [refs[n] for n in names if n.startswith("after")])

        for c in range(CHUNKS):
            across[c].wait()
            start = pl.multiple_of(c * rows + low * half, 8)
            mine = pl.ds(start, half)
            added[mine, :] = own[k, c] + arrived[k, c]
            moved = copy(added.at[mine], added.at[mine], sems("back", c), sibling)
            moved.start()
            back.append(moved)
            if c:
                close(c - 1)
        close(CHUNKS - 1)
        waits = waits[CHUNKS:]
    if after is not None:
        after(None, rows, added, [refs[n] for n in names if n.startswith("after")])
    if not early_pass:
        pass_on()
    for moved in waits + tiles_sent:
        moved.wait()
    if relayed:

        @pl.when(at_end)
        def _():
            for moved in end_tiles + end_blocks:
                moved.wait_send()

        @pl.when(in_middle)
        def _():
            for moved in end_tiles + end_blocks:
                moved.wait_recv()
            passed = [
                copy(half_of(refs[name]), half_of(refs[name]), sems("passed", i), sibling)
                for i, name in enumerate(relays)
            ]
            for moved in passed:
                moved.start()
            for moved in passed:
                moved.wait()

    if early is not None:
        for one in refs["finish"][-1]:
            one.wait()


def exchange(
    number, part=None, state=None, reverse=False, wides=(), narrows=(), work=None, early=None, relay=(), after=None
):
    count, heads = lax.axis_size("seq"), lax.axis_size("head")
    f32 = jnp.float32
    vmem, hbm = pl.BlockSpec(memory_space=pltpu.VMEM), pl.BlockSpec(memory_space=pl.ANY)
    ins, outs, scratch = [], [], []
    buffers = ["part", "near", "own", "arrived", "inside", "received"]
    if part is not None:
        if early is None:
            ins.append(("part", part, vmem))
        else:
            scratch.append(("part", pltpu.VMEM(part.shape, f32)))
        outs.append(("sum", part, vmem))
        half = (CHUNKS, part.shape[0] // CHUNKS // 2, part.shape[1])
        steps = heads.bit_length() - 2
        scratch += [
            ("near", pltpu.VMEM(half, f32)),
            ("own", pltpu.VMEM((steps,) + half, f32)),
            ("arrived", pltpu.VMEM((steps,) + half, f32)),
        ]
        for name, size in (("near", CHUNKS), ("across", steps * CHUNKS), ("back", CHUNKS)):
            scratch += [(name + end, pltpu.SemaphoreType.DMA((size,))) for end in ("_send", "_recv")]
    if state is not None:
        ins.append(("state", state, vmem))
        outs.append(("before", state, vmem))
        steps = count.bit_length() - 1
        scratch += [(n, pltpu.VMEM((steps,) + state.shape, f32)) for n in ("inside", "received")]
        scratch += [("state" + end, pltpu.SemaphoreType.DMA((steps,))) for end in ("_send", "_recv")]
    lines = count // 2
    for kind, arrays, each in (("wide", wides, lines), ("narrow", narrows, 1)):
        for i, a in enumerate(arrays):
            shape = a.shape
            if kind == "wide" and len(shape) == 2:
                shape = (lines, shape[0], shape[1] // count)
            ins.append((f"{kind}_in{i}", a, hbm))
            outs.append((f"{kind}_out{i}", jax.ShapeDtypeStruct(shape, f32), hbm))
        for name, size in ((kind, each), ("onward", 1)) if kind == "wide" else ((kind, 1),):
            if arrays:
                scratch += [
                    (name + end, pltpu.SemaphoreType.DMA((len(arrays) * size,)))
                    for end in ("_send", "_recv")
                ]
    for i, a in enumerate(relay):
        ins.append((f"relay_in{i}", a, hbm))
        shape = a.shape if len(a.shape) == 3 else (lines, a.shape[0], a.shape[1] // count)
        outs.append((f"relay_out{i}", jax.ShapeDtypeStruct(shape, f32), hbm))
    if relay:
        for name, size in (("relay", len(relay) * shape[0] // 2), ("passed", len(relay))):
            scratch += [(name + end, pltpu.SemaphoreType.DMA((size,))) for end in ("_send", "_recv")]
    if early is not None:
        early, given, sent_shape, tiles, made, extra = early
        ins += [(f"early_in{i}", a, hbm) for i, a in enumerate(given)]
        outs.append(("narrow_out0", jax.ShapeDtypeStruct(sent_shape, f32), hbm))
        if lines == 4:
            outs.append(("ends_out", jax.ShapeDtypeStruct(sent_shape, f32), hbm))
            scratch += [("ends" + end, pltpu.SemaphoreType.DMA((tiles,))) for end in ("_send", "_recv")]
        outs += [(f"early_out{i}", a, hbm) for i, a in enumerate(made)]
        scratch += [(f"early_b{i}", a) for i, a in enumerate(extra)]
        buffers += [f"early_b{i}" for i in range(len(extra) - 3)]
        scratch += [("narrow" + end, pltpu.SemaphoreType.DMA((tiles,))) for end in ("_send", "_recv")]
    if after is not None:
        after, given, made, extra = after
        ins += [(f"after_in{i}", a, vmem) for i, a in enumerate(given)]
        outs += [(f"after_out{i}", a, hbm) for i, a in enumerate(made)]
        scratch += [(f"after_b{i}", a) for i, a in enumerate(extra)]
        buffers += [f"after_b{i}" for i in range(len(extra) - 1)]
    if work is not None:
        work, given, made, extra, places = work
        beside = work is not back_query_kernel
        ins += [(f"work_in{i}", a, hbm if p else vmem) for i, (a, p) in enumerate(zip(given, places))]
        outs += [(f"work_out{i}", a, vmem) for i, a in enumerate(made)]
        scratch += [(f"work_b{i}", a) for i, a in enumerate(extra)]
        buffers += [f"work_b{i}" for i in range(len(extra) - beside)]
    names = [n for n, *_ in ins] + [n for n, *_ in outs] + [n for n, _ in scratch]
    held = [a for _, a, spec in ins + outs if spec is vmem]
    held += [jax.ShapeDtypeStruct(a.shape, a.dtype) for n, a in scratch if n in buffers]
    return pl.pallas_call(
        functools.partial(exchange_kernel, names, count, heads, reverse, work, early, after),
        out_shape=tuple(jax.ShapeDtypeStruct(a.shape, a.dtype) for _, a, _ in outs),
        in_specs=[spec for *_, spec in ins],
        out_specs=tuple(spec for *_, spec in outs),
        scratch_shapes=[s for _, s in scratch],
        compiler_params=pltpu.CompilerParams(
            collective_id=number, has_side_effects=True, vmem_limit_bytes=EXCHANGE_VMEM
        ),
        cost_estimate=cost(40 << 30, 16 << 20),
    )(*[a for _, a, _ in ins])


def scatter_kernel(count, in_ref, out_ref, slots, send, receive):
    place = lax.axis_index("seq")
    others = [{"seq": lax.rem(place + k, count)} for k in range(1, count)]
    barrier = pltpu.get_barrier_semaphore()
    for device in others:
        pl.semaphore_signal(barrier, inc=1, device_id=device, device_id_type=MESH)
    pl.semaphore_wait(barrier, count - 1)
    copies = []
    for k, device in enumerate(others):
        moved = pltpu.make_async_remote_copy(
            src_ref=in_ref.at[device["seq"]], dst_ref=slots.at[place],
            send_sem=send.at[k], recv_sem=receive.at[k], device_id=device, device_id_type=MESH,
        )
        moved.start()
        copies.append(moved)
    slots[place] = in_ref[place]
    for moved in copies:
        moved.wait()
    total = slots[0]
    for i in range(1, count):
        total = total + slots[i]
    out_ref[...] = total


def scatter_sum(number, array):
    count = array.shape[0]
    vmem = pl.BlockSpec(memory_space=pltpu.VMEM)
    return pl.pallas_call(
        functools.partial(scatter_kernel, count),
        out_shape=jax.ShapeDtypeStruct(array.shape[1:], jnp.float32),
        in_specs=[vmem],
        out_specs=vmem,
        scratch_shapes=[
            pltpu.VMEM(array.shape, jnp.float32),
            pltpu.SemaphoreType.DMA((count - 1,)),
            pltpu.SemaphoreType.DMA((count - 1,)),
        ],
        compiler_params=pltpu.CompilerParams(
            collective_id=number, has_side_effects=True, vmem_limit_bytes=VMEM
        ),
        cost_estimate=cost(4 << 30, 1 << 20),
    )(array)


def state_of(keep, doc, keys, values):
    keep = jnp.broadcast_to(keep[:, None], (keep.shape[0], 64))
    return jnp.concatenate([keep, jnp.full_like(keep, doc), keys, values], axis=1)


def head_parts(size, count):
    whole = [(at, 256) for at in range(0, size, 256)]
    last = whole[:-1] + [(size - 256, 128), (size - 128, 128)]
    sides = [0, count - 1, *range(1, count - 1)]
    return [(i, *tile) for i in sides for tile in (last if i == sides[-1] else whole)]


def final_kernel(tiles, head_count, *refs):
    act_in, near_in, dy_own, dy_their, dy_near, dy_far, in_own, in_their, branch_own, branch_their = refs[:10]
    sides = refs[10 : 10 + 2 * head_count]
    part, outs = refs[10 + 2 * head_count], refs[11 + 2 * head_count : 11 + 3 * head_count]
    (out_down, added, far, across, wide_in, wide_branch, heads, stage, stage_head,
     act, their_act, near_act, far_act, wide_dy, head_tile, to_middle, from_middle, near, own_sum, arrived,
     own_sems, head_sems, stage_sems, act_sems, *sems) = refs[11 + 3 * head_count :]
    place = lax.axis_index("seq")
    line = place // 2
    at_end = (line == 0) | (line == 3)
    in_middle = jnp.logical_not(at_end)
    partner, beside = {"seq": other_of(place, 1)}, {"seq": other_of(place, 2)}
    opposite = {"seq": place + jnp.where(line == 1, 2, -2)}
    rows = act.shape[0]
    wide = out_down.shape[0]
    head = heads.shape[1] // head_count
    parts = head_parts(head, head_count)
    columns = [pl.ds(i * head + begin, size) for i, begin, size in parts]
    down = [pl.ds(*tile) for tile in tiles]
    out = [outs[i].at[:, pl.ds(begin, size)] for i, begin, size in parts]

    number = lax.axis_index("head")
    sibling, over_y = {"head": other_of(number, 1)}, {"head": other_of(number, 2)}
    barrier = pltpu.get_barrier_semaphore()
    for device in (beside, partner, sibling, over_y):
        pl.semaphore_signal(barrier, inc=1, device_id=device, device_id_type=MESH)

    @pl.when(in_middle)
    def _():
        pl.semaphore_signal(barrier, inc=1, device_id=opposite, device_id_type=MESH)

    roles = [jnp.where(line < 2, a, b) for a, b in ((2, 1), (3, 0), (1, 2), (0, 3))]
    starts = [pl.multiple_of((2 * role + place % 2) * wide, 128) for role in roles]

    def load(source, target, sem):
        copied = pltpu.make_async_copy(source, target, sem)
        copied.start()
        return copied

    in_loads, branch_loads, dy_loads = (
        [
            pltpu.make_async_copy(
                source.at[:, pl.ds(start, wide)],
                target.at[pl.ds(0, rows), pl.ds(r * wide, wide)],
                own_sems.at[k, r],
            )
            for r, start in enumerate(starts)
        ]
        for k, (source, target) in enumerate(
            ((in_own, wide_in), (branch_own, wide_branch), (dy_own, wide_dy))
        )
    )
    for one in in_loads:
        one.start()
    head_loads = [
        load(sides[2 * i], heads.at[pl.ds(0, rows), pl.ds(i * head, head)], head_sems.at[0, i])
        for i in range(head_count)
    ]
    ready = (0, head_count - 1)
    head_loads += [load(sides[2 * i + 1], stage_head.at[i], head_sems.at[1, i]) for i in ready]
    act_loads = [
        pltpu.make_async_copy(act_in, act, act_sems.at[0]),
        pltpu.make_async_copy(near_in, near_act, act_sems.at[1]),
    ]
    jobs = [(in_their, wide_in, 1), (branch_their, wide_branch, 1)]
    jobs += [(dy_their, wide_dy, 1), (dy_near, wide_dy, 2), (dy_far, wide_dy, 3)]

    def staged(k):
        return [
            load(jobs[k][0].at[role], stage.at[k % 2, r], stage_sems.at[k % 2, r])
            for r, role in enumerate(roles)
        ]

    under_way = {0: staged(0)}
    for one in branch_loads:
        one.start()
    under_way[1] = staged(1)
    for one in dy_loads + act_loads:
        one.start()

    def settle(k):
        for one in under_way[k]:
            one.wait()
        _, target, group = jobs[k]
        for r in range(4):
            target[group * rows : (group + 1) * rows, r * wide : (r + 1) * wide] = stage[
                k % 2, r
            ].astype(jnp.bfloat16)

    pl.semaphore_wait(barrier, 4 + in_middle.astype(jnp.int32))

    def remote(source, target, kind, i, device):
        return pltpu.make_async_remote_copy(
            src_ref=source, dst_ref=target, send_sem=sems[2 * kind].at[i],
            recv_sem=sems[2 * kind + 1].at[i], device_id=device, device_id_type=MESH,
        )

    chunk = part.shape[0] // CHUNKS
    half = chunk // 2
    low = number % 2
    mine_of = [pl.ds(pl.multiple_of(c * chunk + low * half, 8), half) for c in range(CHUNKS)]
    other_half = [pl.ds(pl.multiple_of(c * chunk + (1 - low) * half, 8), half) for c in range(CHUNKS)]
    nears = [remote(part.at[h], near.at[c], 8, c, sibling) for c, h in enumerate(other_half)]
    sums = [remote(own_sum.at[c], arrived.at[c], 9, c, over_y) for c in range(CHUNKS)]
    backs = [remote(added.at[h], added.at[h], 10, c, sibling) for c, h in enumerate(mine_of)]
    head_trades = [
        remote(sides[2 * i + 1], stage_head.at[i], 7, i - 1, partner)
        for i in range(1, head_count - 1)
    ]
    second = pl.ds(wide, wide)
    to_side = [remote(far.at[:, c], far.at[:, c], 0, i, beside) for i, c in enumerate(columns)]
    over = [
        remote(far.at[pl.ds(0, 2 * wide), c], across.at[:, c], 1, i, opposite) for i, c in enumerate(columns)
    ]
    home = [remote(across.at[second, c], out[i], 2, i, beside) for i, c in enumerate(columns)]
    trades = [remote(act_in.at[:, c], their_act.at[:, c], 3, i, partner) for i, c in enumerate(down)]
    passes = [remote(near_in.at[:, c], far_act.at[:, c], 4, i, partner) for i, c in enumerate(down)]
    over_down = [
        remote(to_middle.at[:, c], from_middle.at[:, c], 5, i, opposite) for i, c in enumerate(down)
    ]
    home_down = [
        remote(from_middle.at[second, c], out_down.at[:, c], 6, i, beside) for i, c in enumerate(down)
    ]

    down_at = {min(2 * j, len(columns) - len(down) + j - 2): j for j in range(len(down))}
    order = range(len(parts))

    def wide_of(i):
        return wide_branch if parts[i][0] == head_count - 1 else wide_in

    for one in nears:
        one.start()

    @pl.when(in_middle)
    def _():
        trades[0].start()
        passes[0].start()

    for one in in_loads + head_loads:
        one.wait()
    settle(0)

    def receive(i):
        if 0 < i < head_count - 1:
            head_trades[i - 1].wait_recv()
        heads[rows:, i * head : (i + 1) * head] = stage_head[i].astype(jnp.bfloat16)

    receive(0)

    def to_middle_tile(i):
        far[:, columns[i]] = tn(wide_of(i)[:, : 3 * wide], heads[:, columns[i]])
        to_side[i].start()

    first = [i for i in range(len(parts)) if parts[i][0] == 0]

    @pl.when(at_end)
    def _():
        for i in first:
            to_middle_tile(i)

    settle(1)
    receive(head_count - 1)

    @pl.when(at_end)
    def _():
        for one in head_trades:
            one.start()

    @pl.when(in_middle)
    def _():
        under_way[2], under_way[3] = staged(2), staged(3)
        settle(2)
        under_way[4] = staged(4)
        settle(3)
        settle(4)
        for i, (trade, onward) in enumerate(zip(trades, passes)):
            if i:
                trade.start()
                onward.start()
            if i < len(head_trades):
                head_trades[i].start()

    for c in range(CHUNKS):
        nears[c].wait_recv()
        own_sum[c] = part[mine_of[c], :] + near[c]
        sums[c].start()

    def settle_down():
        for one in dy_loads + act_loads:
            one.wait()

    for one in branch_loads:
        one.wait()

    @pl.when(at_end)
    def _():
        for k, i in enumerate(order):
            if parts[i][0] not in ready and parts[i][1] == 0:
                receive(parts[i][0])
            if i not in first:
                to_middle_tile(i)
        settle_down()

    @pl.when(at_end)
    def _():
        for k, i in enumerate(order):
            c = columns[i]
            mine = tn(wide_of(i)[:, 3 * wide :], heads[:, c])
            home[i].wait_recv()
            out[i][...] = out[i][...] + mine
            if k in down_at:
                home_down[down_at[k]].wait_recv()
        for one in to_side:
            one.wait_send()

    @pl.when(in_middle)
    def _():
        def finish(i):
            c = columns[i]
            mine = tn(wide_of(i)[:, 3 * wide :], heads[:, c])
            over[i].wait_recv()
            across[wide:, c] = across[wide:, c] + mine
            home[i].start()
            out[i][...] = far[2 * wide :, c] + across[:wide, c]

        settle_down()
        for k, i in enumerate(order):
            c = columns[i]
            if parts[i][0] not in ready and parts[i][1] == 0:
                receive(parts[i][0])
            j = down_at.get(k)
            if j is not None:
                d = down[j]
                size = tiles[j][1]
                tile = head_tile.at[:, pl.ds(0, size)]
                trades[j].wait_recv()
                passes[j].wait_recv()
                for g, side in enumerate((act, their_act, near_act, far_act)):
                    tile[g * rows : (g + 1) * rows, :] = side[:, d].astype(jnp.bfloat16)
                to_middle[:, d] = tn(wide_dy[:, : 2 * wide], tile[...])
                over_down[j].start()
                out_down[:, d] = tn(wide_dy[:, 2 * wide : 3 * wide], tile[...])
                home_part = tn(wide_dy[:, 3 * wide :], tile[...])
            mine = tn(wide_of(i)[:, : 3 * wide], heads[:, c])
            to_side[i].wait_recv()
            far[:, c] = far[:, c] + mine
            over[i].start()
            if j is not None:
                over_down[j].wait_recv()
                from_middle[wide:, d] = from_middle[wide:, d] + home_part
                home_down[j].start()
                out_down[:, d] = out_down[:, d] + from_middle[:wide, d]
            if k:
                finish(order[k - 1])
        finish(order[-1])
        for one in over + home + trades + passes + over_down + home_down:
            one.wait_send()

    for c in range(CHUNKS):
        sums[c].wait()
        added[mine_of[c], :] = own_sum[c] + arrived[c]
        backs[c].start()
    for one in head_trades + nears:
        one.wait_send()
    for one in backs:
        one.wait()


def final_gradients(number, part, act, near_act, dy, wide_in, wide_branch, heads):
    rows, hidden = act.shape
    wide = dy[1].shape[2]
    head = heads[0][0].shape[1]
    count = len(heads)
    total = head * count
    tiles = column_tiles(hidden)
    f32, bf16 = jnp.float32, jnp.bfloat16
    dma = pltpu.SemaphoreType.DMA
    hbm, vmem = pl.BlockSpec(memory_space=pl.ANY), pl.BlockSpec(memory_space=pltpu.VMEM)
    whole = pltpu.VMEM((rows, hidden), f32)
    sides = [a for pair in heads for a in pair]
    half = (CHUNKS, rows // CHUNKS // 2, part.shape[1])
    return pl.pallas_call(
        functools.partial(final_kernel, tiles, count),
        out_shape=(
            *[jax.ShapeDtypeStruct((wide, head), f32)] * count,
            jax.ShapeDtypeStruct((wide, hidden), f32),
            jax.ShapeDtypeStruct(part.shape, f32),
        ),
        in_specs=[hbm] * (10 + len(sides)) + [vmem],
        out_specs=(vmem,) * (count + 2),
        scratch_shapes=[
            pltpu.VMEM((3 * wide, total), f32),
            pltpu.VMEM((2 * wide, total), f32),
            pltpu.VMEM((2 * rows, 4 * wide), bf16),
            pltpu.VMEM((2 * rows, 4 * wide), bf16),
            pltpu.VMEM((2 * rows, total), bf16),
            pltpu.VMEM((2, 4, rows, wide), f32),
            pltpu.VMEM((count, rows, head), f32),
            whole, whole, whole, whole,
            pltpu.VMEM((4 * rows, 4 * wide), bf16),
            pltpu.VMEM((4 * rows, 256), bf16),
            pltpu.VMEM((2 * wide, hidden), f32),
            pltpu.VMEM((2 * wide, hidden), f32),
            pltpu.VMEM(half, f32), pltpu.VMEM(half, f32), pltpu.VMEM(half, f32),
            dma((3, 4)), dma((2, count)), dma((2, 4)), dma((2,)),
        ]
        + [dma((len(head_parts(head, count)),))] * 6
        + [dma((len(tiles),))] * 8
        + [dma((count - 2,))] * 2
        + [dma((CHUNKS,))] * 6,
        compiler_params=pltpu.CompilerParams(
            collective_id=number, has_side_effects=True, vmem_limit_bytes=FINAL_VMEM
        ),
        cost_estimate=cost(200 << 30, 16 << 20),
    )(act, near_act, *dy, *wide_in, *wide_branch, *sides, part)


def normed_after(c, rows, added, own):
    stream, gain, normed_out, float_out, normed, normed_f, sems = own

    def copies(c):
        mine = pl.ds(c * rows, rows)
        return [
            pltpu.make_async_copy(normed.at[mine], normed_out.at[mine], sems.at[0, c]),
            pltpu.make_async_copy(normed_f.at[mine], float_out.at[mine], sems.at[1, c]),
        ]

    if c is None:
        for i in range(CHUNKS):
            for one in copies(i):
                one.wait()
        return
    mine = pl.ds(c * rows, rows)
    hidden = stream[mine, :].astype(jnp.float32) + added[mine, :]
    added[mine, :] = hidden
    rounded = (hidden * rms_scale(hidden) * gain[...]).astype(jnp.bfloat16)
    normed[mine, :] = rounded
    normed_f[mine, :] = rounded.astype(jnp.float32)
    for one in copies(c):
        one.start()


def norm_after(stream, gain):
    half, full = (jax.ShapeDtypeStruct(stream.shape, t) for t in (jnp.bfloat16, jnp.float32))
    return (
        normed_after,
        (stream, gain.reshape(1, -1)),
        (half, full),
        (
            pltpu.VMEM(stream.shape, jnp.bfloat16),
            pltpu.VMEM(stream.shape, jnp.float32),
            pltpu.SemaphoreType.DMA((2, CHUNKS)),
        ),
    )


def matmul_work(product, column, count, piece, pieces, left_ref, *refs):
    rights, outs, left = refs[:count], refs[count : 2 * count], refs[2 * count]
    sides, sems = refs[2 * count + 1 : -1], refs[-1]
    copies = [pltpu.make_async_copy(left_ref, left, sems.at[0])]
    copies += [pltpu.make_async_copy(a, b, sems.at[1 + i]) for i, (a, b) in enumerate(zip(rights, sides))]
    if piece is None:
        for one in copies:
            one.start()
        return
    if piece == 0:
        for one in copies:
            one.wait()
    for right, out in zip(sides, outs):

        def tile(i, carry):
            columns = pl.ds(pl.multiple_of(i * column, column), column)
            side = right[columns, :] if product is nt else right[:, columns]
            out[:, columns] = product(left[...], side)
            return carry

        tiles = out.shape[1] // column
        lax.fori_loop(tiles * piece // pieces, tiles * (piece + 1) // pieces, tile, 0)


def column_tiles(size):
    wide = 256 if size >= 256 else size
    return [(at, min(wide, size - at)) for at in range(0, size, wide)]


def hidden_units(send_tile, refs, own):
    (normed_in, gate_in, up_in, down_in, d_act_in, act_f_out, d_gate_out, d_up_out, up_f_out, ffn_out,
     gate_f, act_f, act_ref, d_gate_ref, d_up_ref, up_f_ref, ffn_ref, normed, w_gate, w_up, w_down, d_act, sems, tile_sems, out_sems) = own
    whole = [
        pltpu.make_async_copy(normed_in, normed, sems.at[0]),
        pltpu.make_async_copy(d_act_in, d_act, sems.at[1]),
        pltpu.make_async_copy(down_in, w_down, sems.at[2]),
    ]
    parts = []
    tiles = column_tiles(act_ref.shape[1])
    for i, (at, size) in enumerate(tiles):
        columns = pl.ds(at, size)
        parts.append(
            [
                pltpu.make_async_copy(gate_in.at[:, columns], w_gate.at[:, columns], tile_sems.at[0, i]),
                pltpu.make_async_copy(up_in.at[:, columns], w_up.at[:, columns], tile_sems.at[1, i]),
            ]
        )
    whole[0].start()
    for one in parts[0]:
        one.start()
    whole[1].start()
    for pair in parts[1:]:
        for one in pair:
            one.start()
    whole[2].start()
    whole[0].wait()
    for i, (at, size) in enumerate(tiles):
        columns = pl.ds(at, size)
        for one in parts[i]:
            one.wait()
        gate = nn(normed[...], w_gate[:, columns])
        up = nn(normed[...], w_up[:, columns])
        if i == 0:
            whole[1].wait()
        sig = jax.nn.sigmoid(gate)
        silu = gate * sig
        pull = d_act[:, columns]
        act = (silu * up).astype(jnp.bfloat16)
        act_ref[:, columns] = act
        act_f[:, columns] = act.astype(jnp.float32)
        d_gate = (pull * up * sig * (1.0 + gate * (1.0 - sig))).astype(jnp.bfloat16)
        d_up = (pull * silu).astype(jnp.bfloat16)
        d_gate_ref[:, columns] = d_gate
        d_up_ref[:, columns] = d_up
        gate_f[:, columns] = d_gate.astype(jnp.float32)
        send_tile(i, columns)
        up_f_ref[:, columns] = d_up.astype(jnp.float32)

    kept = [(act_f, act_f_out), (d_gate_ref, d_gate_out), (d_up_ref, d_up_out),
            (up_f_ref, up_f_out), (ffn_ref, ffn_out)]
    kept = [pltpu.make_async_copy(a, b, out_sems.at[i]) for i, (a, b) in enumerate(kept)]
    for one in kept[:-1]:
        one.start()
    part = refs["part"]

    def fill(c, rows):
        mine = pl.ds(c * rows, rows)

        def tile(i, carry):
            columns = pl.ds(pl.multiple_of(i * 256, 256), 256)
            part[mine, columns] = nt(d_gate_ref[mine, :], w_gate[columns, :]) + nt(
                d_up_ref[mine, :], w_up[columns, :]
            )
            return carry

        lax.fori_loop(0, part.shape[1] // 256, tile, 0)

    refs["finish"] = (whole[2], act_ref, w_down, ffn_ref, kept)
    return fill


def outer_product_beside(piece, pieces, refs):
    copied, act, w_down, out, kept = refs["finish"]
    copied.wait()

    def tile(i, carry):
        columns = pl.ds(pl.multiple_of(i * 256, 256), 256)
        out[:, columns] = nn(act[...], w_down[:, columns])
        return carry

    lax.fori_loop(0, out.shape[1] // 256, tile, 0)
    kept[-1].start()


def hidden_units_early(normed_mid, w_gate, w_up, w_down, d_act):
    rows, width = normed_mid.shape
    hidden = w_gate.shape[1]
    tiles = len(column_tiles(hidden))
    half = jax.ShapeDtypeStruct((rows, hidden), jnp.bfloat16)
    full = jax.ShapeDtypeStruct((rows, hidden), jnp.float32)
    return (
        hidden_units,
        (normed_mid, w_gate, w_up, w_down, d_act),
        (rows, hidden),
        tiles,
        (full, half, half, full, jax.ShapeDtypeStruct((rows, width), jnp.float32)),
        (
            pltpu.VMEM((rows, hidden), jnp.float32),
            pltpu.VMEM((rows, hidden), jnp.float32),
            pltpu.VMEM((rows, hidden), jnp.bfloat16),
            pltpu.VMEM((rows, hidden), jnp.bfloat16),
            pltpu.VMEM((rows, hidden), jnp.bfloat16),
            pltpu.VMEM((rows, hidden), jnp.float32),
            pltpu.VMEM((rows, width), jnp.float32),
            pltpu.VMEM(normed_mid.shape, jnp.bfloat16),
            pltpu.VMEM(w_gate.shape, jnp.bfloat16),
            pltpu.VMEM(w_up.shape, jnp.bfloat16),
            pltpu.VMEM(w_down.shape, jnp.bfloat16),
            pltpu.VMEM(d_act.shape, jnp.float32),
            pltpu.SemaphoreType.DMA((3,)),
            pltpu.SemaphoreType.DMA((2, tiles)),
            pltpu.SemaphoreType.DMA((5,)),
        ),
    )


def matmul_beside(product, left, *rights):
    columns = rights[0].shape[0] if product is nt else rights[0].shape[1]
    column = 256 if columns % 256 == 0 else 128
    return (
        functools.partial(matmul_work, product, column, len(rights)),
        (left, *rights),
        (jax.ShapeDtypeStruct((left.shape[0], columns), jnp.float32),) * len(rights),
        (
            pltpu.VMEM(left.shape, left.dtype),
            *[pltpu.VMEM(right.shape, right.dtype) for right in rights],
            pltpu.SemaphoreType.DMA((1 + len(rights),)),
        ),
        (True,) * (1 + len(rights)),
    )


def body(
    stream,
    seg_ids,
    attn_gain,
    w_query,
    w_key,
    w_value,
    w_outgate,
    w_low,
    w_slot,
    forget_bias,
    head_gain,
    w_out,
    mlp_gain,
    w_gate,
    w_up,
    w_down,
    cotangent,
):
    tok_rows = stream.shape[0]
    width = stream.shape[1]
    slots = w_slot.shape[2]
    head_width = w_query.shape[1]
    stream_f = stream.astype(jnp.float32)
    scale_in = rms_scale(stream_f)
    normed_in = (stream_f * scale_in * attn_gain).astype(jnp.bfloat16)
    key_rows = plain_dot(normed_in, w_key).astype(jnp.bfloat16)
    value_rows = plain_dot(normed_in, w_value).astype(jnp.bfloat16)
    ranked = plain_dot(normed_in, w_low)

    def decay_logs(ranked_in, slot_map, bias_row):
        return jax.nn.log_sigmoid(precise_dot(ranked_in, slot_map[0]) + bias_row[0]) / GATE_NORM

    log_decay, gate_pull = jax.vjp(decay_logs, ranked, w_slot, forget_bias)

    new = -jnp.expm1(log_decay)
    last_doc = seg_ids[tok_rows - 1]
    running = precise_dot(jnp.tril(jnp.ones((tok_rows, tok_rows), jnp.float32)), log_decay)
    total = running[tok_rows - 1]
    in_last = (seg_ids == last_doc)[:, None]
    factor = jnp.where(in_last, jnp.exp(jnp.where(in_last, total - running, 0.0)) * new, 0.0)
    def wide_float(array):
        return array.astype(jnp.float32)

    local_key = precise_left_t(factor, key_rows.astype(jnp.float32))
    local_value = precise_left_t(factor, value_rows.astype(jnp.float32))
    docs = seg_ids.astype(jnp.float32)
    own_state = state_of(jnp.exp(total), docs[tok_rows - 1], local_key, local_value)
    dy_f = cotangent.astype(jnp.float32)
    prefix, query_rows, gate_act = exchange(
        0,
        state=own_state,
        work=matmul_beside(nn, normed_in, w_query, w_outgate),
    )
    query_rows = query_rows.astype(jnp.bfloat16)
    key_in, value_in = prefix[:, 128 : 128 + head_width], prefix[:, 128 + head_width :]
    prior = prefix[0, 64]
    decay_all = jnp.where(docs[tok_rows - 1] == prior, jnp.exp(total), 0.0)
    before = jnp.concatenate([prior[None], docs[CHUNK - 1 : -1 : CHUNK]])
    docs = jnp.broadcast_to(docs[:, None], (tok_rows, slots))
    before = jnp.broadcast_to(jnp.repeat(before, CHUNK)[:, None], (tok_rows, slots))
    slot_read, scores, probs, key_states, value_states = read_slots(
        query_rows, key_rows, value_rows, log_decay, new, docs, before, key_in, value_in
    )
    scale_read = rms_scale(slot_read)
    normed_read = slot_read * scale_read * head_gain[0]
    gate_sig = jax.nn.sigmoid(gate_act)
    gate_silu = gate_act * gate_sig
    mixed_heads = (normed_read * gate_silu).astype(jnp.bfloat16)
    four = lax.axis_size("seq") == 8
    hidden, from_dy, *near_dy, normed_mid, normed_mid_f, d_act = exchange(
        1,
        part=plain_dot(mixed_heads, w_out),
        wides=(wide_to_send(cotangent),),
        relay=(dy_f,) if four else (),
        work=matmul_beside(nt, cotangent, w_down),
        after=norm_after(stream, mlp_gain),
    )
    wide_dy = cotangent, from_dy
    scale_mid = rms_scale(hidden)
    upstream = cotangent.astype(jnp.float32)
    d_mid, from_mid, *made = exchange(
        2,
        part=jax.ShapeDtypeStruct((tok_rows, width), jnp.float32),
        wides=(wide_to_send(normed_mid_f),),
        relay=(from_dy,) if four else (),
        early=hidden_units_early(normed_mid, w_gate, w_up, w_down, d_act),
    )
    if four:
        far_dy, from_gate, end_act, *made = made
    else:
        from_gate, *made = made
    act_f, d_gate, d_up, d_up_f, ffn_part = made
    wide_mid = normed_mid, from_mid
    grad_gate = pair_products((wide_mid, [(d_gate, from_gate)]))
    d_mid, grad_gate = together(d_mid, grad_gate)
    grad_gate = line_sum(grad_gate)
    grad_mlp_gain = jnp.sum(d_mid * hidden * scale_mid, axis=0)
    scaled_mid = d_mid * mlp_gain
    d_hidden = (
        upstream
        + scale_mid * scaled_mid
        - hidden * scale_mid**3 * jnp.mean(scaled_mid * hidden, axis=1, keepdims=True)
    )
    d_branch = d_hidden.astype(jnp.bfloat16)
    d_mixed = dot_right_t(d_branch, w_out)
    d_gate_act = (d_mixed * normed_read * gate_sig * (1.0 + gate_act * (1.0 - gate_sig))).astype(
        jnp.bfloat16
    )
    d_normed = d_mixed * gate_silu
    grad_head_gain = jnp.sum(d_normed * slot_read * scale_read, axis=0)[None, :]
    scaled_read = d_normed * head_gain[0]
    d_read = scale_read * scaled_read - slot_read * scale_read**3 * jnp.mean(
        scaled_read * slot_read, axis=1, keepdims=True
    )
    normed_f, ffn_part = together(wide_to_send(normed_in), ffn_part)
    ffn_out, from_in, from_up, *back = exchange(
        3,
        part=ffn_part,
        wides=(normed_f,),
        narrows=(d_up_f,),
        work=back_query(
            query_rows, key_rows, value_rows, log_decay, new, docs, before, scores, probs, key_states, value_states, d_read
        ),
    )
    wide_in = normed_in, from_in
    grad_up = pair_products((wide_mid, [(d_up, from_up)]))
    d_query, d_key, d_value, held, gained, to_keys, to_values, key_back, value_back = back
    query_back = d_query.astype(jnp.bfloat16)
    result = hidden + ffn_out
    squares = jnp.stack(
        [jnp.sum(stream_f * stream_f), jnp.sum(hidden * hidden), jnp.sum(result * result)]
    )
    key_back, grad_up, grad_gate, grad_mlp_gain, grad_head_gain, squares = together(
        key_back, grad_up, grad_gate, grad_mlp_gain, grad_head_gain, squares
    )
    grad_up = line_sum(grad_up)
    suffix, from_branch, from_outgate, from_mixed = exchange(
        4,
        state=state_of(decay_all, 0.0, key_back, value_back),
        reverse=True,
        wides=(wide_to_send(d_branch),),
        narrows=(wide_float(d_gate_act), wide_float(mixed_heads)),
    )
    key_end, value_end = suffix[:, 128 : 128 + head_width], suffix[:, 128 + head_width :]
    end_total = jnp.sum(key_states[-1] * key_end + value_states[-1] * value_end, axis=1)[None, :]
    key_back, value_back, d_logs = back_key(
        key_rows, value_rows, log_decay, new, docs, before, d_key, d_value, held, gained,
        to_keys, to_values, key_end, value_end, end_total,
    )
    d_ranked, grad_slot, grad_bias = gate_pull(d_logs)
    normed_f = normed_in.astype(jnp.float32)
    grad_low = precise_left_t(normed_f, d_ranked)
    d_in_part = (
        dot_right_t(query_back, w_query)
        + dot_right_t(key_back, w_key)
        + dot_right_t(value_back, w_value)
        + dot_right_t(d_gate_act, w_outgate)
        + precise_right_t(d_ranked, w_low.astype(jnp.float32))
    )
    late = [wide_float(a) for a in (query_back, key_back, value_back)]
    wide_branch = d_branch, from_branch
    if four:
        sides = [(d_gate_act, from_outgate), *zip((query_back, key_back, value_back), late), (mixed_heads, from_mixed)]
        act_f, grad_up = together(act_f, grad_up)
        *grad_rest, grad_down, d_in = final_gradients(
            5, d_in_part, act_f, end_act, (cotangent, from_dy, *near_dy, far_dy), wide_in, wide_branch, sides
        )
    else:
        d_in, *late = exchange(5, part=d_in_part, narrows=late)
        head_sides = [(d_gate_act, from_outgate), *zip((query_back, key_back, value_back), late), (mixed_heads, from_mixed)]
        grad_rest = pair_products((wide_in, head_sides[:4]), (wide_branch, head_sides[4:]))
        grad_rest = line_sum(grad_rest)
        (from_act,) = exchange(6, narrows=(act_f,))
        grad_down = pair_products((wide_dy, [(act_f.astype(jnp.bfloat16), from_act)]))
        grad_down = line_sum(grad_down)
        grad_rest = jnp.split(grad_rest, 5, axis=1)
    grad_outgate, grad_query, grad_key, grad_value, grad_out = grad_rest
    grad_attn_gain = jnp.sum(d_in * stream_f * scale_in, axis=0)
    scaled_in = d_in * attn_gain
    grad_stream = (
        d_hidden
        + scale_in * scaled_in
        - stream_f * scale_in**3 * jnp.mean(scaled_in * stream_f, axis=1, keepdims=True)
    ).astype(jnp.bfloat16)
    count = lax.axis_size("seq")
    small = [
        grad_attn_gain.reshape(count, -1),
        grad_mlp_gain.reshape(count, -1),
        grad_low.reshape(count, -1),
        jnp.moveaxis(grad_slot[0].reshape(-1, count, slots // count), 1, 0).reshape(count, -1),
        grad_bias.reshape(count, -1),
        grad_head_gain.reshape(count, -1),
        jnp.broadcast_to(squares, (count, 3)),
    ]
    sizes = [a.shape[1] for a in small]
    packed = jnp.concatenate(small, axis=1)
    packed = jnp.pad(packed, ((0, 0), (0, -packed.shape[1] % 1024)))
    packed = scatter_sum(7, packed.reshape(count, -1, 128)).reshape(-1)
    ends = [sum(sizes[: i + 1]) for i in range(len(sizes))]
    small = [packed[end - size : end] for end, size in zip(ends, sizes)]
    stream_rms = jnp.sqrt(small[6] / (tok_rows * count * width))
    summed = (
        small[0],
        grad_query,
        grad_key,
        grad_value,
        grad_outgate,
        small[2].reshape(width // count, -1),
        small[3].reshape(1, -1, slots // count),
        small[4][None, :],
        small[5][None, :],
        grad_out.T,
        small[1],
        grad_gate,
        grad_up,
        grad_down.T,
    )
    mixer_parts = summed[:10]
    ffn_parts = summed[10:]
    return (
        result.astype(jnp.bfloat16),
        grad_stream,
        mixer_parts[0],
        mixer_parts[1],
        mixer_parts[2],
        mixer_parts[3],
        mixer_parts[4],
        mixer_parts[5],
        mixer_parts[6],
        mixer_parts[7],
        mixer_parts[8],
        mixer_parts[9],
        ffn_parts[0],
        ffn_parts[1],
        ffn_parts[2],
        ffn_parts[3],
        stream_rms,
    )


def solution(mesh):
    in_specs = (
        P("seq", None),
        P("seq"),
        P(),
        P(None, "head"),
        P(None, "head"),
        P(None, "head"),
        P(None, "head"),
        P(None, "head"),
        P("head", None, None),
        P("head", None),
        P("head", None),
        P("head", None),
        P(),
        P(None, "head"),
        P(None, "head"),
        P("head", None),
        P("seq", None),
    )
    out_specs = (
        P("seq", None),
        P("seq", None),
        P("seq"),
        P("seq", "head"),
        P("seq", "head"),
        P("seq", "head"),
        P("seq", "head"),
        P("seq", "head"),
        P("head", None, "seq"),
        P("head", "seq"),
        P("head", "seq"),
        P("head", "seq"),
        P("seq"),
        P("seq", "head"),
        P("seq", "head"),
        P("head", "seq"),
        P(),
    )
    return jax.shard_map(body, mesh=mesh, in_specs=in_specs, out_specs=out_specs, check_vma=False)
```

```python
import functools
import math

import jax
import jax.numpy as jnp
from jax import lax
from jax.experimental import pallas as pl
from jax.experimental.pallas import tpu as pltpu
from jax.sharding import PartitionSpec as P

CHUNK = 64
CHUNKS = 4
MESH = pl.DeviceIdType.MESH
VMEM = 24 << 20
MORE = 10 << 20
EXCHANGE_VMEM = 50 << 20
FINAL_VMEM = 60 << 20
READ_COST = 17 << 30


EPSILON = 1e-06
GATE_NORM = 8.0
PRECISE = lax.Precision.HIGHEST


def width_blocks(array, parity):
    count = lax.axis_size("seq")
    wide = array.shape[1] // count
    return jnp.stack(
        [
            lax.dynamic_slice_in_dim(array, (2 * line + parity) * wide, wide, 1)
            for line in range(count // 2)
        ]
    )


def whole_tiles(array):
    return array.shape[1] // lax.axis_size("seq") % 128 == 0


def wide_to_send(array):
    array = array.astype(jnp.float32)
    if whole_tiles(array):
        return array
    return width_blocks(array, 1 - lax.axis_index("seq") % 2)


def product_kernel(layout, *refs):
    out_ref, sides = refs[-2:]
    refs = list(refs[1:-2])
    first = pl.program_id(0) == 0
    at = 0
    for narrows in layout:
        own, theirs = refs.pop(0), refs.pop(0)
        block = jnp.concatenate(
            [own[...].reshape(own.shape[-2:]), theirs[0].astype(jnp.bfloat16)], axis=0
        )
        for _ in range(narrows):
            own_narrow, their_narrow = refs.pop(0), refs.pop(0)
            rows, size = own_narrow.shape

            @pl.when(first)
            def _(at=at, own_narrow=own_narrow, their_narrow=their_narrow, rows=rows, size=size):
                sides[:rows, at : at + size] = own_narrow[...]
                sides[rows:, at : at + size] = their_narrow[...].astype(jnp.bfloat16)

            out_ref[0, :, at : at + size] = tn(block, sides[:, at : at + size])
            at += size


def pair_products(*jobs):
    count = lax.axis_size("seq")
    lines = count // 2
    parity = lax.axis_index("seq") % 2
    ins, specs, total = [], [], 0
    for (own, theirs), narrows in jobs:
        rows, wide = own.shape[0], own.shape[1] // count
        if whole_tiles(own):
            ins.append(own)
            specs.append(pl.BlockSpec((rows, wide), lambda i, p: (0, 2 * i + p[0])))
        else:
            ins.append(width_blocks(own, parity))
            specs.append(pl.BlockSpec((1, rows, wide), lambda i, p: (i, 0, 0)))
        ins.append(theirs)
        specs.append(pl.BlockSpec((1, rows, wide), lambda i, p: (i, 0, 0)))
        for pair in narrows:
            for side in pair:
                ins.append(side)
                specs.append(pl.BlockSpec(side.shape, lambda i, p: (0, 0)))
            total += pair[0].shape[1]
    return pl.pallas_call(
        functools.partial(product_kernel, [len(narrows) for _, narrows in jobs]),
        out_shape=jax.ShapeDtypeStruct((lines, wide, total), jnp.float32),
        grid_spec=pltpu.PrefetchScalarGridSpec(
            num_scalar_prefetch=1,
            grid=(lines,),
            in_specs=specs,
            out_specs=pl.BlockSpec((1, wide, total), lambda i, p: (i, 0, 0)),
            scratch_shapes=[pltpu.VMEM((2 * rows, total), jnp.bfloat16)],
        ),
        compiler_params=pltpu.CompilerParams(vmem_limit_bytes=VMEM),
        cost_estimate=cost(4 * rows * wide * lines * total, 8 * wide * lines * total),
    )(parity.reshape(1).astype(jnp.int32), *ins)


def line_sum(product):
    lines = product.shape[0]
    groups = [[line * 2 + x for line in range(lines)] for x in range(2)]
    return lax.psum_scatter(
        product, "seq", scatter_dimension=0, axis_index_groups=groups, tiled=True
    )[0]


def together(*arrays):
    return lax.optimization_barrier(arrays)


def precise_dot(left, right):
    return jnp.dot(left, right, precision=PRECISE, preferred_element_type=jnp.float32)


def plain_dot(left, right):
    return jnp.dot(left, right, preferred_element_type=jnp.float32)


def dot_right_t(left, right):
    return lax.dot_general(
        left, right, (((1,), (1,)), ((), ())), preferred_element_type=jnp.float32
    )


def dot_left_t(left, right):
    return lax.dot_general(
        left, right, (((0,), (0,)), ((), ())), preferred_element_type=jnp.float32
    )


def precise_left_t(left, right):
    return lax.dot_general(
        left, right, (((0,), (0,)), ((), ())), precision=PRECISE, preferred_element_type=jnp.float32
    )


def precise_right_t(left, right):
    return lax.dot_general(
        left, right, (((1,), (1,)), ((), ())), precision=PRECISE, preferred_element_type=jnp.float32
    )


def rms_scale(value):
    return lax.rsqrt(jnp.mean(value * value, axis=-1, keepdims=True) + EPSILON)


def split(value):
    high = value.astype(jnp.bfloat16)
    return high, (value - high.astype(jnp.float32)).astype(jnp.bfloat16)


def nn(left, right):
    return jnp.dot(left, right, preferred_element_type=jnp.float32)


def nt(left, right):
    return lax.dot_general(
        left, right, (((1,), (1,)), ((), ())), preferred_element_type=jnp.float32
    )


def tn(left, right):
    return lax.dot_general(
        left, right, (((0,), (0,)), ((), ())), preferred_element_type=jnp.float32
    )


def two(product, left, right):
    high, low = split(right)
    return product(left, high) + product(left, low)


def three(product, left, right):
    left_high, left_low = split(left)
    right_high, right_low = split(right)
    return product(left_high, right_high) + (
        product(left_low, right_high) + product(left_high, right_low)
    )


def row_blocks(value):
    return [value[r : r + 8] for r in range(0, value.shape[0], 8)]


def exact_dot(left, right):
    return jnp.dot(left, right, precision=PRECISE, preferred_element_type=jnp.float32)


def triangle(size, upper):
    row = lax.broadcasted_iota(jnp.int32, (size, size), 0)
    column = lax.broadcasted_iota(jnp.int32, (size, size), 1)
    keep = row <= column if upper else row >= column
    return jnp.where(keep, 1.0, 0.0)


def spans(running, docs, span_s):
    size = running.shape[0]
    run, doc = row_blocks(running), row_blocks(docs)
    place = lax.broadcasted_iota(jnp.int32, (8, running.shape[1]), 0)
    for j in range(size):
        for r in range(j // 8, size // 8):
            ok = doc[r] == docs[j : j + 1]
            if r == j // 8 and j % 8:
                ok = ok & (place >= j % 8)
            span_s[j, 8 * r : 8 * r + 8] = jnp.where(ok, jnp.exp(run[r] - running[j : j + 1]), 0.0)


def doc_before(doc_ref, first_ref, i, size):
    row = doc_ref[pl.ds(jnp.maximum(i * size - 1, 0), 1), :]
    return jnp.where(i == 0, first_ref[...], row)


def to_end(running, docs):
    last = running.shape[0] - 1
    return jnp.where(
        docs == docs[last : last + 1], jnp.exp(running[last : last + 1] - running), 0.0
    )


def turned(to_end_weights, kept):
    size, slots = to_end_weights.shape
    fill = jnp.broadcast_to(kept, (128 - size, slots))
    both = jnp.concatenate([to_end_weights, fill], axis=0).T
    return both[:, :size], both[:, size : size + 1]


def read_kernel(
    q_ref, k_ref, v_ref, log_ref, new_ref, doc_ref, prev_ref, kin_ref, vin_ref,
    read_ref, score_ref, prob_ref, ks_ref, vs_ref, span_s,
):
    size = span_s.shape[0]
    lower = triangle(size, False)
    scaling = q_ref.shape[1] ** (-0.5)
    ks_ref[0] = kin_ref[...]
    vs_ref[0] = vin_ref[...]
    lane = lax.broadcasted_iota(jnp.int32, (8, size), 1)

    def chunk(i, carry):
        rows = pl.ds(pl.multiple_of(i * size, size), size)
        queries, keys, values = q_ref[rows, :], k_ref[rows, :], v_ref[rows, :]
        new, docs = new_ref[rows, :], doc_ref[rows, :]
        running = exact_dot(lower, log_ref[rows, :])
        carried = jnp.where(docs == doc_before(doc_ref, prev_ref, i, size), jnp.exp(running), 0.0)
        key_state, value_state = ks_ref[i], vs_ref[i]
        spans(running, docs, span_s)
        affinity = row_blocks(nt(queries, keys))
        scores = row_blocks(carried * two(nt, queries, key_state))
        for j in range(size):
            for r in range(j // 8, size // 8):
                weight = span_s[j, 8 * r : 8 * r + 8] * new[j : j + 1]
                scores[r] = scores[r] + weight * affinity[r][:, j : j + 1]
        scores = scaling * jnp.concatenate(scores, axis=0)
        probs = jnp.exp(scores - jnp.max(scores, axis=1, keepdims=True))
        probs = probs / jnp.sum(probs, axis=1, keepdims=True)
        score_ref[rows, :] = scores
        prob_ref[rows, :] = probs
        used = probs.astype(jnp.bfloat16).astype(jnp.float32)
        part = row_blocks(used)
        mixing = [jnp.zeros((8, size), jnp.float32) for _ in part]
        for j in range(size):
            for r in range(j // 8, size // 8):
                weight = span_s[j, 8 * r : 8 * r + 8] * new[j : j + 1]
                total = jnp.sum(part[r] * weight, axis=1, keepdims=True)
                mixing[r] = jnp.where(lane == j, total, mixing[r])
        high, low = split(jnp.concatenate(mixing, axis=0))
        read_ref[rows, :] = (
            three(nn, used * carried, value_state) + nn(high, values) + nn(low, values)
        )
        end, kept = turned(to_end(running, docs) * new, carried[size - 1 : size])
        high, low = split(end)
        ks_ref[i + 1] = kept * key_state + (nn(high, keys) + nn(low, keys))
        vs_ref[i + 1] = kept * value_state + (nn(high, values) + nn(low, values))
        return carry

    lax.fori_loop(0, q_ref.shape[0] // size, chunk, 0)


def back_query_kernel(
    piece, pieces, q_ref, k_ref, v_ref, log_ref, new_ref, doc_ref, prev_ref, score_ref, prob_ref, ks_ref, vs_ref, g_ref,
    dq_ref, dk_ref, dv_ref, held_ref, gained_ref, xk_ref, xv_ref, dkin_ref, dvin_ref, span_s,
):
    if piece is None:
        return
    size = span_s.shape[0]
    count = q_ref.shape[0] // size
    lower = triangle(size, False)
    scaling = q_ref.shape[1] ** (-0.5)
    dkin_ref[...] = jnp.zeros_like(dkin_ref)
    dvin_ref[...] = jnp.zeros_like(dvin_ref)
    lane = lax.broadcasted_iota(jnp.int32, (8, size), 1)

    def chunk(turn, carry):
        i = count - 1 - turn
        start = pl.multiple_of(i * size, size)
        rows = pl.ds(start, size)
        queries, keys, values, grads = q_ref[rows, :], k_ref[rows, :], v_ref[rows, :], g_ref[rows, :]
        new, docs = new_ref[rows, :], doc_ref[rows, :]
        running = exact_dot(lower, log_ref[rows, :])
        carried = jnp.where(docs == doc_before(doc_ref, prev_ref, i, size), jnp.exp(running), 0.0)
        spans(running, docs, span_s)
        affinity = row_blocks(nt(queries, keys))
        grad_high, grad_low = split(grads)
        pull = row_blocks(nt(grad_high, values) + nt(grad_low, values))
        back = row_blocks(carried * three(nt, grads, vs_ref[i]))
        for j in range(size):
            for r in range(j // 8, size // 8):
                weight = span_s[j, 8 * r : 8 * r + 8] * new[j : j + 1]
                back[r] = back[r] + weight * pull[r][:, j : j + 1]
        back = jnp.concatenate(back, axis=0)
        probs = prob_ref[rows, :]
        used = probs.astype(jnp.bfloat16).astype(jnp.float32)
        inner = probs * (back - jnp.sum(probs * back, axis=1, keepdims=True))
        gained_ref[rows, :] = inner * score_ref[rows, :] + used * back
        outer = scaling * inner
        part, used_part = row_blocks(outer), row_blocks(used)
        key_mix = [jnp.zeros((8, size), jnp.float32) for _ in part]
        value_mix = [jnp.zeros((8, size), jnp.float32) for _ in part]
        for j in range(size):
            held = None
            for r in range(j // 8, size // 8):
                span = span_s[j, 8 * r : 8 * r + 8]
                key_side, value_side = part[r] * span, used_part[r] * span
                own = key_side * affinity[r][:, j : j + 1] + value_side * pull[r][:, j : j + 1]
                held = own if held is None else held + own
                fresh = new[j : j + 1]
                key_mix[r] = jnp.where(
                    lane == j, jnp.sum(key_side * fresh, axis=1, keepdims=True), key_mix[r]
                )
                value_mix[r] = jnp.where(
                    lane == j, jnp.sum(value_side * fresh, axis=1, keepdims=True), value_mix[r]
                )
            held_ref[pl.ds(start + j, 1), :] = jnp.sum(held, axis=0, keepdims=True)
        key_mix = jnp.concatenate(key_mix, axis=0)
        value_mix = jnp.concatenate(value_mix, axis=0)
        outer_in, used_in = outer * carried, used * carried
        high, low = split(key_mix)
        dq_ref[rows, :] = three(nn, outer_in, ks_ref[i]) + (nn(high, keys) + nn(low, keys))
        fill = jnp.zeros((128 - size, size), jnp.float32)
        high, low = split(jnp.concatenate([key_mix, fill], axis=0).T[:, :size])
        dk_ref[rows, :] = nn(high, queries) + nn(low, queries)
        mixed = jnp.concatenate([value_mix, fill], axis=0).T[:, :size]
        dv_ref[rows, :] = three(nn, mixed, grads)
        outer_t, kept = turned(outer_in, carried[size - 1 : size])
        used_t, kept = turned(used_in, carried[size - 1 : size])
        high, low = split(outer_t)
        to_key = nn(high, queries) + nn(low, queries)
        to_value = three(nn, used_t, grads)
        xk_ref[i] = to_key
        xv_ref[i] = to_value
        dkin_ref[...] = kept * dkin_ref[...] + to_key
        dvin_ref[...] = kept * dvin_ref[...] + to_value
        return carry

    lax.fori_loop(0, count, chunk, 0)


def back_key_kernel(
    k_ref, v_ref, log_ref, new_ref, doc_ref, prev_ref, dk_in_ref, dv_in_ref, held_ref, gained_ref,
    xk_ref, xv_ref, dkend_ref, dvend_ref, total_ref,
    dk_ref, dv_ref, dlog_ref, ks, vs, total,
):
    size = CHUNK
    count = k_ref.shape[0] // size
    lower, upper = triangle(size, False), triangle(size, True)
    ks[...] = dkend_ref[...]
    vs[...] = dvend_ref[...]
    total[...] = total_ref[...]

    def chunk(turn, carry):
        i = count - 1 - turn
        rows = pl.ds(pl.multiple_of(i * size, size), size)
        keys, values = k_ref[rows, :], v_ref[rows, :]
        logs, new, docs = log_ref[rows, :], new_ref[rows, :], doc_ref[rows, :]
        running = exact_dot(lower, logs)
        carried = jnp.where(docs == doc_before(doc_ref, prev_ref, i, size), jnp.exp(running), 0.0)
        end = to_end(running, docs)
        weight = end * new
        dk_ref[rows, :] = (dk_in_ref[rows, :] + three(nn, weight, ks[...])).astype(dk_ref.dtype)
        dv_ref[rows, :] = (dv_in_ref[rows, :] + three(nn, weight, vs[...])).astype(dv_ref.dtype)
        held = held_ref[rows, :] + end * (two(nt, keys, ks[...]) + two(nt, values, vs[...]))
        change = gained_ref[rows, :] - new * held
        after = exact_dot(upper, change) + total[...]
        dlog_ref[rows, :] = after - jnp.exp(logs) * held
        total[...] = after[:1]
        unused, kept = turned(carried, carried[size - 1 : size])
        ks[...] = kept * ks[...] + xk_ref[i]
        vs[...] = kept * vs[...] + xv_ref[i]
        return carry

    lax.fori_loop(0, count, chunk, 0)


def room(arrays):
    total = 0
    for a in arrays:
        shape = a.shape[:-1] + (-(-a.shape[-1] // 128) * 128,)
        total += math.prod(shape) * jnp.dtype(a.dtype).itemsize
    return total + MORE


def cost(flops, moved):
    return pl.CostEstimate(flops=flops, bytes_accessed=moved, transcendentals=0)


def read_slots(queries, keys, values, logs, new, docs, prev, key_in, value_in):
    rows, width = queries.shape
    slots = logs.shape[1]
    count = rows // CHUNK
    f32 = jnp.float32
    return pl.pallas_call(
        read_kernel,
        out_shape=(
            jax.ShapeDtypeStruct((rows, width), f32),
            jax.ShapeDtypeStruct((rows, slots), f32),
            jax.ShapeDtypeStruct((rows, slots), f32),
            jax.ShapeDtypeStruct((count + 1, slots, width), f32),
            jax.ShapeDtypeStruct((count + 1, slots, width), f32),
        ),
        scratch_shapes=[pltpu.VMEM((CHUNK, CHUNK, slots), f32)],
        compiler_params=pltpu.CompilerParams(vmem_limit_bytes=VMEM),
        cost_estimate=cost(READ_COST, 5 << 20),
    )(queries, keys, values, logs, new, docs, prev, key_in, value_in)


def back_query(queries, keys, values, logs, new, docs, prev, scores, probs, key_states, value_states, grads):
    rows, width = queries.shape
    slots = logs.shape[1]
    count = rows // CHUNK
    f32 = jnp.float32
    narrow = jax.ShapeDtypeStruct((rows, slots), f32)
    wide = jax.ShapeDtypeStruct((rows, width), f32)
    states = jax.ShapeDtypeStruct((count, slots, width), f32)
    state = jax.ShapeDtypeStruct((slots, width), f32)
    return (
        back_query_kernel,
        (queries, keys, values, logs, new, docs, prev, scores, probs, key_states, value_states, grads),
        (wide, wide, wide, narrow, narrow, states, states, state, state),
        (pltpu.VMEM((CHUNK, CHUNK, slots), f32),),
        (False,) * 12,
    )


def back_key(keys, values, logs, new, docs, prev, dk, dv, held, gained, xk, xv, dk_end, dv_end, total):
    rows, width = keys.shape
    slots = logs.shape[1]
    f32 = jnp.float32
    wide = jax.ShapeDtypeStruct((rows, width), jnp.bfloat16)
    return pl.pallas_call(
        back_key_kernel,
        out_shape=(wide, wide, jax.ShapeDtypeStruct((rows, slots), f32)),
        scratch_shapes=[
            pltpu.VMEM((slots, width), f32),
            pltpu.VMEM((slots, width), f32),
            pltpu.VMEM((1, slots), f32),
        ],
        compiler_params=pltpu.CompilerParams(vmem_limit_bytes=VMEM),
        cost_estimate=cost(READ_COST, 8 << 20),
    )(keys, values, logs, new, docs, prev, dk, dv, held, gained, xk, xv, dk_end, dv_end, total)


def other_of(place, by):
    return place + by * (1 - 2 * ((place // by) % 2))


def exchange_kernel(names, count, heads, reverse, work, early, after, *refs):
    refs = dict(zip(names, refs))
    wides = [n for n in names if n.startswith("wide_in")]
    narrows = [n for n in names if n.startswith("narrow_in")]
    place, head = lax.axis_index("seq"), lax.axis_index("head")
    partner, sibling = {"seq": other_of(place, 1)}, {"head": other_of(head, 1)}
    line = -1 if reverse else 1
    ahead = count - 1 - place if reverse else place
    left = count - 1 - ahead
    spans_of = [1 << k for k in range(count.bit_length() - 1)]
    hops = [1 << k for k in range(1, heads.bit_length() - 1)]

    relays = [n for n in names if n.startswith("relay_out")]
    relayed = bool(relays) or "ends_out" in refs
    beside = {"seq": other_of(place, 2)}
    at_end = (place // 2 == 0) | (place // 2 == 3)
    in_middle = jnp.logical_not(at_end)
    greeted = []
    if relayed:
        greeted.append((beside, None))
    if wides or narrows or early is not None:
        greeted.append((partner, None))
    if wides or relays or "part" in refs:
        greeted.append((sibling, None))
    if "part" in refs:
        greeted += [({"head": other_of(head, by)}, None) for by in hops]
    if "state" in refs:
        greeted += [({"seq": place + line * by}, left >= by) for by in spans_of]
        greeted += [({"seq": place - line * by}, ahead >= by) for by in spans_of]
    if work is not None:
        work(None, None, *[refs[n] for n in names if n.startswith("work")])
    barrier = pltpu.get_barrier_semaphore()
    total = 0
    for device, ok in greeted:
        if ok is None:
            pl.semaphore_signal(barrier, inc=1, device_id=device, device_id_type=MESH)
            total = total + 1
        else:

            @pl.when(ok)
            def _(device=device):
                pl.semaphore_signal(barrier, inc=1, device_id=device, device_id_type=MESH)

            total = total + ok.astype(jnp.int32)
    pl.semaphore_wait(barrier, total)

    def copy(source, target, sems, device):
        return pltpu.make_async_remote_copy(
            src_ref=source, dst_ref=target, send_sem=sems[0], recv_sem=sems[1],
            device_id=device, device_id_type=MESH,
        )

    def sems(name, i):
        return refs[name + "_send"].at[i], refs[name + "_recv"].at[i]

    def half_of(ref):
        size = ref.shape[0] // 2
        return ref.at[pl.ds((head % 2) * size, size)]

    def blocks_of(source, target, i):
        lines, rows, wide = target.shape
        if len(source.shape) == 3:
            return [copy(half_of(source), half_of(target), sems("wide", i * lines), partner)]
        copies = []
        for k in range(lines // 2):
            line = (head % 2) * (lines // 2) + k
            start = pl.multiple_of((2 * line + 1 - place % 2) * wide, 128)
            copies.append(
                copy(
                    source.at[:, pl.ds(start, wide)], target.at[line],
                    sems("wide", i * lines + k), partner,
                )
            )
        return copies

    waits, forwards, states = [], [], []
    fill = None
    if "state" in refs:
        inside, received, before = refs["inside"], refs["received"], refs["before"]
        inside[0] = refs["state"][...]
        states = [
            copy(inside.at[k], received.at[k], sems("state", k), {"seq": place + line * by})
            for k, by in enumerate(spans_of)
        ]

        @pl.when(left >= 1)
        def _():
            states[0].start()

    for i, name in enumerate(wides):
        name, source = name.replace("in", "out"), refs[name]
        moved = blocks_of(source, refs[name], i)
        for one in moved:
            one.start()
        forwards.append((name, moved))
    end_tiles, end_blocks = [], []
    for i, name in enumerate(relays):
        source, target = refs[f"relay_in{i}"], refs[name]
        lines, _, wide = target.shape
        for k in range(lines // 2):
            at = (head % 2) * (lines // 2) + k
            if len(source.shape) == 2:
                start = pl.multiple_of((2 * at + place % 2) * wide, 128)
                block = source.at[:, pl.ds(start, wide)]
            else:
                block = source.at[at]
            end_blocks.append(
                copy(block, target.at[at], sems("relay", i * (lines // 2) + k), beside)
            )

    @pl.when(at_end)
    def _():
        for moved in end_blocks:
            moved.start()

    if early is not None:
        source, target = refs["early_b0"], refs["narrow_out0"]

        def send_tile(i, columns):
            moved = copy(source.at[:, columns], target.at[:, columns], sems("narrow", i), partner)
            moved.start()
            waits.append(moved)
            if relayed:
                onward = copy(
                    refs["early_b1"].at[:, columns], refs["ends_out"].at[:, columns],
                    sems("ends", i), beside,
                )

                @pl.when(at_end)
                def _():
                    onward.start()

                end_tiles.append(onward)

        fill = early(send_tile, refs, [refs[n] for n in names if n.startswith("early")])
    tiles_sent, waits = waits, []
    if "part" in refs:
        part, added = refs["part"], refs["sum"]
        rows = part.shape[0] // CHUNKS
        half = rows // 2
        low = head % 2
        own, arrived = refs["own"], refs["arrived"]
        across = []

        def cross(c):
            waits[c].wait_recv()
            start = pl.multiple_of(c * rows + low * half, 8)
            own[0, c] = part[pl.ds(start, half), :] + refs["near"][c]
            moved = copy(
                own.at[0, c], arrived.at[0, c], sems("across", c), {"head": other_of(head, 2)}
            )
            moved.start()
            across.append(moved)

        for c in range(CHUNKS):
            if fill is not None:
                fill(c, rows)
            start = pl.multiple_of(c * rows + (1 - low) * half, 8)
            moved = copy(part.at[pl.ds(start, half)], refs["near"].at[c], sems("near", c), sibling)
            moved.start()
            waits.append(moved)
            if fill is not None:
                cross(c)
    for i, name in enumerate(narrows):
        moved = copy(refs[name], refs[name.replace("in", "out")], sems("narrow", i), partner)
        moved.start()
        waits.append(moved)

    def run_work(piece, pieces):
        if early is not None:
            outer_product_beside(piece, pieces, refs)
        if work is not None:
            work(piece, pieces, *[refs[n] for n in names if n.startswith("work")])

    if "part" in refs and fill is None:
        for c in range(CHUNKS):
            cross(c)
    if "state" not in refs:
        run_work(0, 1)
    if "state" in refs:
        lane = lax.broadcasted_iota(jnp.int32, before.shape, 1)
        before[...] = jnp.where(lane < 64, 1.0, jnp.where(lane < 128, -1.0, 0.0))

        def composed(earlier, later):
            keep = later[:, :1]
            if not reverse:
                keep = jnp.where(earlier[:, 64:65] == later[:, 64:65], keep, 0.0)
            values = keep * earlier + later
            return jnp.where(lane >= 128, values, jnp.where(lane < 64, earlier * later, later))

        for k, by in enumerate(spans_of):
            moved = states[k]
            if k:

                @pl.when(left >= by)
                def _(moved=moved):
                    moved.start()

            if k + 1 < len(spans_of):
                inside[k + 1] = inside[k]

            run_work(k, len(spans_of))

            @pl.when(ahead >= by)
            def _(k=k, moved=moved):
                moved.wait_recv()
                before[...] = composed(received[k], before[...]) if k else received[k]
                if k + 1 < len(spans_of):
                    inside[k + 1] = composed(received[k], inside[k])

            @pl.when(left >= by)
            def _(moved=moved):
                moved.wait_send()

    def pass_on():
        for i, (name, moved) in enumerate(forwards):
            for one in moved:
                one.wait()
            onward = copy(half_of(refs[name]), half_of(refs[name]), sems("onward", i), sibling)
            onward.start()
            waits.append(onward)

    early_pass = "part" in refs and "state" not in refs
    if early_pass:
        pass_on()
    if "part" in refs:
        for k in range(1, len(hops)):
            later = []
            for c in range(CHUNKS):
                across[c].wait()
                own[k, c] = own[k - 1, c] + arrived[k - 1, c]
                moved = copy(
                    own.at[k, c], arrived.at[k, c], sems("across", k * CHUNKS + c),
                    {"head": other_of(head, hops[k])},
                )
                moved.start()
                later.append(moved)
            across = later
        back = []
        k = len(hops) - 1

        def close(c):
            waits[c].wait_send()
            back[c].wait()
            if after is not None:
                after(c, rows, added, [refs[n] for n in names if n.startswith("after")])

        for c in range(CHUNKS):
            across[c].wait()
            start = pl.multiple_of(c * rows + low * half, 8)
            mine = pl.ds(start, half)
            added[mine, :] = own[k, c] + arrived[k, c]
            moved = copy(added.at[mine], added.at[mine], sems("back", c), sibling)
            moved.start()
            back.append(moved)
            if c:
                close(c - 1)
        close(CHUNKS - 1)
        waits = waits[CHUNKS:]
    if after is not None:
        after(None, rows, added, [refs[n] for n in names if n.startswith("after")])
    if not early_pass:
        pass_on()
    for moved in waits + tiles_sent:
        moved.wait()
    if relayed:

        @pl.when(at_end)
        def _():
            for moved in end_tiles + end_blocks:
                moved.wait_send()

        @pl.when(in_middle)
        def _():
            for moved in end_tiles + end_blocks:
                moved.wait_recv()
            passed = [
                copy(half_of(refs[name]), half_of(refs[name]), sems("passed", i), sibling)
                for i, name in enumerate(relays)
            ]
            for moved in passed:
                moved.start()
            for moved in passed:
                moved.wait()

    if early is not None:
        for one in refs["finish"][-1]:
            one.wait()


def exchange(
    number, part=None, state=None, reverse=False, wides=(), narrows=(), work=None, early=None, relay=(), after=None
):
    count, heads = lax.axis_size("seq"), lax.axis_size("head")
    f32 = jnp.float32
    vmem, hbm = pl.BlockSpec(memory_space=pltpu.VMEM), pl.BlockSpec(memory_space=pl.ANY)
    ins, outs, scratch = [], [], []
    buffers = ["part", "near", "own", "arrived", "inside", "received"]
    if part is not None:
        if early is None:
            ins.append(("part", part, vmem))
        else:
            scratch.append(("part", pltpu.VMEM(part.shape, f32)))
        outs.append(("sum", part, vmem))
        half = (CHUNKS, part.shape[0] // CHUNKS // 2, part.shape[1])
        steps = heads.bit_length() - 2
        scratch += [
            ("near", pltpu.VMEM(half, f32)),
            ("own", pltpu.VMEM((steps,) + half, f32)),
            ("arrived", pltpu.VMEM((steps,) + half, f32)),
        ]
        for name, size in (("near", CHUNKS), ("across", steps * CHUNKS), ("back", CHUNKS)):
            scratch += [(name + end, pltpu.SemaphoreType.DMA((size,))) for end in ("_send", "_recv")]
    if state is not None:
        ins.append(("state", state, vmem))
        outs.append(("before", state, vmem))
        steps = count.bit_length() - 1
        scratch += [(n, pltpu.VMEM((steps,) + state.shape, f32)) for n in ("inside", "received")]
        scratch += [("state" + end, pltpu.SemaphoreType.DMA((steps,))) for end in ("_send", "_recv")]
    lines = count // 2
    for kind, arrays, each in (("wide", wides, lines), ("narrow", narrows, 1)):
        for i, a in enumerate(arrays):
            shape = a.shape
            if kind == "wide" and len(shape) == 2:
                shape = (lines, shape[0], shape[1] // count)
            ins.append((f"{kind}_in{i}", a, hbm))
            outs.append((f"{kind}_out{i}", jax.ShapeDtypeStruct(shape, f32), hbm))
        for name, size in ((kind, each), ("onward", 1)) if kind == "wide" else ((kind, 1),):
            if arrays:
                scratch += [
                    (name + end, pltpu.SemaphoreType.DMA((len(arrays) * size,)))
                    for end in ("_send", "_recv")
                ]
    for i, a in enumerate(relay):
        ins.append((f"relay_in{i}", a, hbm))
        shape = a.shape if len(a.shape) == 3 else (lines, a.shape[0], a.shape[1] // count)
        outs.append((f"relay_out{i}", jax.ShapeDtypeStruct(shape, f32), hbm))
    if relay:
        for name, size in (("relay", len(relay) * shape[0] // 2), ("passed", len(relay))):
            scratch += [(name + end, pltpu.SemaphoreType.DMA((size,))) for end in ("_send", "_recv")]
    if early is not None:
        early, given, sent_shape, tiles, made, extra = early
        ins += [(f"early_in{i}", a, hbm) for i, a in enumerate(given)]
        outs.append(("narrow_out0", jax.ShapeDtypeStruct(sent_shape, f32), hbm))
        if lines == 4:
            outs.append(("ends_out", jax.ShapeDtypeStruct(sent_shape, f32), hbm))
            scratch += [("ends" + end, pltpu.SemaphoreType.DMA((tiles,))) for end in ("_send", "_recv")]
        outs += [(f"early_out{i}", a, hbm) for i, a in enumerate(made)]
        scratch += [(f"early_b{i}", a) for i, a in enumerate(extra)]
        buffers += [f"early_b{i}" for i in range(len(extra) - 3)]
        scratch += [("narrow" + end, pltpu.SemaphoreType.DMA((tiles,))) for end in ("_send", "_recv")]
    if after is not None:
        after, given, made, extra = after
        ins += [(f"after_in{i}", a, vmem) for i, a in enumerate(given)]
        outs += [(f"after_out{i}", a, hbm) for i, a in enumerate(made)]
        scratch += [(f"after_b{i}", a) for i, a in enumerate(extra)]
        buffers += [f"after_b{i}" for i in range(len(extra) - 1)]
    if work is not None:
        work, given, made, extra, places = work
        beside = work is not back_query_kernel
        ins += [(f"work_in{i}", a, hbm if p else vmem) for i, (a, p) in enumerate(zip(given, places))]
        outs += [(f"work_out{i}", a, vmem) for i, a in enumerate(made)]
        scratch += [(f"work_b{i}", a) for i, a in enumerate(extra)]
        buffers += [f"work_b{i}" for i in range(len(extra) - beside)]
    names = [n for n, *_ in ins] + [n for n, *_ in outs] + [n for n, _ in scratch]
    held = [a for _, a, spec in ins + outs if spec is vmem]
    held += [jax.ShapeDtypeStruct(a.shape, a.dtype) for n, a in scratch if n in buffers]
    return pl.pallas_call(
        functools.partial(exchange_kernel, names, count, heads, reverse, work, early, after),
        out_shape=tuple(jax.ShapeDtypeStruct(a.shape, a.dtype) for _, a, _ in outs),
        in_specs=[spec for *_, spec in ins],
        out_specs=tuple(spec for *_, spec in outs),
        scratch_shapes=[s for _, s in scratch],
        compiler_params=pltpu.CompilerParams(
            collective_id=number, has_side_effects=True, vmem_limit_bytes=EXCHANGE_VMEM
        ),
        cost_estimate=cost(40 << 30, 16 << 20),
    )(*[a for _, a, _ in ins])


def scatter_kernel(count, in_ref, out_ref, slots, send, receive):
    place = lax.axis_index("seq")
    others = [{"seq": lax.rem(place + k, count)} for k in range(1, count)]
    barrier = pltpu.get_barrier_semaphore()
    for device in others:
        pl.semaphore_signal(barrier, inc=1, device_id=device, device_id_type=MESH)
    pl.semaphore_wait(barrier, count - 1)
    copies = []
    for k, device in enumerate(others):
        moved = pltpu.make_async_remote_copy(
            src_ref=in_ref.at[device["seq"]], dst_ref=slots.at[place],
            send_sem=send.at[k], recv_sem=receive.at[k], device_id=device, device_id_type=MESH,
        )
        moved.start()
        copies.append(moved)
    slots[place] = in_ref[place]
    for moved in copies:
        moved.wait()
    total = slots[0]
    for i in range(1, count):
        total = total + slots[i]
    out_ref[...] = total


def scatter_sum(number, array):
    count = array.shape[0]
    vmem = pl.BlockSpec(memory_space=pltpu.VMEM)
    return pl.pallas_call(
        functools.partial(scatter_kernel, count),
        out_shape=jax.ShapeDtypeStruct(array.shape[1:], jnp.float32),
        in_specs=[vmem],
        out_specs=vmem,
        scratch_shapes=[
            pltpu.VMEM(array.shape, jnp.float32),
            pltpu.SemaphoreType.DMA((count - 1,)),
            pltpu.SemaphoreType.DMA((count - 1,)),
        ],
        compiler_params=pltpu.CompilerParams(
            collective_id=number, has_side_effects=True, vmem_limit_bytes=VMEM
        ),
        cost_estimate=cost(4 << 30, 1 << 20),
    )(array)


def state_of(keep, doc, keys, values):
    keep = jnp.broadcast_to(keep[:, None], (keep.shape[0], 64))
    return jnp.concatenate([keep, jnp.full_like(keep, doc), keys, values], axis=1)


def head_parts(size, count):
    whole = [(at, 256) for at in range(0, size, 256)]
    last = whole[:-1] + [(size - 256, 128), (size - 128, 128)]
    sides = [0, count - 1, *range(1, count - 1)]
    return [(i, *tile) for i in sides for tile in (last if i == sides[-1] else whole)]


def final_kernel(tiles, head_count, *refs):
    act_in, near_in, dy_own, dy_their, dy_near, dy_far, in_own, in_their, branch_own, branch_their = refs[:10]
    sides = refs[10 : 10 + 2 * head_count]
    part, outs = refs[10 + 2 * head_count], refs[11 + 2 * head_count : 11 + 3 * head_count]
    (out_down, added, far, across, wide_in, wide_branch, heads, stage, stage_head,
     act, their_act, near_act, far_act, wide_dy, head_tile, to_middle, from_middle, near, own_sum, arrived,
     own_sems, head_sems, stage_sems, act_sems, *sems) = refs[11 + 3 * head_count :]
    place = lax.axis_index("seq")
    line = place // 2
    at_end = (line == 0) | (line == 3)
    in_middle = jnp.logical_not(at_end)
    partner, beside = {"seq": other_of(place, 1)}, {"seq": other_of(place, 2)}
    opposite = {"seq": place + jnp.where(line == 1, 2, -2)}
    rows = act.shape[0]
    wide = out_down.shape[0]
    head = heads.shape[1] // head_count
    parts = head_parts(head, head_count)
    columns = [pl.ds(i * head + begin, size) for i, begin, size in parts]
    down = [pl.ds(*tile) for tile in tiles]
    out = [outs[i].at[:, pl.ds(begin, size)] for i, begin, size in parts]

    number = lax.axis_index("head")
    sibling, over_y = {"head": other_of(number, 1)}, {"head": other_of(number, 2)}
    barrier = pltpu.get_barrier_semaphore()
    for device in (beside, partner, sibling, over_y):
        pl.semaphore_signal(barrier, inc=1, device_id=device, device_id_type=MESH)

    @pl.when(in_middle)
    def _():
        pl.semaphore_signal(barrier, inc=1, device_id=opposite, device_id_type=MESH)

    roles = [jnp.where(line < 2, a, b) for a, b in ((2, 1), (3, 0), (1, 2), (0, 3))]
    starts = [pl.multiple_of((2 * role + place % 2) * wide, 128) for role in roles]

    def load(source, target, sem):
        copied = pltpu.make_async_copy(source, target, sem)
        copied.start()
        return copied

    in_loads, branch_loads, dy_loads = (
        [
            pltpu.make_async_copy(
                source.at[:, pl.ds(start, wide)],
                target.at[pl.ds(0, rows), pl.ds(r * wide, wide)],
                own_sems.at[k, r],
            )
            for r, start in enumerate(starts)
        ]
        for k, (source, target) in enumerate(
            ((in_own, wide_in), (branch_own, wide_branch), (dy_own, wide_dy))
        )
    )
    for one in in_loads:
        one.start()
    head_loads = [
        load(sides[2 * i], heads.at[pl.ds(0, rows), pl.ds(i * head, head)], head_sems.at[0, i])
        for i in range(head_count)
    ]
    ready = (0, head_count - 1)
    head_loads += [load(sides[2 * i + 1], stage_head.at[i], head_sems.at[1, i]) for i in ready]
    act_loads = [
        pltpu.make_async_copy(act_in, act, act_sems.at[0]),
        pltpu.make_async_copy(near_in, near_act, act_sems.at[1]),
    ]
    jobs = [(in_their, wide_in, 1), (branch_their, wide_branch, 1)]
    jobs += [(dy_their, wide_dy, 1), (dy_near, wide_dy, 2), (dy_far, wide_dy, 3)]

    def staged(k):
        return [
            load(jobs[k][0].at[role], stage.at[k % 2, r], stage_sems.at[k % 2, r])
            for r, role in enumerate(roles)
        ]

    under_way = {0: staged(0)}
    for one in branch_loads:
        one.start()
    under_way[1] = staged(1)
    for one in dy_loads + act_loads:
        one.start()

    def settle(k):
        for one in under_way[k]:
            one.wait()
        _, target, group = jobs[k]
        for r in range(4):
            target[group * rows : (group + 1) * rows, r * wide : (r + 1) * wide] = stage[
                k % 2, r
            ].astype(jnp.bfloat16)

    pl.semaphore_wait(barrier, 4 + in_middle.astype(jnp.int32))

    def remote(source, target, kind, i, device):
        return pltpu.make_async_remote_copy(
            src_ref=source, dst_ref=target, send_sem=sems[2 * kind].at[i],
            recv_sem=sems[2 * kind + 1].at[i], device_id=device, device_id_type=MESH,
        )

    chunk = part.shape[0] // CHUNKS
    half = chunk // 2
    low = number % 2
    mine_of = [pl.ds(pl.multiple_of(c * chunk + low * half, 8), half) for c in range(CHUNKS)]
    other_half = [pl.ds(pl.multiple_of(c * chunk + (1 - low) * half, 8), half) for c in range(CHUNKS)]
    nears = [remote(part.at[h], near.at[c], 8, c, sibling) for c, h in enumerate(other_half)]
    sums = [remote(own_sum.at[c], arrived.at[c], 9, c, over_y) for c in range(CHUNKS)]
    backs = [remote(added.at[h], added.at[h], 10, c, sibling) for c, h in enumerate(mine_of)]
    head_trades = [
        remote(sides[2 * i + 1], stage_head.at[i], 7, i - 1, partner)
        for i in range(1, head_count - 1)
    ]
    second = pl.ds(wide, wide)
    to_side = [remote(far.at[:, c], far.at[:, c], 0, i, beside) for i, c in enumerate(columns)]
    over = [
        remote(far.at[pl.ds(0, 2 * wide), c], across.at[:, c], 1, i, opposite) for i, c in enumerate(columns)
    ]
    home = [remote(across.at[second, c], out[i], 2, i, beside) for i, c in enumerate(columns)]
    trades = [remote(act_in.at[:, c], their_act.at[:, c], 3, i, partner) for i, c in enumerate(down)]
    passes = [remote(near_in.at[:, c], far_act.at[:, c], 4, i, partner) for i, c in enumerate(down)]
    over_down = [
        remote(to_middle.at[:, c], from_middle.at[:, c], 5, i, opposite) for i, c in enumerate(down)
    ]
    home_down = [
        remote(from_middle.at[second, c], out_down.at[:, c], 6, i, beside) for i, c in enumerate(down)
    ]

    down_at = {min(2 * j, len(columns) - len(down) + j - 2): j for j in range(len(down))}
    order = range(len(parts))

    def wide_of(i):
        return wide_branch if parts[i][0] == head_count - 1 else wide_in

    for one in nears:
        one.start()

    @pl.when(in_middle)
    def _():
        trades[0].start()
        passes[0].start()

    for one in in_loads + head_loads:
        one.wait()
    settle(0)

    def receive(i):
        if 0 < i < head_count - 1:
            head_trades[i - 1].wait_recv()
        heads[rows:, i * head : (i + 1) * head] = stage_head[i].astype(jnp.bfloat16)

    receive(0)

    def to_middle_tile(i):
        far[:, columns[i]] = tn(wide_of(i)[:, : 3 * wide], heads[:, columns[i]])
        to_side[i].start()

    first = [i for i in range(len(parts)) if parts[i][0] == 0]

    @pl.when(at_end)
    def _():
        for i in first:
            to_middle_tile(i)

    settle(1)
    receive(head_count - 1)

    @pl.when(at_end)
    def _():
        for one in head_trades:
            one.start()

    @pl.when(in_middle)
    def _():
        under_way[2], under_way[3] = staged(2), staged(3)
        settle(2)
        under_way[4] = staged(4)
        settle(3)
        settle(4)
        for i, (trade, onward) in enumerate(zip(trades, passes)):
            if i:
                trade.start()
                onward.start()
            if i < len(head_trades):
                head_trades[i].start()

    for c in range(CHUNKS):
        nears[c].wait_recv()
        own_sum[c] = part[mine_of[c], :] + near[c]
        sums[c].start()

    def settle_down():
        for one in dy_loads + act_loads:
            one.wait()

    for one in branch_loads:
        one.wait()

    @pl.when(at_end)
    def _():
        for k, i in enumerate(order):
            if parts[i][0] not in ready and parts[i][1] == 0:
                receive(parts[i][0])
            if i not in first:
                to_middle_tile(i)
        settle_down()

    @pl.when(at_end)
    def _():
        for k, i in enumerate(order):
            c = columns[i]
            mine = tn(wide_of(i)[:, 3 * wide :], heads[:, c])
            home[i].wait_recv()
            out[i][...] = out[i][...] + mine
            if k in down_at:
                home_down[down_at[k]].wait_recv()
        for one in to_side:
            one.wait_send()

    @pl.when(in_middle)
    def _():
        def finish(i):
            c = columns[i]
            mine = tn(wide_of(i)[:, 3 * wide :], heads[:, c])
            over[i].wait_recv()
            across[wide:, c] = across[wide:, c] + mine
            home[i].start()
            out[i][...] = far[2 * wide :, c] + across[:wide, c]

        settle_down()
        for k, i in enumerate(order):
            c = columns[i]
            if parts[i][0] not in ready and parts[i][1] == 0:
                receive(parts[i][0])
            j = down_at.get(k)
            if j is not None:
                d = down[j]
                size = tiles[j][1]
                tile = head_tile.at[:, pl.ds(0, size)]
                trades[j].wait_recv()
                passes[j].wait_recv()
                for g, side in enumerate((act, their_act, near_act, far_act)):
                    tile[g * rows : (g + 1) * rows, :] = side[:, d].astype(jnp.bfloat16)
                to_middle[:, d] = tn(wide_dy[:, : 2 * wide], tile[...])
                over_down[j].start()
                out_down[:, d] = tn(wide_dy[:, 2 * wide : 3 * wide], tile[...])
                home_part = tn(wide_dy[:, 3 * wide :], tile[...])
            mine = tn(wide_of(i)[:, : 3 * wide], heads[:, c])
            to_side[i].wait_recv()
            far[:, c] = far[:, c] + mine
            over[i].start()
            if j is not None:
                over_down[j].wait_recv()
                from_middle[wide:, d] = from_middle[wide:, d] + home_part
                home_down[j].start()
                out_down[:, d] = out_down[:, d] + from_middle[:wide, d]
            if k:
                finish(order[k - 1])
        finish(order[-1])
        for one in over + home + trades + passes + over_down + home_down:
            one.wait_send()

    for c in range(CHUNKS):
        sums[c].wait()
        added[mine_of[c], :] = own_sum[c] + arrived[c]
        backs[c].start()
    for one in head_trades + nears:
        one.wait_send()
    for one in backs:
        one.wait()


def final_gradients(number, part, act, near_act, dy, wide_in, wide_branch, heads):
    rows, hidden = act.shape
    wide = dy[1].shape[2]
    head = heads[0][0].shape[1]
    count = len(heads)
    total = head * count
    tiles = column_tiles(hidden)
    f32, bf16 = jnp.float32, jnp.bfloat16
    dma = pltpu.SemaphoreType.DMA
    hbm, vmem = pl.BlockSpec(memory_space=pl.ANY), pl.BlockSpec(memory_space=pltpu.VMEM)
    whole = pltpu.VMEM((rows, hidden), f32)
    sides = [a for pair in heads for a in pair]
    half = (CHUNKS, rows // CHUNKS // 2, part.shape[1])
    return pl.pallas_call(
        functools.partial(final_kernel, tiles, count),
        out_shape=(
            *[jax.ShapeDtypeStruct((wide, head), f32)] * count,
            jax.ShapeDtypeStruct((wide, hidden), f32),
            jax.ShapeDtypeStruct(part.shape, f32),
        ),
        in_specs=[hbm] * (10 + len(sides)) + [vmem],
        out_specs=(vmem,) * (count + 2),
        scratch_shapes=[
            pltpu.VMEM((3 * wide, total), f32),
            pltpu.VMEM((2 * wide, total), f32),
            pltpu.VMEM((2 * rows, 4 * wide), bf16),
            pltpu.VMEM((2 * rows, 4 * wide), bf16),
            pltpu.VMEM((2 * rows, total), bf16),
            pltpu.VMEM((2, 4, rows, wide), f32),
            pltpu.VMEM((count, rows, head), f32),
            whole, whole, whole, whole,
            pltpu.VMEM((4 * rows, 4 * wide), bf16),
            pltpu.VMEM((4 * rows, 256), bf16),
            pltpu.VMEM((2 * wide, hidden), f32),
            pltpu.VMEM((2 * wide, hidden), f32),
            pltpu.VMEM(half, f32), pltpu.VMEM(half, f32), pltpu.VMEM(half, f32),
            dma((3, 4)), dma((2, count)), dma((2, 4)), dma((2,)),
        ]
        + [dma((len(head_parts(head, count)),))] * 6
        + [dma((len(tiles),))] * 8
        + [dma((count - 2,))] * 2
        + [dma((CHUNKS,))] * 6,
        compiler_params=pltpu.CompilerParams(
            collective_id=number, has_side_effects=True, vmem_limit_bytes=FINAL_VMEM
        ),
        cost_estimate=cost(200 << 30, 16 << 20),
    )(act, near_act, *dy, *wide_in, *wide_branch, *sides, part)


def normed_after(c, rows, added, own):
    stream, gain, normed_out, float_out, normed, normed_f, sems = own

    def copies(c):
        mine = pl.ds(c * rows, rows)
        return [
            pltpu.make_async_copy(normed.at[mine], normed_out.at[mine], sems.at[0, c]),
            pltpu.make_async_copy(normed_f.at[mine], float_out.at[mine], sems.at[1, c]),
        ]

    if c is None:
        for i in range(CHUNKS):
            for one in copies(i):
                one.wait()
        return
    mine = pl.ds(c * rows, rows)
    hidden = stream[mine, :].astype(jnp.float32) + added[mine, :]
    added[mine, :] = hidden
    rounded = (hidden * rms_scale(hidden) * gain[...]).astype(jnp.bfloat16)
    normed[mine, :] = rounded
    normed_f[mine, :] = rounded.astype(jnp.float32)
    for one in copies(c):
        one.start()


def norm_after(stream, gain):
    half, full = (jax.ShapeDtypeStruct(stream.shape, t) for t in (jnp.bfloat16, jnp.float32))
    return (
        normed_after,
        (stream, gain.reshape(1, -1)),
        (half, full),
        (
            pltpu.VMEM(stream.shape, jnp.bfloat16),
            pltpu.VMEM(stream.shape, jnp.float32),
            pltpu.SemaphoreType.DMA((2, CHUNKS)),
        ),
    )


def matmul_work(product, column, count, piece, pieces, left_ref, *refs):
    rights, outs, left = refs[:count], refs[count : 2 * count], refs[2 * count]
    sides, sems = refs[2 * count + 1 : -1], refs[-1]
    copies = [pltpu.make_async_copy(left_ref, left, sems.at[0])]
    copies += [pltpu.make_async_copy(a, b, sems.at[1 + i]) for i, (a, b) in enumerate(zip(rights, sides))]
    if piece is None:
        for one in copies:
            one.start()
        return
    if piece == 0:
        for one in copies:
            one.wait()
    for right, out in zip(sides, outs):

        def tile(i, carry):
            columns = pl.ds(pl.multiple_of(i * column, column), column)
            side = right[columns, :] if product is nt else right[:, columns]
            out[:, columns] = product(left[...], side)
            return carry

        tiles = out.shape[1] // column
        lax.fori_loop(tiles * piece // pieces, tiles * (piece + 1) // pieces, tile, 0)


def column_tiles(size):
    wide = 256 if size >= 256 else size
    return [(at, min(wide, size - at)) for at in range(0, size, wide)]


def hidden_units(send_tile, refs, own):
    (normed_in, gate_in, up_in, down_in, d_act_in, act_f_out, d_gate_out, d_up_out, up_f_out, ffn_out,
     gate_f, act_f, act_ref, d_gate_ref, d_up_ref, up_f_ref, ffn_ref, normed, w_gate, w_up, w_down, d_act, sems, tile_sems, out_sems) = own
    whole = [
        pltpu.make_async_copy(normed_in, normed, sems.at[0]),
        pltpu.make_async_copy(d_act_in, d_act, sems.at[1]),
        pltpu.make_async_copy(down_in, w_down, sems.at[2]),
    ]
    parts = []
    tiles = column_tiles(act_ref.shape[1])
    for i, (at, size) in enumerate(tiles):
        columns = pl.ds(at, size)
        parts.append(
            [
                pltpu.make_async_copy(gate_in.at[:, columns], w_gate.at[:, columns], tile_sems.at[0, i]),
                pltpu.make_async_copy(up_in.at[:, columns], w_up.at[:, columns], tile_sems.at[1, i]),
            ]
        )
    whole[0].start()
    for one in parts[0]:
        one.start()
    whole[1].start()
    for pair in parts[1:]:
        for one in pair:
            one.start()
    whole[2].start()
    whole[0].wait()
    for i, (at, size) in enumerate(tiles):
        columns = pl.ds(at, size)
        for one in parts[i]:
            one.wait()
        gate = nn(normed[...], w_gate[:, columns])
        up = nn(normed[...], w_up[:, columns])
        if i == 0:
            whole[1].wait()
        sig = jax.nn.sigmoid(gate)
        silu = gate * sig
        pull = d_act[:, columns]
        act = (silu * up).astype(jnp.bfloat16)
        act_ref[:, columns] = act
        act_f[:, columns] = act.astype(jnp.float32)
        d_gate = (pull * up * sig * (1.0 + gate * (1.0 - sig))).astype(jnp.bfloat16)
        d_up = (pull * silu).astype(jnp.bfloat16)
        d_gate_ref[:, columns] = d_gate
        d_up_ref[:, columns] = d_up
        gate_f[:, columns] = d_gate.astype(jnp.float32)
        send_tile(i, columns)
        up_f_ref[:, columns] = d_up.astype(jnp.float32)

    kept = [(act_f, act_f_out), (d_gate_ref, d_gate_out), (d_up_ref, d_up_out),
            (up_f_ref, up_f_out), (ffn_ref, ffn_out)]
    kept = [pltpu.make_async_copy(a, b, out_sems.at[i]) for i, (a, b) in enumerate(kept)]
    for one in kept[:-1]:
        one.start()
    part = refs["part"]

    def fill(c, rows):
        mine = pl.ds(c * rows, rows)

        def tile(i, carry):
            columns = pl.ds(pl.multiple_of(i * 256, 256), 256)
            part[mine, columns] = nt(d_gate_ref[mine, :], w_gate[columns, :]) + nt(
                d_up_ref[mine, :], w_up[columns, :]
            )
            return carry

        lax.fori_loop(0, part.shape[1] // 256, tile, 0)

    refs["finish"] = (whole[2], act_ref, w_down, ffn_ref, kept)
    return fill


def outer_product_beside(piece, pieces, refs):
    copied, act, w_down, out, kept = refs["finish"]
    copied.wait()

    def tile(i, carry):
        columns = pl.ds(pl.multiple_of(i * 256, 256), 256)
        out[:, columns] = nn(act[...], w_down[:, columns])
        return carry

    lax.fori_loop(0, out.shape[1] // 256, tile, 0)
    kept[-1].start()


def hidden_units_early(normed_mid, w_gate, w_up, w_down, d_act):
    rows, width = normed_mid.shape
    hidden = w_gate.shape[1]
    tiles = len(column_tiles(hidden))
    half = jax.ShapeDtypeStruct((rows, hidden), jnp.bfloat16)
    full = jax.ShapeDtypeStruct((rows, hidden), jnp.float32)
    return (
        hidden_units,
        (normed_mid, w_gate, w_up, w_down, d_act),
        (rows, hidden),
        tiles,
        (full, half, half, full, jax.ShapeDtypeStruct((rows, width), jnp.float32)),
        (
            pltpu.VMEM((rows, hidden), jnp.float32),
            pltpu.VMEM((rows, hidden), jnp.float32),
            pltpu.VMEM((rows, hidden), jnp.bfloat16),
            pltpu.VMEM((rows, hidden), jnp.bfloat16),
            pltpu.VMEM((rows, hidden), jnp.bfloat16),
            pltpu.VMEM((rows, hidden), jnp.float32),
            pltpu.VMEM((rows, width), jnp.float32),
            pltpu.VMEM(normed_mid.shape, jnp.bfloat16),
            pltpu.VMEM(w_gate.shape, jnp.bfloat16),
            pltpu.VMEM(w_up.shape, jnp.bfloat16),
            pltpu.VMEM(w_down.shape, jnp.bfloat16),
            pltpu.VMEM(d_act.shape, jnp.float32),
            pltpu.SemaphoreType.DMA((3,)),
            pltpu.SemaphoreType.DMA((2, tiles)),
            pltpu.SemaphoreType.DMA((5,)),
        ),
    )


def matmul_beside(product, left, *rights):
    columns = rights[0].shape[0] if product is nt else rights[0].shape[1]
    column = 256 if columns % 256 == 0 else 128
    return (
        functools.partial(matmul_work, product, column, len(rights)),
        (left, *rights),
        (jax.ShapeDtypeStruct((left.shape[0], columns), jnp.float32),) * len(rights),
        (
            pltpu.VMEM(left.shape, left.dtype),
            *[pltpu.VMEM(right.shape, right.dtype) for right in rights],
            pltpu.SemaphoreType.DMA((1 + len(rights),)),
        ),
        (True,) * (1 + len(rights)),
    )


def body(
    stream,
    seg_ids,
    attn_gain,
    w_query,
    w_key,
    w_value,
    w_outgate,
    w_low,
    w_slot,
    forget_bias,
    head_gain,
    w_out,
    mlp_gain,
    w_gate,
    w_up,
    w_down,
    cotangent,
):
    tok_rows = stream.shape[0]
    width = stream.shape[1]
    slots = w_slot.shape[2]
    head_width = w_query.shape[1]
    stream_f = stream.astype(jnp.float32)
    scale_in = rms_scale(stream_f)
    normed_in = (stream_f * scale_in * attn_gain).astype(jnp.bfloat16)
    key_rows = plain_dot(normed_in, w_key).astype(jnp.bfloat16)
    value_rows = plain_dot(normed_in, w_value).astype(jnp.bfloat16)
    ranked = plain_dot(normed_in, w_low)

    def decay_logs(ranked_in, slot_map, bias_row):
        return jax.nn.log_sigmoid(precise_dot(ranked_in, slot_map[0]) + bias_row[0]) / GATE_NORM

    log_decay, gate_pull = jax.vjp(decay_logs, ranked, w_slot, forget_bias)

    new = -jnp.expm1(log_decay)
    last_doc = seg_ids[tok_rows - 1]
    running = precise_dot(jnp.tril(jnp.ones((tok_rows, tok_rows), jnp.float32)), log_decay)
    total = running[tok_rows - 1]
    in_last = (seg_ids == last_doc)[:, None]
    factor = jnp.where(in_last, jnp.exp(jnp.where(in_last, total - running, 0.0)) * new, 0.0)
    def wide_float(array):
        return array.astype(jnp.float32)

    local_key = precise_left_t(factor, key_rows.astype(jnp.float32))
    local_value = precise_left_t(factor, value_rows.astype(jnp.float32))
    docs = seg_ids.astype(jnp.float32)
    own_state = state_of(jnp.exp(total), docs[tok_rows - 1], local_key, local_value)
    dy_f = cotangent.astype(jnp.float32)
    prefix, query_rows, gate_act = exchange(
        0,
        state=own_state,
        work=matmul_beside(nn, normed_in, w_query, w_outgate),
    )
    query_rows = query_rows.astype(jnp.bfloat16)
    key_in, value_in = prefix[:, 128 : 128 + head_width], prefix[:, 128 + head_width :]
    prior = prefix[0, 64]
    decay_all = jnp.where(docs[tok_rows - 1] == prior, jnp.exp(total), 0.0)
    docs = jnp.broadcast_to(docs[:, None], (tok_rows, slots))
    before = jnp.broadcast_to(prior, (1, slots))
    slot_read, scores, probs, key_states, value_states = read_slots(
        query_rows, key_rows, value_rows, log_decay, new, docs, before, key_in, value_in
    )
    scale_read = rms_scale(slot_read)
    normed_read = slot_read * scale_read * head_gain[0]
    gate_sig = jax.nn.sigmoid(gate_act)
    gate_silu = gate_act * gate_sig
    mixed_heads = (normed_read * gate_silu).astype(jnp.bfloat16)
    four = lax.axis_size("seq") == 8
    hidden, from_dy, *near_dy, normed_mid, normed_mid_f, d_act = exchange(
        1,
        part=plain_dot(mixed_heads, w_out),
        wides=(wide_to_send(cotangent),),
        relay=(dy_f,) if four else (),
        work=matmul_beside(nt, cotangent, w_down),
        after=norm_after(stream, mlp_gain),
    )
    wide_dy = cotangent, from_dy
    scale_mid = rms_scale(hidden)
    upstream = cotangent.astype(jnp.float32)
    d_mid, from_mid, *made = exchange(
        2,
        part=jax.ShapeDtypeStruct((tok_rows, width), jnp.float32),
        wides=(wide_to_send(normed_mid_f),),
        relay=(from_dy,) if four else (),
        early=hidden_units_early(normed_mid, w_gate, w_up, w_down, d_act),
    )
    if four:
        far_dy, from_gate, end_act, *made = made
    else:
        from_gate, *made = made
    act_f, d_gate, d_up, d_up_f, ffn_part = made
    wide_mid = normed_mid, from_mid
    grad_gate = pair_products((wide_mid, [(d_gate, from_gate)]))
    d_mid, grad_gate = together(d_mid, grad_gate)
    grad_gate = line_sum(grad_gate)
    grad_mlp_gain = jnp.sum(d_mid * hidden * scale_mid, axis=0)
    scaled_mid = d_mid * mlp_gain
    d_hidden = (
        upstream
        + scale_mid * scaled_mid
        - hidden * scale_mid**3 * jnp.mean(scaled_mid * hidden, axis=1, keepdims=True)
    )
    d_branch = d_hidden.astype(jnp.bfloat16)
    d_mixed = dot_right_t(d_branch, w_out)
    d_gate_act = (d_mixed * normed_read * gate_sig * (1.0 + gate_act * (1.0 - gate_sig))).astype(
        jnp.bfloat16
    )
    d_normed = d_mixed * gate_silu
    grad_head_gain = jnp.sum(d_normed * slot_read * scale_read, axis=0)[None, :]
    scaled_read = d_normed * head_gain[0]
    d_read = scale_read * scaled_read - slot_read * scale_read**3 * jnp.mean(
        scaled_read * slot_read, axis=1, keepdims=True
    )
    normed_f, ffn_part = together(wide_to_send(normed_in), ffn_part)
    ffn_out, from_in, from_up, *back = exchange(
        3,
        part=ffn_part,
        wides=(normed_f,),
        narrows=(d_up_f,),
        work=back_query(
            query_rows, key_rows, value_rows, log_decay, new, docs, before, scores, probs, key_states, value_states, d_read
        ),
    )
    wide_in = normed_in, from_in
    grad_up = pair_products((wide_mid, [(d_up, from_up)]))
    d_query, d_key, d_value, held, gained, to_keys, to_values, key_back, value_back = back
    query_back = d_query.astype(jnp.bfloat16)
    result = hidden + ffn_out
    squares = jnp.stack(
        [jnp.sum(stream_f * stream_f), jnp.sum(hidden * hidden), jnp.sum(result * result)]
    )
    key_back, grad_up, grad_gate, grad_mlp_gain, grad_head_gain, squares = together(
        key_back, grad_up, grad_gate, grad_mlp_gain, grad_head_gain, squares
    )
    grad_up = line_sum(grad_up)
    suffix, from_branch, from_outgate, from_mixed = exchange(
        4,
        state=state_of(decay_all, 0.0, key_back, value_back),
        reverse=True,
        wides=(wide_to_send(d_branch),),
        narrows=(wide_float(d_gate_act), wide_float(mixed_heads)),
    )
    key_end, value_end = suffix[:, 128 : 128 + head_width], suffix[:, 128 + head_width :]
    end_total = jnp.sum(key_states[-1] * key_end + value_states[-1] * value_end, axis=1)[None, :]
    key_back, value_back, d_logs = back_key(
        key_rows, value_rows, log_decay, new, docs, before, d_key, d_value, held, gained,
        to_keys, to_values, key_end, value_end, end_total,
    )
    d_ranked, grad_slot, grad_bias = gate_pull(d_logs)
    normed_f = normed_in.astype(jnp.float32)
    grad_low = precise_left_t(normed_f, d_ranked)
    d_in_part = (
        dot_right_t(query_back, w_query)
        + dot_right_t(key_back, w_key)
        + dot_right_t(value_back, w_value)
        + dot_right_t(d_gate_act, w_outgate)
        + precise_right_t(d_ranked, w_low.astype(jnp.float32))
    )
    late = [wide_float(a) for a in (query_back, key_back, value_back)]
    wide_branch = d_branch, from_branch
    if four:
        sides = [(d_gate_act, from_outgate), *zip((query_back, key_back, value_back), late), (mixed_heads, from_mixed)]
        act_f, grad_up = together(act_f, grad_up)
        *grad_rest, grad_down, d_in = final_gradients(
            5, d_in_part, act_f, end_act, (cotangent, from_dy, *near_dy, far_dy), wide_in, wide_branch, sides
        )
    else:
        d_in, *late = exchange(5, part=d_in_part, narrows=late)
        head_sides = [(d_gate_act, from_outgate), *zip((query_back, key_back, value_back), late), (mixed_heads, from_mixed)]
        grad_rest = pair_products((wide_in, head_sides[:4]), (wide_branch, head_sides[4:]))
        grad_rest = line_sum(grad_rest)
        (from_act,) = exchange(6, narrows=(act_f,))
        grad_down = pair_products((wide_dy, [(act_f.astype(jnp.bfloat16), from_act)]))
        grad_down = line_sum(grad_down)
        grad_rest = jnp.split(grad_rest, 5, axis=1)
    grad_outgate, grad_query, grad_key, grad_value, grad_out = grad_rest
    grad_attn_gain = jnp.sum(d_in * stream_f * scale_in, axis=0)
    scaled_in = d_in * attn_gain
    grad_stream = (
        d_hidden
        + scale_in * scaled_in
        - stream_f * scale_in**3 * jnp.mean(scaled_in * stream_f, axis=1, keepdims=True)
    ).astype(jnp.bfloat16)
    count = lax.axis_size("seq")
    small = [
        grad_attn_gain.reshape(count, -1),
        grad_mlp_gain.reshape(count, -1),
        grad_low.reshape(count, -1),
        jnp.moveaxis(grad_slot[0].reshape(-1, count, slots // count), 1, 0).reshape(count, -1),
        grad_bias.reshape(count, -1),
        grad_head_gain.reshape(count, -1),
        jnp.broadcast_to(squares, (count, 3)),
    ]
    sizes = [a.shape[1] for a in small]
    packed = jnp.concatenate(small, axis=1)
    packed = jnp.pad(packed, ((0, 0), (0, -packed.shape[1] % 1024)))
    packed = scatter_sum(7, packed.reshape(count, -1, 128)).reshape(-1)
    ends = [sum(sizes[: i + 1]) for i in range(len(sizes))]
    small = [packed[end - size : end] for end, size in zip(ends, sizes)]
    stream_rms = jnp.sqrt(small[6] / (tok_rows * count * width))
    summed = (
        small[0],
        grad_query,
        grad_key,
        grad_value,
        grad_outgate,
        small[2].reshape(width // count, -1),
        small[3].reshape(1, -1, slots // count),
        small[4][None, :],
        small[5][None, :],
        grad_out.T,
        small[1],
        grad_gate,
        grad_up,
        grad_down.T,
    )
    mixer_parts = summed[:10]
    ffn_parts = summed[10:]
    return (
        result.astype(jnp.bfloat16),
        grad_stream,
        mixer_parts[0],
        mixer_parts[1],
        mixer_parts[2],
        mixer_parts[3],
        mixer_parts[4],
        mixer_parts[5],
        mixer_parts[6],
        mixer_parts[7],
        mixer_parts[8],
        mixer_parts[9],
        ffn_parts[0],
        ffn_parts[1],
        ffn_parts[2],
        ffn_parts[3],
        stream_rms,
    )


def solution(mesh):
    in_specs = (
        P("seq", None),
        P("seq"),
        P(),
        P(None, "head"),
        P(None, "head"),
        P(None, "head"),
        P(None, "head"),
        P(None, "head"),
        P("head", None, None),
        P("head", None),
        P("head", None),
        P("head", None),
        P(),
        P(None, "head"),
        P(None, "head"),
        P("head", None),
        P("seq", None),
    )
    out_specs = (
        P("seq", None),
        P("seq", None),
        P("seq"),
        P("seq", "head"),
        P("seq", "head"),
        P("seq", "head"),
        P("seq", "head"),
        P("seq", "head"),
        P("head", None, "seq"),
        P("head", "seq"),
        P("head", "seq"),
        P("head", "seq"),
        P("seq"),
        P("seq", "head"),
        P("seq", "head"),
        P("head", "seq"),
        P(),
    )
    return jax.shard_map(body, mesh=mesh, in_specs=in_specs, out_specs=out_specs, check_vma=False)
```
